32 devices in a mesh: dp: 8 (over z, y), head: 4 (over x, core).
Axes of the slice: x: 2, y: 2, z: 4, core: 2. Of those that a mesh axis runs over, the one named last changes fastest.
Arguments:
- inputs: bfloat16 [32768, 768], P(('dp', 'head')), may hold values from -6 to 6
- segment_ids: int32 [32768], P('dp'), may hold values from 0 to 3, as said below
- norm_gain: float32 [768], replicated, may hold values from 0.5 to 1.5
- up_weight: bfloat16 [768, 2, 1536], P('dp', None, 'head'), may hold values from -0.21875 to 0.21875
- conv_weight: float32 [4, 1536], P(None, 'head'), may hold values from -3 to 3
- conv_bias: float32 [1536], P('head'), may hold values from -3 to 3
- qkv_weight: float32 [3, 384, 4, 4], P(None, 'head'), may hold values from -3 to 3
- gate_weight: bfloat16 [3, 1536, 8], P(None, 'head'), may hold values from -0.078125 to 0.078125
- gate_bias: float32 [2, 4], P(None, 'head'), may hold values from -3 to 8, as said below
- group_gain: float32 [1536], P('head'), may hold values from 0.5 to 1.5
- skip_gain: float32 [1536], P('head'), may hold values from 0.5 to 1.5
- down_weight: bfloat16 [1536, 768], P('head', 'dp'), may hold values from -0.15625 to 0.15625
- out_grad: bfloat16 [32768, 768], P(('dp', 'head')), may hold values from -6 to 6
Outputs:
- output: bfloat16 [32768, 768], P(('dp', 'head'))
- input_grad: float32 [32768, 768], P(('dp', 'head'))
- norm_gain_grad: float32 [768], replicated
- up_weight_grad: float32 [768, 2, 1536], P('dp', None, 'head')
- conv_weight_grad: float32 [4, 1536], P(None, 'head')
- conv_bias_grad: float32 [1536], P('head')
- qkv_weight_grad: float32 [3, 384, 4, 4], P(None, 'head')
- gate_weight_grad: float32 [3, 1536, 8], P(None, 'head')
- gate_bias_grad: float32 [2, 4], P(None, 'head')
- group_gain_grad: float32 [1536], P('head')
- skip_gain_grad: float32 [1536], P('head')
- down_weight_grad: float32 [1536, 768], P('head', 'dp')
The draws below stay inside these ranges and needn't reach their ends.
Inputs may be any that keep to these rules, and one draw needn't show every extreme that they name: `segment_ids`: within each group of 4096 consecutive tokens the number is constant over each aligned block of 1024 tokens, starts at 0 and rises by 0 or 1 from one block to the next, so that each segment holds 1, 2 or 4 such blocks; some group holds four segments. `gate_bias`: the first row (input gates) lies in -3 to -1, the second (forget gates) in 3 to 8.
All inputs are finite; a program needn't handle non-finite values.
Results may differ from the reference program's by a relative error of at most 0.012.
Values may be sent and summed in bfloat16 or wider, within the bound.
A program may use at most 320 MiB of HBM per device.

```python
import jax
import jax.numpy as jnp
import numpy as np
from jax import lax

D = 768
INNER = 1536
NH = 4
KS = 4
BS = 4
SPAN = 64
TOK_DEV = 1024
DH = 384
BLOCKS = 384
GROUP_TOK = 4096
TOKENS = 32768
N_DP = 8


def draw_segment_ids(key, part):
    layouts = jnp.array(np.array([[0, 0, 0, 0], [0, 0, 1, 1], [0, 0, 1, 2], [0, 1, 1, 2], [0, 1, 2, 2], [0, 1, 2, 3]], np.int32))
    groups = TOKENS // GROUP_TOK
    pick_key, force_key = jax.random.split(jax.random.fold_in(key, 11))
    picked = jax.random.randint(pick_key, (groups,), 0, 6)
    forced = jax.random.randint(force_key, (), 0, groups)
    picked = jnp.where(jnp.arange(groups) == forced, 5, picked)
    positions = jnp.arange(TOKENS)
    unit_of = positions % GROUP_TOK // TOK_DEV
    return layouts[picked[positions // GROUP_TOK], unit_of].astype(jnp.int32)


def draw_gate_bias(key, part):
    in_key, forget_key = jax.random.split(jax.random.fold_in(key, 23))
    in_row = jax.random.uniform(in_key, (NH,), jnp.float32, -3.0, -1.0)
    forget_row = jax.random.uniform(forget_key, (NH,), jnp.float32, 3.0, 8.0)
    return jnp.stack([in_row, forget_row]).astype(jnp.float32)


def strengthened(result, key, source, target, blocks, factor):
    def block_of(axis_at):
        return (jnp.arange(result.shape[axis_at]) // (result.shape[axis_at] // blocks)).reshape((-1,) + (1,) * (result.ndim - 1 - axis_at))

    one_side = jax.random.permutation(key, blocks)[block_of(target)]
    second = (block_of(target) + blocks // 2) % blocks
    return jnp.where((block_of(source) == one_side) | (block_of(source) == second), factor * result, result)


def shard_levels(rng, extent, shards, low, largest):
    factor_of, own = 1.0, jax.random.fold_in(rng, 6)
    for axis_at, parts in shards:
        draws = jnp.exp(jax.random.uniform(jax.random.fold_in(own, axis_at), (parts,), jnp.float32, low / len(shards), largest / len(shards)))
        factor_of = factor_of * jnp.repeat(draws, extent[axis_at] // parts).reshape([-1 if axis == axis_at else 1 for axis in range(len(extent))])
    return factor_of


def scatter_about(stream_key, dims, spread, bound, cuts=(), held_as=jnp.bfloat16):
    result = jax.random.normal(stream_key, dims, jnp.float32) * spread
    if len(cuts) > 0:
        result = shard_levels(stream_key, dims, cuts, -0.22, 0.18) * result
    return jnp.clip(result, min=-bound, max=bound).astype(held_as)


def noise_with(rng, shape, deviation, limit, shards, heavy, kind=jnp.bfloat16):
    entries = deviation * jax.random.normal(rng, shape, jnp.float32)
    if shards:
        entries = entries * shard_levels(rng, shape, shards, -0.22, 0.18)
    return jnp.clip(strengthened(entries, jax.random.fold_in(rng, 3), *heavy), -limit, limit).astype(kind)


def setup_inputs(seed: int = 0) -> dict:
    streams_of = jax.random.split(jax.random.key(seed), 14)
    return {
        "inputs": noise_with(streams_of[0], (TOKENS, D), 1.0, 6.0, ((0, 32),), (0, 1, 32, 2.75)),
        "segment_ids": draw_segment_ids(jax.random.fold_in(streams_of[13], 71), 0),
        "norm_gain": jnp.clip(1.0 + 0.1 * jax.random.normal(streams_of[2], (D,), jnp.float32), 0.5, 1.5),
        "up_weight": scatter_about(streams_of[3], (D, 2, INNER), D ** -0.5, 0.21875, ((0, 8), (2, 4))),
        "conv_weight": scatter_about(streams_of[4], (KS, INNER), KS ** -0.5, 3.0, ((1, 4),), jnp.float32),
        "conv_bias": scatter_about(streams_of[5], (INNER,), 0.5, 3.0, ((0, 4),), jnp.float32),
        "qkv_weight": scatter_about(streams_of[6], (3, BLOCKS, BS, BS), BS ** -0.5, 3.0, ((1, 4),), jnp.float32),
        "gate_weight": scatter_about(streams_of[7], (3, INNER, 2 * NH), (4 * INNER) ** -0.5, 0.078125, ((1, 4),)),
        "gate_bias": draw_gate_bias(jax.random.fold_in(streams_of[13], 71), 0),
        "group_gain": jnp.clip(1.0 + 0.1 * jax.random.normal(streams_of[9], (INNER,), jnp.float32), 0.5, 1.5),
        "skip_gain": jnp.clip(0.5 + 1.0 * jax.random.uniform(streams_of[10], (INNER,), jnp.float32) ** shard_levels(streams_of[10], (INNER,), ((0, 4),), -0.2, 0.2), 0.5, 1.5),
        "down_weight": scatter_about(streams_of[11], (INNER, D), INNER ** -0.5, 0.15625, ((0, 4), (1, 8))),
        "out_grad": noise_with(streams_of[12], (TOKENS, D), 1.0, 6.0, ((0, 32),), (0, 1, 32, 2.75)),
    }


EPSILON = 1e-05
NEGATIVE = -10000.0

@jax.custom_vjp
def low(v):
    return lax.optimization_barrier(v.astype(jnp.bfloat16)).astype(jnp.float32)

@jax.custom_vjp
def low_back(v):
    return v

def low_keep(v):
    return (low(v), None)

def low_pass(kept, grad):
    return (grad,)

def back_keep(v):
    return (v, None)

def back_low(kept, grad):
    return (low(grad),)
low.defvjp(low_keep, low_pass)
low_back.defvjp(back_keep, back_low)

def matmul(left_side, right_side):
    return jnp.dot(left_side, right_side, precision=lax.Precision.HIGHEST)

def causal_conv(branch, conv_weight, conv_bias, seg_ids):
    length = branch.shape[0]
    summed_taps = conv_bias[None, :] + conv_weight[0][None, :] * branch
    for offset in range(1, conv_weight.shape[0]):
        shifted = jnp.concatenate([jnp.zeros((offset, branch.shape[1]), branch.dtype), branch[:length - offset]], axis=0)
        earlier = jnp.concatenate([jnp.full((offset,), -1, jnp.int32), seg_ids[:length - offset].astype(jnp.int32)], axis=0)
        summed_taps = summed_taps + conv_weight[offset][None, :] * jnp.where((earlier == seg_ids.astype(jnp.int32))[:, None], shifted, 0.0)
    return summed_taps

def blockwise(source, blocks):
    shaped = source.reshape(source.shape[0], blocks.shape[0], blocks.shape[1])
    return jnp.einsum('tbi,bio->tbo', shaped, blocks, precision=lax.Precision.HIGHEST).reshape(source.shape)

def memory_cell(queries, key_rows, values, in_gate, log_forget, seg_ids):
    length = queries.shape[0]
    spans = length // SPAN
    scaling = DH ** (-0.5)
    causal = jnp.arange(SPAN)[:, None] >= jnp.arange(SPAN)[None, :]

    def advance(carried, pieces):
        memory, normal, prev_seg = carried
        q_span, k_span, v_span, i_span, f_span, s_span = pieces
        cumulative = jnp.cumsum(f_span, axis=0)
        allowed = causal & (s_span[:, None] == s_span[None, :])
        decays = jnp.exp(jnp.where(allowed[:, :, None], cumulative[:, None, :] - cumulative[None, :, :] + i_span[None, :, :], NEGATIVE))
        scores = jnp.einsum('thd,shd->tsh', q_span, k_span, precision=lax.Precision.HIGHEST) * scaling
        weights = scores * decays
        factor = jnp.where((s_span == prev_seg)[:, None], jnp.exp(cumulative), 0.0) * scaling
        numerator = jnp.einsum('tsh,shd->thd', weights, v_span, precision=lax.Precision.HIGHEST)
        numerator = numerator + factor[:, :, None] * jnp.einsum('thd,hde->the', q_span, memory, precision=lax.Precision.HIGHEST)
        denominator = lax.optimization_barrier(jnp.sum(weights, axis=1)) + factor * jnp.einsum('thd,hd->th', q_span, normal, precision=lax.Precision.HIGHEST)
        hidden = numerator / jnp.sqrt(denominator * denominator + 1.0)[:, :, None]
        last_seg = s_span[SPAN - 1].astype(jnp.int32)
        retain = jnp.where(last_seg == prev_seg, jnp.exp(cumulative[SPAN - 1]), 0.0)
        ending = jnp.exp(jnp.where((s_span == last_seg)[:, None], cumulative[SPAN - 1][None, :] - cumulative + i_span, NEGATIVE))
        weighted = k_span * ending[:, :, None]
        memory = retain[:, None, None] * memory + jnp.einsum('shd,she->hde', weighted, v_span, precision=lax.Precision.HIGHEST)
        normal = retain[:, None] * normal + lax.optimization_barrier(jnp.sum(weighted, axis=0))
        return ((memory, normal, last_seg), hidden)
    start_carry = (jnp.zeros((NH, DH, DH), queries.dtype), jnp.zeros((NH, DH), queries.dtype), jnp.int32(-1))
    pieces = (queries.reshape(spans, SPAN, NH, DH), key_rows.reshape(spans, SPAN, NH, DH), values.reshape(spans, SPAN, NH, DH), in_gate.reshape(spans, SPAN, NH), log_forget.reshape(spans, SPAN, NH), seg_ids.reshape(spans, SPAN).astype(jnp.int32))
    _, hidden = lax.scan(jax.checkpoint(advance), start_carry, pieces)
    return hidden.reshape(length, NH, DH)

def group_forward(params, row_block, seg_ids):
    norm_gain, up_weight, conv_weight, conv_bias, qkv_weight, gate_weight, gate_bias, group_gain, skip_gain, down_weight = params
    length = row_block.shape[0]
    centred = row_block - lax.optimization_barrier(jnp.mean(row_block, axis=1, keepdims=True))
    inv_std = lax.rsqrt(lax.optimization_barrier(jnp.mean(centred * centred, axis=1, keepdims=True)) + EPSILON)
    normed = low(centred * inv_std * norm_gain[None, :])
    lifted = low_back(matmul(normed, up_weight.reshape(D, 2 * INNER))).reshape(length, 2, INNER)
    branch = lifted[:, 0]
    out_gate = lifted[:, 1]
    conv_out = jax.nn.silu(causal_conv(branch, conv_weight, conv_bias, seg_ids))
    queries = low(blockwise(conv_out, qkv_weight[0]))
    key_rows = low(blockwise(conv_out, qkv_weight[1]))
    values = low(blockwise(branch, qkv_weight[2]))
    preact = matmul(queries, gate_weight[0]) + matmul(key_rows, gate_weight[1]) + matmul(values, gate_weight[2])
    preact = preact + gate_bias.reshape(1, 2 * NH)
    in_gate = preact[:, :NH]
    log_forget = jax.nn.log_sigmoid(preact[:, NH:])
    hidden = memory_cell(queries.reshape(length, NH, DH), key_rows.reshape(length, NH, DH), values.reshape(length, NH, DH), in_gate, log_forget, seg_ids)
    head_centred = hidden - lax.optimization_barrier(jnp.mean(hidden, axis=2, keepdims=True))
    head_normed = head_centred * lax.rsqrt(lax.optimization_barrier(jnp.mean(head_centred * head_centred, axis=2, keepdims=True)) + EPSILON)
    hnorm = head_normed.reshape(length, INNER) * group_gain[None, :]
    mixed = low((hnorm + skip_gain[None, :] * conv_out) * jax.nn.silu(out_gate))
    return row_block + matmul(mixed, down_weight)

def forward(params, inputs, seg_ids):
    grouped = inputs.reshape(N_DP, GROUP_TOK, D)
    grouped_ids = seg_ids.reshape(N_DP, GROUP_TOK).astype(jnp.int32)
    checked = jax.checkpoint(group_forward)

    def one_group(carried, pieces):
        return (carried, checked(params, pieces[0], pieces[1]))
    _, outputs = lax.scan(one_group, None, (grouped, grouped_ids))
    return outputs.reshape(TOKENS, D)

def reference(inputs, segment_ids, norm_gain, up_weight, conv_weight, conv_bias, qkv_weight, gate_weight, gate_bias, group_gain, skip_gain, down_weight, out_grad):
    params = (norm_gain.astype(jnp.float32), up_weight.astype(jnp.float32), conv_weight.astype(jnp.float32), conv_bias.astype(jnp.float32), qkv_weight.astype(jnp.float32), gate_weight.astype(jnp.float32), gate_bias.astype(jnp.float32), group_gain.astype(jnp.float32), skip_gain.astype(jnp.float32), down_weight.astype(jnp.float32))

    def wrapped(weights_in, rows_in):
        return forward(weights_in, rows_in, segment_ids)
    output, pullback = jax.vjp(wrapped, params, inputs.astype(jnp.float32))
    param_grads, input_grad = pullback(out_grad.astype(jnp.float32))
    return (output.astype(jnp.bfloat16), input_grad, param_grads[0], param_grads[1], param_grads[2], param_grads[3], param_grads[4], param_grads[5], param_grads[6], param_grads[7], param_grads[8], param_grads[9])
```

```python
import math
from functools import partial

import jax
import jax.numpy as jnp
from jax import lax
from jax.experimental import pallas as pl
from jax.experimental.pallas import tpu as pltpu
from jax.sharding import PartitionSpec as P

EPS = 1e-05
NEG = -10000.0
CH = 256
HALO = 16
TAPS = 4
F32, BF16 = jnp.float32, jnp.bfloat16
HIGHEST = lax.Precision.HIGHEST


def nn(a, b, **kw):
    return lax.dot_general(a, b, (((1,), (0,)), ((), ())), preferred_element_type=F32, **kw)


def nt(a, b, **kw):
    return lax.dot_general(a, b, (((1,), (1,)), ((), ())), preferred_element_type=F32, **kw)


def tn(a, b, **kw):
    return lax.dot_general(a, b, (((0,), (0,)), ((), ())), preferred_element_type=F32, **kw)


def sigmoid(u):
    return 0.5 * jnp.tanh(0.5 * u) + 0.5


def log_sigmoid(u):
    return jnp.minimum(u, 0.0) - jnp.log(1.0 + jnp.exp(-jnp.abs(u)))


def iota(shape, dim):
    return lax.broadcasted_iota(jnp.int32, shape, dim)


def pick(block, lane):
    return jnp.sum(jnp.where(iota(block.shape, 1) == lane, block, 0.0), axis=1, keepdims=True)


def normalised(rows):
    centred = rows - jnp.mean(rows, axis=1, keepdims=True)
    inv_std = lax.rsqrt(jnp.mean(centred * centred, axis=1, keepdims=True) + EPS)
    return centred * inv_std, inv_std


def row_chunks(total, size):
    return [(r, min(size, total - r)) for r in range(0, total, size)]


def lift_kernel(x_ref, gain_ref, link_ref, w_ref, small_ref, wqk_ref, wv_ref, gw_ref,
                q_ref, k_ref, va_ref, pre_ref, br_ref, og_ref, gates_ref, normt_ref,
                normed, ext):
    h = pl.program_id(0)
    dh = q_ref.shape[1]
    n = q_ref.shape[0]

    @pl.when(h == 0)
    def _():
        gain = gain_ref[0:1]
        unit, _ = normalised(x_ref[0:HALO].astype(F32))
        normed[0:HALO] = (unit * gain).astype(BF16)
        for r, rows in row_chunks(n, CH):
            unit, _ = normalised(x_ref[HALO + r : HALO + r + rows].astype(F32))
            scaled = unit * gain
            normed[HALO + r : HALO + r + rows] = scaled.astype(BF16)
            normt_ref[:, r : r + rows] = scaled.T.astype(BF16)
        gates_ref[...] = jnp.zeros_like(gates_ref)

    w = w_ref.at[0]
    halo = nn(normed[0:HALO], w[:, 0:dh]) * link_ref[0:1, 0:1]
    ext[0:HALO] = halo
    br_ref[0:HALO] = halo.astype(BF16)
    for r, rows in row_chunks(n, 512):
        lifted = nn(normed[HALO + r : HALO + r + rows], w[:, 0 : 2 * dh])
        branch = lifted[:, 0:dh]
        ext[HALO + r : HALO + r + rows] = branch
        og_ref[r : r + rows] = lifted[:, dh:].astype(BF16)
        branch_b = branch.astype(BF16)
        br_ref[HALO + r : HALO + r + rows] = branch_b
        pre = small_ref[0, TAPS : TAPS + 1] + small_ref[0, 0:1] * branch
        for j in range(1, TAPS):
            pre = pre + small_ref[0, j : j + 1] * ext[HALO + r - j : HALO + r - j + rows]
        pre_ref[r : r + rows] = pre.astype(BF16)
        conv = pre * sigmoid(pre)
        conv_b = conv.astype(BF16)
        conv_rest = (conv - conv_b.astype(F32)).astype(BF16)
        branch_rest = (branch - branch_b.astype(F32)).astype(BF16)
        for b in range(dh // 128):
            cols = slice(128 * b, 128 * b + 128)
            parts = [conv_b[:, cols], conv_rest[:, cols], conv_b[:, cols]]
            qk = nn(jnp.concatenate(parts, axis=1), wqk_ref[0, b]).astype(BF16)
            q_ref[r : r + rows, cols] = qk[:, 0:128]
            k_ref[r : r + rows, cols] = qk[:, 128:256]
            parts = [branch_b[:, cols], branch_rest[:, cols], branch_b[:, cols]]
            va_ref[0, r : r + rows, cols] = nn(jnp.concatenate(parts, axis=1), wv_ref[0, b]).astype(BF16)
        va_ref[0, r : r + rows, dh : dh + 128] = jnp.where(
            iota((rows, 128), 1) == 0, 1.0, 0.0
        ).astype(BF16)
        gates_ref[r : r + rows] += (
            nn(q_ref[r : r + rows], gw_ref[0, 0])
            + nn(k_ref[r : r + rows], gw_ref[0, 1])
            + nn(va_ref[0, r : r + rows, 0:dh], gw_ref[0, 2])
        )


def state_kernel(n_heads, gates_ref, bias_ref, k_ref, va_ref, gcol_ref, grow_ref, sloc_ref, st, ns):
    h = pl.program_id(0)
    n, dh = k_ref.shape

    @pl.when(h == 0)
    def _():
        lower = jnp.where(iota((CH, CH), 0) >= iota((CH, CH), 1), 1.0, 0.0)
        for r, rows in row_chunks(n, CH):
            pre = gates_ref[r : r + rows] + bias_ref[0:1]
            cum = nn(lower, log_sigmoid(pre), precision=HIGHEST)
            cum = pltpu.roll(cum, 128 - n_heads, 1)
            after = pltpu.roll(pre - cum, n_heads, 1)
            lane = iota((rows, 128), 1)
            both = jnp.where(lane < n_heads, cum, jnp.where(lane < 2 * n_heads, after, 0.0))
            gcol_ref[r : r + rows] = both
            grow_ref[:, r : r + rows] = both.T[0 : grow_ref.shape[0]]

    st[...] = jnp.zeros_like(st)
    ns[...] = jnp.zeros_like(ns)
    for c, (r, rows) in enumerate(row_chunks(n, CH)):
        block = gcol_ref[r : r + rows]
        total = pick(block[rows - 8 : rows], h)[7:8]
        ending = jnp.exp(total + pick(block, n_heads + h))
        weighted = k_ref[r : r + rows].astype(F32) * ending
        st[...] = jnp.exp(total) * st[...] + tn(va_ref[0, r : r + rows, 0:dh], weighted.astype(BF16))
        ns[...] = jnp.exp(total) * ns[...] + jnp.sum(weighted, axis=0, keepdims=True)
        sloc_ref[0, c, 0:dh] = st[...].astype(BF16)
        sloc_ref[0, c, dh : dh + 16] = jnp.where(iota((16, dh), 0) == 0, ns[0:1], 0.0).astype(BF16)


def decay_of(block, grow_ref, h, n_heads, r, rows, log_scale):
    cum = pick(block, h)
    after = grow_ref[pl.ds(n_heads + h, 1), r : r + rows]
    exponent = jnp.where(
        iota((rows, rows), 0) >= iota((rows, rows), 1), (cum + log_scale) + after, NEG
    )
    return jnp.exp(exponent), cum


def mix_kernel(n_heads, log_scale,
               x_ref, og_all_ref, ogt_ref, gcol_ref, grow_ref, q_ref, k_ref, va_ref, sloc_ref, sin_ref,
               gate_ref, pre_ref, small_ref, w_ref,
               out_ref, dng_ref, sttot_ref, gloc_ref, gaug_ref, ogg_ref, dskip_ref, sums_ref,
               acc, mixed_s, stb, gt, gn):
    h = pl.program_id(0)
    n, dh = q_ref.shape
    gain = small_ref[0, TAPS + 1 : TAPS + 2]
    skip = small_ref[0, TAPS + 2 : TAPS + 3]
    down_t = w_ref.at[0]

    @pl.when(h == 0)
    def _():
        acc[...] = jnp.zeros_like(acc)
        stb[dh + 16 :] = jnp.zeros((stb.shape[0] - dh - 16, dh), BF16)

    prefix = jnp.zeros((1, 1), F32)
    gain_sum = jnp.zeros((1, dh), F32)
    skip_sum = jnp.zeros((1, dh), F32)
    pair_sum = jnp.zeros((1, 1), F32)
    for c, (r, rows) in enumerate(row_chunks(n, CH)):
        span = slice(r, r + rows)
        block = gcol_ref[span]
        total = pick(block[rows - 8 : rows], h)[7:8]
        state = sin_ref[0].astype(F32) * jnp.exp(prefix)
        if c > 0:
            state = state + sloc_ref[0, c - 1].astype(F32)
        prefix = prefix + total
        state_b = state.astype(BF16)
        sttot_ref[0, c] = state_b
        stb[0 : dh + 16] = state_b
        decay, cum = decay_of(block, grow_ref, h, n_heads, r, rows, log_scale)
        weights = (nt(q_ref[span], k_ref[span]) * decay).astype(BF16)
        factor = jnp.exp(cum + log_scale)
        both = nn(weights, va_ref[0, span]) + factor * nt(q_ref[span], stb[...])
        denom = both[:, dh : dh + 1]
        r_inv = lax.rsqrt(denom * denom + 1.0)
        unit, inv_std = normalised(both[:, 0:dh] * r_inv)
        gate = gate_ref[span].astype(F32)
        sg = sigmoid(gate)
        silu_gate = gate * sg
        pre = pre_ref[span].astype(F32)
        conv = pre * sigmoid(pre)
        inner = unit * gain + skip * conv
        mixed = (inner * silu_gate).astype(BF16)
        mixed_s[span] = mixed
        acc[span] += nt(mixed, down_t[...])
        mixed_grad = nn(og_all_ref[span], down_t[...])
        hskip = mixed_grad * silu_gate
        ogg_ref[span] = (mixed_grad * inner * (sg * (1.0 + gate * (1.0 - sg)))).astype(BF16)
        dskip_ref[span] = (hskip * skip).astype(BF16)
        skip_sum = skip_sum + jnp.sum(hskip * conv, axis=0, keepdims=True)
        gain_sum = gain_sum + jnp.sum(hskip * unit, axis=0, keepdims=True)
        dhh = hskip * gain
        along = jnp.mean(dhh * unit, axis=1, keepdims=True)
        grad = (inv_std * r_inv) * (dhh - jnp.mean(dhh, axis=1, keepdims=True) - unit * along)
        radial = dh * EPS * along * inv_std * inv_std
        gaug_ref[0, span, 0:dh] = grad.astype(BF16)
        gaug_ref[0, span, dh : dh + 128] = jnp.where(
            iota((rows, 128), 1) == 0, -radial * denom * r_inv * r_inv, 0.0
        ).astype(BF16)
        pair_sum = pair_sum + jnp.sum(radial * r_inv * r_inv, axis=0, keepdims=True)
    sums_ref[0, 0:1] = gain_sum
    sums_ref[0, 1:2] = skip_sum
    sums_ref[0, 2:3] = jnp.broadcast_to(pair_sum, (1, dh))
    sums_ref[0, 3:8] = jnp.zeros((5, dh), F32)

    @pl.when(h == n_heads - 1)
    def _():
        for r, rows in row_chunks(n, CH):
            out_ref[r : r + rows] = (x_ref[r : r + rows].astype(F32) + acc[r : r + rows]).astype(BF16)

    dng_ref[0] = nn(ogt_ref[...], mixed_s[...]).astype(BF16)

    gt[...] = jnp.zeros_like(gt)
    gn[...] = jnp.zeros_like(gn)
    for c, (r, rows) in reversed(list(enumerate(row_chunks(n, CH)))):
        span = slice(r, r + rows)
        block = gcol_ref[span]
        cum = pick(block, h)
        keep = jnp.exp(pick(block[rows - 8 : rows], h)[7:8])
        weighted = q_ref[span].astype(F32) * jnp.exp(cum + log_scale)
        side = gaug_ref[0, span, dh : dh + 128].astype(F32)[:, 0:1]
        gt[...] = keep * gt[...] + tn(gaug_ref[0, span, 0:dh], weighted.astype(BF16))
        gn[...] = keep * gn[...] + jnp.sum(weighted * side, axis=0, keepdims=True)
        gloc_ref[0, c, 0:dh] = gt[...].astype(BF16)
        gloc_ref[0, c, dh : dh + 16] = jnp.where(iota((16, dh), 0) == 0, gn[0:1], 0.0).astype(BF16)


def memory_back_kernel(n_heads, log_scale,
                       gates_ref, bias_ref, gcol_ref, grow_ref, q_ref, k_ref, va_ref, gaug_ref,
                       sttot_ref, gloc_ref, gin_ref,
                       dq_ref, dk_ref, dv_ref, pg_ref, bsum_ref,
                       stb, gtb, cols, rowsb, across):
    h = pl.program_id(0)
    n, dh = q_ref.shape
    chunks = row_chunks(n, CH)

    @pl.when(h == 0)
    def _():
        stb[dh + 16 :] = jnp.zeros((stb.shape[0] - dh - 16, dh), BF16)
        gtb[dh + 16 :] = jnp.zeros((gtb.shape[0] - dh - 16, dh), BF16)
        cols[...] = jnp.zeros_like(cols)
        rowsb[...] = jnp.zeros_like(rowsb)
        across[...] = jnp.zeros_like(across)

    suffix = jnp.zeros((1, 1), F32)
    for c, (r, rows) in reversed(list(enumerate(chunks))):
        span = slice(r, r + rows)
        block = gcol_ref[span]
        total = pick(block[rows - 8 : rows], h)[7:8]
        after_col = pick(block, n_heads + h)
        grad_state = gin_ref[0].astype(F32) * jnp.exp(suffix)
        if c < len(chunks) - 1:
            grad_state = grad_state + gloc_ref[0, c + 1].astype(F32)
        suffix = suffix + total
        gtb[0 : dh + 16] = grad_state.astype(BF16)
        stb[0 : dh + 16] = sttot_ref[0, c]
        through = jnp.exp(total) * jnp.sum(
            jnp.sum(sttot_ref[0, c].astype(F32) * grad_state, axis=1, keepdims=True), axis=0, keepdims=True
        )
        q, k, va, gaug = q_ref[span], k_ref[span], va_ref[0, span], gaug_ref[0, span]
        decay, cum = decay_of(block, grow_ref, h, n_heads, r, rows, log_scale)
        weights = nt(q, k) * decay
        wg = nt(gaug, va)
        d_scores = (wg * decay).astype(BF16)
        pair = wg * weights
        factor = jnp.exp(cum + log_scale)
        ending = jnp.exp(total + after_col)
        dq_far = factor * nn(gaug, stb[...])
        dk_far = ending * nn(va, gtb[...])
        dv_far = ending * nt(k, gtb[...])
        dq_ref[span] = (nn(d_scores, k) + dq_far).astype(BF16)
        dk_ref[span] = (tn(d_scores, q) + dk_far).astype(BF16)
        dv_ref[span] = (tn(weights.astype(BF16), gaug[:, 0:dh]) + dv_far[:, 0:dh]).astype(BF16)
        row_sum = jnp.sum(pair, axis=1, keepdims=True) + jnp.sum(dq_far * q.astype(F32), axis=1, keepdims=True)
        col_far = jnp.sum(dk_far * k.astype(F32), axis=1, keepdims=True)
        lane = iota((rows, 128), 1)
        cols[span] = jnp.where(lane == h, row_sum, jnp.where(lane == n_heads + h, col_far, cols[span]))
        rowsb[pl.ds(h, 1), span] = jnp.sum(pair, axis=0, keepdims=True)
        across[c : c + 1] = jnp.where(iota((1, 128), 1) == h, through, across[c : c + 1])

    @pl.when(h == n_heads - 1)
    def _():
        upper = jnp.where(iota((CH, CH), 0) <= iota((CH, CH), 1), 1.0, 0.0)
        strict = jnp.where(iota((CH, CH), 0) > iota((CH, CH), 1), 1.0, 0.0)
        lane = iota((CH, 128), 1)
        bias_sum = jnp.zeros((1, 128), F32)
        for c, (r, rows) in enumerate(chunks):
            span = slice(r, r + rows)
            near_col = rowsb[:, span].T
            far = pltpu.roll(cols[span], 128 - n_heads, 1)
            forget = (
                nn(upper, cols[span] - near_col, precision=HIGHEST)
                + nn(strict, far, precision=HIGHEST)
                + across[c : c + 1]
            )
            pre = gates_ref[span] + bias_ref[0:1]
            forget = pltpu.roll(forget, n_heads, 1) * sigmoid(-pre)
            grads = jnp.where(
                lane < n_heads, near_col + far, jnp.where(lane < 2 * n_heads, forget, 0.0)
            )
            bias_sum = bias_sum + jnp.sum(grads, axis=0, keepdims=True)
            pg_ref[span] = grads.astype(BF16)
        bsum_ref[...] = jnp.where(iota((8, 128), 0) == 0, bias_sum, 0.0)


def lower_kernel(n_heads,
                 x_ref, gain_ref, link_ref, og_all_ref, normt_ref, pg_ref, q_ref, k_ref, va_ref,
                 dq_ref, dk_ref, dv_ref, pre_ref, br_ref, ogg_ref, dskip_ref,
                 small_ref, wqk_ref, wv_ref, gw_ref, w_ref, dng_ref, sums_ref,
                 upg_ref, ing_ref, corr_ref, minor_ref,
                 nacc, pext, brx, lifted, conv_s, dqk_s, dv_s):
    h = pl.program_id(0)
    n, dh = q_ref.shape
    link = link_ref[0:1, 0:1]
    w = w_ref.at[0]

    minor_out = minor_ref
    minor_ref = minor_out.at[pl.ds(h, 1)]
    minor_ref[0, 64:] = jnp.zeros((minor_ref.shape[1] - 64, dh), F32)

    @pl.when(h == 0)
    def _():
        nacc[...] = jnp.zeros_like(nacc)
        pext[0:HALO] = jnp.zeros((HALO, dh), F32)
        pext[HALO + n :] = jnp.zeros((HALO, dh), F32)

    for r, rows in row_chunks(n + HALO, 208):
        brx[r : r + rows] = br_ref[r : r + rows].astype(F32)

    taps = [jnp.zeros((1, dh), F32) for _ in range(TAPS)]
    bias_sum = jnp.zeros((1, dh), F32)
    for r, rows in row_chunks(n, CH):
        span = slice(r, r + rows)
        pg = pg_ref[span]
        dqt = (dq_ref[span].astype(F32) + nt(pg, gw_ref[0, 0])).astype(BF16)
        dkt = (dk_ref[span].astype(F32) + nt(pg, gw_ref[0, 1])).astype(BF16)
        dvt = (dv_ref[span].astype(F32) + nt(pg, gw_ref[0, 2])).astype(BF16)
        pre = pre_ref[span].astype(F32)
        sg = sigmoid(pre)
        conv_s[span] = (pre * sg).astype(BF16)
        slope = sg * (1.0 + pre * (1.0 - sg))
        dv_s[span] = dvt
        for b in range(dh // 128):
            at = slice(128 * b, 128 * b + 128)
            both = jnp.concatenate([dqt[:, at], dkt[:, at]], axis=1)
            dqk_s[span, 256 * b : 256 * b + 256] = both
            conv_grad = nt(both, wqk_ref[0, b, 0:128]) + dskip_ref[span, at].astype(F32)
            pext[HALO + r : HALO + r + rows, at] = conv_grad * slope[:, at]
        pre_grad = pext[HALO + r : HALO + r + rows]
        bias_sum = bias_sum + jnp.sum(pre_grad, axis=0, keepdims=True)
        for j in range(TAPS):
            taps[j] = taps[j] + jnp.sum(
                pre_grad * brx[HALO + r - j : HALO + r - j + rows], axis=0, keepdims=True
            )
    for j in range(TAPS):
        minor_ref[0, j : j + 1] = taps[j]
    minor_ref[0, TAPS : TAPS + 1] = bias_sum
    minor_ref[0, TAPS + 1 : 8] = jnp.zeros((8 - TAPS - 1, dh), F32)
    minor_ref[0, 8:16] = sums_ref[0]
    upg_ref[0, :, 2 * dh : 3 * dh] = dng_ref[0]

    halo_grad = jnp.zeros((HALO, dh), F32)
    for j in range(1, TAPS):
        halo_grad = halo_grad + small_ref[0, j : j + 1] * pext[j : HALO + j]
    halo_b = (halo_grad * link).astype(BF16)
    nacc[0:HALO] += nt(halo_b, w[:, 0:dh])
    for r, rows in row_chunks(n, CH):
        span = slice(r, r + rows)
        grad = jnp.zeros((rows, dh), F32)
        for j in range(TAPS):
            grad = grad + small_ref[0, j : j + 1] * pext[HALO + r + j : HALO + r + j + rows]
        for b in range(dh // 128):
            at = slice(128 * b, 128 * b + 128)
            lifted[span, at] = (grad[:, at] + nt(dv_s[span, at], wv_ref[0, b, 0:128])).astype(BF16)
        lifted[span, dh : 2 * dh] = ogg_ref[span]
        nacc[HALO + r : HALO + r + rows] += nt(lifted[span], w[...])

    unit_halo, std_halo = normalised(x_ref[0:HALO].astype(F32))
    gain = gain_ref[0:1]
    upg = nn(normt_ref[...], lifted[...])
    upg_ref[0, :, dh : 2 * dh] = upg[:, dh:].astype(BF16)
    upg_ref[0, :, 0:dh] = (upg[:, 0:dh] + tn((unit_halo * gain).astype(BF16), halo_b)).astype(BF16)

    fold = jnp.where(iota((8, 128), 1) % 4 == iota((8, 128), 0), 1.0, 0.0)
    diagonal = iota((128, 128), 0) // 4 == iota((128, 128), 1) // 4
    for b in range(dh // 128):
        at = slice(128 * b, 128 * b + 128)
        qk_grad = tn(conv_s[:, at], dqk_s[:, 256 * b : 256 * b + 256])
        v_grad = tn(brx[HALO:, at].astype(BF16), dv_s[:, at])
        for m, full in enumerate((qk_grad[:, 0:128], qk_grad[:, 128:256], v_grad)):
            minor_ref[0, 16 + 8 * m : 24 + 8 * m, at] = nt(fold, jnp.where(diagonal, full, 0.0), precision=HIGHEST)
    minor_ref[0, 40:48] = tn(pg_ref[...], q_ref[...])[0:8]
    minor_ref[0, 48:56] = tn(pg_ref[...], k_ref[...])[0:8]
    minor_ref[0, 56:64] = tn(pg_ref[...], va_ref[0, :, 0:dh])[0:8]

    @pl.when(h == n_heads - 1)
    def _():
        def back(normed_grad, unit, inv_std):
            scaled = normed_grad * gain
            return inv_std * (
                scaled
                - jnp.mean(scaled, axis=1, keepdims=True)
                - unit * jnp.mean(scaled * unit, axis=1, keepdims=True)
            )

        corr_ref[...] = back(nacc[0:HALO], unit_halo, std_halo)
        total = jnp.sum(nacc[0:HALO] * unit_halo, axis=0, keepdims=True)
        for r, rows in row_chunks(n, CH):
            unit, inv_std = normalised(x_ref[HALO + r : HALO + r + rows].astype(F32))
            grads = nacc[HALO + r : HALO + r + rows]
            total = total + jnp.sum(grads * unit, axis=0, keepdims=True)
            ing_ref[r : r + rows] = og_all_ref[r : r + rows].astype(F32) + back(grads, unit, inv_std)
        for i in range(n_heads):
            for j in range(total.shape[1] // dh):
                minor_out[i, 64 + j : 65 + j] = total[:, dh * j : dh * j + dh]


def whole(shape):
    return pl.BlockSpec(shape, lambda h: (0,) * len(shape))


def head_cols(rows, cols):
    return pl.BlockSpec((rows, cols), lambda h: (0, h))


def head_lead(*shape, last=0):
    return pl.BlockSpec((1, *shape), lambda h: (h,) + (0,) * (len(shape) - 1) + (last,))


def params(**kw):
    return pltpu.CompilerParams(dimension_semantics=("arbitrary",), vmem_limit_bytes=60 << 20, **kw)


def sds(shape, dtype):
    return jax.ShapeDtypeStruct(shape, dtype)


def shifted(x, by):
    heads = lax.axis_size("head")
    pairs = [(i, i + by) for i in range(heads) if 0 <= i + by < heads]
    return lax.ppermute(x, "head", pairs)


MESH = pl.DeviceIdType.MESH


class Place:
    def __init__(self):
        dp, head = lax.axis_index("dp"), lax.axis_index("head")
        self.z, self.y = lax.div(dp, 2), lax.rem(dp, 2)
        self.x, self.c = lax.div(head, 2), lax.rem(head, 2)

    def along_z(self, k):
        z = self.z
        return (z, z + 1 - 2 * lax.rem(z, 2), lax.rem(z + 2, 4), 3 - z)[k]

    def device(self, k=0, fy=0, fx=0, fc=0):
        y, x, c = (1 - v if f else v for v, f in ((self.y, fy), (self.x, fx), (self.c, fc)))
        return (self.along_z(k) * 2 + y, x * 2 + c)

    def rows(self, k, fy, size):
        y = 1 - self.y if fy else self.y
        return pl.multiple_of((self.along_z(k) * 2 + y) * size, 16)


NEIGHBOURS = (dict(fc=1), dict(fx=1), dict(fx=1, fc=1), dict(fy=1), dict(k=1), dict(k=2), dict(k=3))


def greet(devices):
    barrier = pltpu.get_barrier_semaphore()
    for device in devices:
        pl.semaphore_signal(barrier, inc=1, device_id=device, device_id_type=MESH)
    pl.semaphore_wait(barrier, len(devices))


def remote(src, dst, sems, at, device):
    send, recv = sems
    return pltpu.make_async_remote_copy(
        src_ref=src, dst_ref=dst, send_sem=send.at[at], recv_sem=recv.at[at], device_id=device, device_id_type=MESH
    )


def gather_kernel(shard, pack, gates, x, w, pack_all, gates_all, halo,
                  local_sem, zs, zr, fs, fr, ss, sr, ds, dr, ms, mr):
    here = Place()
    rows = shard.shape[0]
    half = rows // 2
    n = x.shape[0]
    flips = ((dict(fx=1), dict(fy=1)), (dict(fy=1), dict(fx=1)))

    def block(p, k=0, fy=0, fx=0, fc=0):
        xx = 1 - here.x if fx else here.x
        cc = 1 - here.c if fc else here.c
        return w.at[xx * 2 + cc, pl.ds(here.rows(k, fy, rows) + half * p, half)]

    own = [pltpu.make_async_copy(shard, w.at[here.x * 2 + here.c, pl.ds(here.rows(0, 0, rows), rows)], local_sem.at[0])]
    own.append(pltpu.make_async_copy(pack, pack_all.at[here.x * 2 + here.c], local_sem.at[1]))
    own.append(pltpu.make_async_copy(gates, gates_all.at[here.x * 2 + here.c], local_sem.at[2]))
    for copy in own:
        copy.start()
    greet([here.device(**to) for to in NEIGHBOURS])
    started = []

    def send(src, dst, sems, at, to):
        copy = remote(src, dst, sems, at, here.device(**to))
        copy.start()
        started.append(copy)

    def arrived(dst, sems, at):
        remote(dst, dst, sems, at, here.device(fc=1)).wait_recv()

    for p in (0, 1):
        mine = shard.at[pl.ds(half * p, half)]
        first, second = flips[p]
        send(mine, block(p), (fs, fr), (p, 0), first)
        send(mine, block(p), (ss, sr), (p, 0, 0), second)
        for k in (1, 2, 3):
            send(mine, block(p), (zs, zr), (p, k - 1), dict(k=k))
        send(mine, block(p), (ds, dr), (p, 0, 0), dict(fc=1))
    for i, to in enumerate(NEIGHBOURS[:3]):
        send(pack, pack_all.at[here.x * 2 + here.c], (ms, mr), (0, i), to)
        send(gates, gates_all.at[here.x * 2 + here.c], (ms, mr), (1, i), to)
    head = here.x * 2 + here.c
    after = lax.rem(head + 1, 4)
    copy = pltpu.make_async_remote_copy(
        src_ref=x.at[pl.ds(n - HALO, HALO)], dst_ref=halo, send_sem=ms.at[2, 0], recv_sem=mr.at[2, 0],
        device_id=(here.z * 2 + here.y, after), device_id_type=MESH,
    )
    copy.start()
    started.append(copy)
    for k in (1, 2, 3):
        for p in (0, 1):
            first, second = flips[p]
            arrived(block(p, k), (zs, zr), (p, k - 1))
            send(block(p, k), block(p, k), (fs, fr), (p, k), first)
            send(block(p, k), block(p, k), (ss, sr), (p, k, 0), second)
            send(block(p, k), block(p, k), (ds, dr), (p, k, 0), dict(fc=1))
    for k in range(4):
        for p in (0, 1):
            first, second = flips[p]
            arrived(block(p, k, **first), (fs, fr), (p, k))
            send(block(p, k, **first), block(p, k, **first), (ss, sr), (p, k, 1), second)
            send(block(p, k, **first), block(p, k, **first), (ds, dr), (p, k, 1), dict(fc=1))
    for k in range(4):
        for p in (0, 1):
            first, second = flips[p]
            for i, over in enumerate((second, dict(**first, **second))):
                arrived(block(p, k, **over), (ss, sr), (p, k, i))
                send(block(p, k, **over), block(p, k, **over), (ds, dr), (p, k, 2 + i), dict(fc=1))
    for k in range(4):
        for p in (0, 1):
            first, second = flips[p]
            for i, over in enumerate((dict(), first, second, dict(**first, **second))):
                arrived(block(p, k, fc=1, **over), (ds, dr), (p, k, i))
    for i, to in enumerate(NEIGHBOURS[:3]):
        who = (1 - here.x if to.get("fx") else here.x) * 2 + (1 - here.c if to.get("fc") else here.c)
        arrived(pack_all.at[who], (ms, mr), (0, i))
        arrived(gates_all.at[who], (ms, mr), (1, i))
    arrived(halo, (ms, mr), (2, 0))
    for copy in started:
        copy.wait_send()
    for copy in own:
        copy.wait()


def gathered(shard, pack, gates, x, heads):
    dp = lax.axis_size("dp")
    rows, cols = shard.shape
    n, d = x.shape
    if not by_hand(rows):
        w = lax.all_gather(shard, ("dp", "head"), axis=0)
        w = w.reshape(dp, heads, rows, cols).transpose(1, 0, 2, 3).reshape(heads, dp * rows, cols)
        return (w, lax.all_gather(pack, "head", axis=0), lax.all_gather(gates, "head", axis=0),
                shifted(x[n - HALO :], 1))
    sem = pltpu.SemaphoreType.DMA
    return pl.pallas_call(
        gather_kernel,
        out_shape=[sds((heads, dp * rows, cols), BF16), sds((heads, *pack.shape), F32),
                   sds((heads, *gates.shape), BF16), sds((HALO, d), BF16)],
        in_specs=[pl.BlockSpec(memory_space=pl.ANY)] * 4,
        out_specs=[pl.BlockSpec(memory_space=pl.ANY)] * 4,
        scratch_shapes=[sem((3,)), sem((2, 3)), sem((2, 3)), sem((2, 4)), sem((2, 4)), sem((2, 4, 2)), sem((2, 4, 2)),
                        sem((2, 4, 4)), sem((2, 4, 4)), sem((3, 3)), sem((3, 3))],
        compiler_params=pltpu.CompilerParams(collective_id=0, has_side_effects=True),
        name="gather",
    )(shard, pack, gates, x)


def by_hand(rows):
    return lax.axis_size("dp") == 8 and lax.axis_size("head") == 4 and rows % 32 == 0


def scatter_kernel(part, minor, total, minor_total,
                   own, r0, r1a, r1b, r2, r3, m0, m1, n0, n1,
                   load, s0, t0, s1, t1, s2, t2, s3, t3, ms, mr):
    here = Place()
    rows = total.shape[0]
    half = rows // 2
    spans = (pl.ds(0, half), pl.ds(half, half))
    order = (1, 2, 3, 0)

    def block(k, fy, fx, fc):
        xx = 1 - here.x if fx else here.x
        cc = 1 - here.c if fc else here.c
        return part.at[xx * 2 + cc, pl.ds(here.rows(k, fy, rows), rows)]

    def head(fx, fc):
        return (1 - here.x if fx else here.x) * 2 + (1 - here.c if fc else here.c)

    loads = {}
    for k in order:
        for fx in (1, 0):
            for fy in (1, 0):
                loads[k, fx, fy] = pltpu.make_async_copy(block(k, fy, fx, 0), own.at[fx, k, fy], load.at[fx, k, fy])
                loads[k, fx, fy].start()
    small = [pltpu.make_async_copy(minor.at[head(fx, 0)], m0.at[fx], load.at[fx, 4, 0]) for fx in (0, 1)]
    for copy in small:
        copy.start()
    greet([here.device(**to) for to in NEIGHBOURS])
    started = []

    def send(src, dst, sems, at, to):
        copy = remote(src, dst, sems, at, here.device(**to))
        copy.start()
        started.append(copy)

    def arrived(dst, sems, at):
        remote(dst, dst, sems, at, here.device(fc=1)).wait_recv()

    def add(into, other):
        into[...] = (into[...].astype(F32) + other[...].astype(F32)).astype(into.dtype)

    for fx in (0, 1):
        send(minor.at[head(fx, 1)], n0.at[fx], (ms, mr), fx, dict(fc=1))
    for k in order:
        for fx in (1, 0):
            for fy in (1, 0):
                send(block(k, fy, fx, 1), r0.at[fx, k, fy], (s0, t0), (fx, k, fy), dict(fc=1))
    for fx in (0, 1):
        small[fx].wait()
        arrived(n0.at[fx], (ms, mr), fx)
        add(m0.at[fx], n0.at[fx])
    send(m0.at[1], n1.at[0], (ms, mr), 2, dict(fx=1))
    for k in order:
        for fx in (1, 0):
            for fy in (1, 0):
                loads[k, fx, fy].wait()
                arrived(r0.at[fx, k, fy], (s0, t0), (fx, k, fy))
                add(own.at[fx, k, fy], r0.at[fx, k, fy])
                if fy:
                    send(own.at[fx, k, 1, spans[0]], r1a.at[fx, k], (s1, t1), (0, fx, k), dict(fy=1))
                if fx:
                    send(own.at[1, k, fy, spans[1]], r1b.at[fy, k], (s1, t1), (1, fy, k), dict(fx=1))
    arrived(n1.at[0], (ms, mr), 2)
    m1[0] = m0[0] + n1[0]
    send(m1.at[0], n1.at[1], (ms, mr), 3, dict(fy=1))
    for k in order:
        for f in (1, 0):
            arrived(r1a.at[f, k], (s1, t1), (0, f, k))
            add(own.at[f, k, 0, spans[0]], r1a.at[f, k])
            if f:
                send(own.at[1, k, 0, spans[0]], r2.at[0, k], (s2, t2), (0, k), dict(fx=1))
            arrived(r1b.at[f, k], (s1, t1), (1, f, k))
            add(own.at[0, k, f, spans[1]], r1b.at[f, k])
            if f:
                send(own.at[0, k, 1, spans[1]], r2.at[1, k], (s2, t2), (1, k), dict(fy=1))
    arrived(n1.at[1], (ms, mr), 3)
    m1[1] = m1[0] + n1[1]
    send(m1.at[1], n1.at[2], (ms, mr), 4, dict(k=1))
    for k in order:
        for p in (0, 1):
            arrived(r2.at[p, k], (s2, t2), (p, k))
            add(own.at[0, k, 0, spans[p]], r2.at[p, k])
            if k:
                send(own.at[0, k, 0, spans[p]], r3.at[p, k - 1], (s3, t3), (p, k - 1), dict(k=k))
    arrived(n1.at[2], (ms, mr), 4)
    m1[2] = m1[1] + n1[2]
    send(m1.at[2], n1.at[3], (ms, mr), 5, dict(k=2))
    for p in (0, 1):
        summed = own[0, 0, 0, spans[p]].astype(F32)
        for k in range(3):
            arrived(r3.at[p, k], (s3, t3), (p, k))
            summed = summed + r3[p, k].astype(F32)
        total[spans[p]] = summed
    arrived(n1.at[3], (ms, mr), 5)
    minor_total[...] = m1[2] + n1[3]
    for copy in started:
        copy.wait_send()


def scattered(part, minor):
    dp = lax.axis_size("dp")
    heads, d, cols = part.shape
    rows = d // dp
    if not by_hand(rows):
        part = lax.psum_scatter(part, "head", scatter_dimension=0, tiled=True)
        part = lax.psum_scatter(part, "dp", scatter_dimension=1, tiled=True)[0].astype(F32)
        return part, lax.psum(lax.psum_scatter(minor, "head", scatter_dimension=0, tiled=True), "dp")[0]
    sem = pltpu.SemaphoreType.DMA
    half = rows // 2
    lines = minor.shape[1:]
    vmem = pl.BlockSpec(memory_space=pltpu.VMEM)
    return pl.pallas_call(
        scatter_kernel,
        out_shape=[sds((rows, cols), F32), sds(lines, F32)],
        in_specs=[pl.BlockSpec(memory_space=pl.ANY)] * 2,
        out_specs=[vmem] * 2,
        scratch_shapes=[
            pltpu.VMEM((2, 4, 2, rows, cols), BF16), pltpu.VMEM((2, 4, 2, rows, cols), BF16),
            pltpu.VMEM((2, 4, half, cols), BF16), pltpu.VMEM((2, 4, half, cols), BF16),
            pltpu.VMEM((2, 4, half, cols), BF16), pltpu.VMEM((2, 3, half, cols), BF16),
            pltpu.VMEM((2, *lines), F32), pltpu.VMEM((3, *lines), F32),
            pltpu.VMEM((2, *lines), F32), pltpu.VMEM((4, *lines), F32),
            sem((2, 5, 2)), sem((2, 4, 2)), sem((2, 4, 2)), sem((2, 2, 4)), sem((2, 2, 4)), sem((2, 4)), sem((2, 4)),
            sem((2, 3)), sem((2, 3)), sem((6,)), sem((6,)),
        ],
        compiler_params=pltpu.CompilerParams(collective_id=1, has_side_effects=True, vmem_limit_bytes=60 << 20),
        name="scatter",
    )(part, minor)


def chain_kernel(by, own, retain, link, entering, leaving, landed, ss, rs):
    dp, head = lax.axis_index("dp"), lax.axis_index("head")
    heads = lax.axis_size("head")
    ahead = lax.rem(head + 1, heads)
    behind = lax.rem(head + heads - 1, heads)
    greet([(dp, ahead), (dp, behind)])
    first, last = (0, heads - 1) if by > 0 else (heads - 1, 0)
    to = (dp, ahead if by > 0 else behind)
    for i in range(own.shape[0]):
        copy = remote(leaving.at[i], landed.at[i], (ss, rs), i, to)

        @pl.when(head != first)
        def _():
            copy.wait_recv()
            entering[i] = (landed[i].astype(F32) * link[0:1, 0:1]).astype(BF16)

        @pl.when(head == first)
        def _():
            entering[i] = jnp.zeros(entering.shape[1:], BF16)

        leaving[i] = (own[i].astype(F32) + entering[i].astype(F32) * retain[i, 0:1, 0:1]).astype(BF16)

        @pl.when(head != last)
        def _():
            copy.start()

    for i in range(own.shape[0]):
        copy = remote(leaving.at[i], landed.at[i], (ss, rs), i, to)

        @pl.when(head != last)
        def _():
            copy.wait_send()


def chain(own, retain, link, by):
    vmem = pl.BlockSpec(memory_space=pltpu.VMEM)
    sem = pltpu.SemaphoreType.DMA((own.shape[0],))
    return pl.pallas_call(
        partial(chain_kernel, by),
        out_shape=sds(own.shape, BF16),
        in_specs=[vmem] * 3,
        out_specs=vmem,
        scratch_shapes=[pltpu.VMEM(own.shape, BF16), pltpu.VMEM(own.shape, BF16), sem, sem],
        compiler_params=pltpu.CompilerParams(
            collective_id=2 if by > 0 else 3, has_side_effects=True, vmem_limit_bytes=32 << 20
        ),
        name="chain",
    )(own, retain, link)


def local(inputs, segment_ids, norm_gain, up_weight, conv_weight, conv_bias, qkv_weight,
          gate_weight, gate_bias, group_gain, skip_gain, down_weight, out_grad):
    H = lax.axis_size("head")
    n, d = inputs.shape
    dh = up_weight.shape[2]
    inner = H * dh
    srows = dh + 16
    nch = n // CH
    log_scale = -0.5 * math.log(dh)
    me = lax.axis_index("head")

    own_seg = lax.dynamic_slice_in_dim(segment_ids, me * n, 1)
    prev_seg = lax.dynamic_slice_in_dim(segment_ids, jnp.maximum(me * n - 1, 0), 1)
    next_seg = lax.dynamic_slice_in_dim(segment_ids, jnp.minimum(me * n + n, segment_ids.shape[0] - 1), 1)
    link_prev = jnp.where((me > 0) & (own_seg == prev_seg), 1.0, 0.0).astype(F32)[0]
    link_next = jnp.where((me < H - 1) & (own_seg == next_seg), 1.0, 0.0).astype(F32)[0]
    link = jnp.full((8, 128), link_prev, F32)

    shard = jnp.concatenate([up_weight.reshape(up_weight.shape[0], 2 * dh), down_weight.T], axis=1)
    qkv_rows = qkv_weight.reshape(3, dh, 4).transpose(0, 2, 1).reshape(12, dh)
    bias_row = jnp.pad(gate_bias[:, 0], (0, dh - 2))[None]
    pack = jnp.concatenate([conv_weight, conv_bias[None], group_gain[None], skip_gain[None], bias_row, qkv_rows,
                            jnp.zeros((4, dh), F32)])
    gate_rows = gate_weight.transpose(0, 2, 1).reshape(6 * H, dh)
    gate_rows = jnp.pad(gate_rows, ((0, -6 * H % 16), (0, 0)))
    w_all, pack, gate_rows, halo = gathered(shard, pack, gate_rows, inputs, H)
    small = pack[:, 0:8]
    qkv_full = pack[:, 8:20].reshape(H, 3, 4, dh // 128, 128).transpose(0, 1, 3, 4, 2)
    diagonal = jnp.arange(128)[:, None] // 4 == jnp.arange(128)[None, :] // 4
    dense = jnp.where(diagonal, jnp.tile(qkv_full, (1, 1, 1, 1, 32)), 0.0)
    high = lax.reduce_precision(dense, 8, 7)
    low = (dense - high).astype(BF16)
    high = high.astype(BF16)
    dense = jnp.concatenate([high, high, low], axis=3)
    wqk = jnp.concatenate([dense[:, 0], dense[:, 1]], axis=-1)
    wv = dense[:, 2]
    gw = gate_rows[:, 0 : 6 * H].reshape(H, 3, 2 * H, dh).transpose(0, 1, 3, 2)
    gw = jnp.pad(gw, ((0, 0), (0, 0), (0, 0), (0, 128 - 2 * H)))
    bias = pack[:, 7, 0:2].T.reshape(1, 2 * H)
    bias = jnp.pad(bias, ((0, 7), (0, 128 - 2 * H)))

    x_ext = jnp.concatenate([halo, inputs])
    gain = jnp.broadcast_to(norm_gain[None], (8, d))

    q, k, va, pre, br, og, gates, normt = pl.pallas_call(
        lift_kernel,
        grid=(H,),
        out_shape=[
            sds((n, inner), BF16), sds((n, inner), BF16), sds((H, n, dh + 128), BF16), sds((n, inner), BF16),
            sds((n + HALO, inner), BF16), sds((n, inner), BF16), sds((n, 128), F32), sds((d, n), BF16),
        ],
        in_specs=[
            whole((n + HALO, d)), whole((8, d)), whole((8, 128)), head_lead(d, 2 * dh), head_lead(8, dh),
            head_lead(dh // 128, 384, 256), head_lead(dh // 128, 384, 128), head_lead(3, dh, 128),
        ],
        out_specs=[
            head_cols(n, dh), head_cols(n, dh), head_lead(n, dh + 128), head_cols(n, dh),
            head_cols(n + HALO, dh), head_cols(n, dh), whole((n, 128)), whole((d, n)),
        ],
        scratch_shapes=[pltpu.VMEM((n + HALO, d), BF16), pltpu.VMEM((n + HALO, dh), F32)],
        compiler_params=params(),
        name="lift",
    )(x_ext, gain, link, w_all, small, wqk, wv, gw)

    def call_heads(kernel, name, ins, outs, scratch):
        return pl.pallas_call(
            kernel, grid=(H,), out_shape=[o[0] for o in outs], in_specs=[i[1] for i in ins],
            out_specs=[o[1] for o in outs], scratch_shapes=scratch, compiler_params=params(), name=name,
        )(*[i[0] for i in ins])

    gcol, grow, sloc = call_heads(
        partial(state_kernel, H), "states",
        [(gates, whole((n, 128))), (bias, whole((8, 128))), (k, head_cols(n, dh)), (va, head_lead(n, dh + 128))],
        [(sds((n, 128), F32), whole((n, 128))), (sds((8, n), F32), whole((8, n))),
         (sds((H, nch, srows, dh), BF16), head_lead(nch, srows, dh))],
        [pltpu.VMEM((dh, dh), F32), pltpu.VMEM((1, dh), F32)],
    )
    totals = gcol[CH - 1 :: CH, 0:H].sum(axis=0)
    retain = jnp.exp(totals)[:, None, None]

    flags = jnp.stack([link_prev, link_next])
    flags = jnp.broadcast_to(flags[:, None, None], (2, 8, 128))
    retain = jnp.broadcast_to(retain, (H, 8, 128))
    sin = chain(sloc[:, nch - 1], retain, flags[0], 1)

    ogt = out_grad.T
    output, dng, sttot, gloc, gaug, ogg, dskip, sums = call_heads(
        partial(mix_kernel, H, log_scale), "mix",
        [(inputs, whole((n, d))), (out_grad, whole((n, d))), (ogt, whole((d, n))), (gcol, whole((n, 128))),
         (grow, whole((8, n))), (q, head_cols(n, dh)), (k, head_cols(n, dh)), (va, head_lead(n, dh + 128)),
         (sloc, head_lead(nch, srows, dh)), (sin, head_lead(srows, dh)), (og, head_cols(n, dh)),
         (pre, head_cols(n, dh)), (small, head_lead(8, dh)), (w_all, head_lead(d, dh, last=2))],
        [(sds((n, d), BF16), whole((n, d))), (sds((H, d, dh), BF16), head_lead(d, dh)),
         (sds((H, nch, srows, dh), BF16), head_lead(nch, srows, dh)),
         (sds((H, nch, srows, dh), BF16), head_lead(nch, srows, dh)),
         (sds((H, n, dh + 128), BF16), head_lead(n, dh + 128)), (sds((n, inner), BF16), head_cols(n, dh)),
         (sds((n, inner), BF16), head_cols(n, dh)), (sds((H, 8, dh), F32), head_lead(8, dh))],
        [pltpu.VMEM((n, d), F32), pltpu.VMEM((n, dh), BF16), pltpu.VMEM((dh + 128, dh), BF16),
         pltpu.VMEM((dh, dh), F32), pltpu.VMEM((1, dh), F32)],
    )

    gin = chain(gloc[:, 0], retain, flags[1], -1)

    dq, dk, dv, pg, bsum = call_heads(
        partial(memory_back_kernel, H, log_scale), "memory_back",
        [(gates, whole((n, 128))), (bias, whole((8, 128))), (gcol, whole((n, 128))), (grow, whole((8, n))),
         (q, head_cols(n, dh)), (k, head_cols(n, dh)), (va, head_lead(n, dh + 128)), (gaug, head_lead(n, dh + 128)),
         (sttot, head_lead(nch, srows, dh)), (gloc, head_lead(nch, srows, dh)), (gin, head_lead(srows, dh))],
        [(sds((n, inner), BF16), head_cols(n, dh))] * 3
        + [(sds((n, 128), BF16), whole((n, 128))), (sds((8, 128), F32), whole((8, 128)))],
        [pltpu.VMEM((dh + 128, dh), BF16), pltpu.VMEM((dh + 128, dh), BF16), pltpu.VMEM((n, 128), F32),
         pltpu.VMEM((128, n), F32), pltpu.VMEM((8, 128), F32)],
    )

    grads, ing, corr, minor = call_heads(
        partial(lower_kernel, H), "lower",
        [(x_ext, whole((n + HALO, d))), (gain, whole((8, d))), (link, whole((8, 128))), (out_grad, whole((n, d))),
         (normt, whole((d, n))), (pg, whole((n, 128))), (q, head_cols(n, dh)), (k, head_cols(n, dh)),
         (va, head_lead(n, dh + 128)), (dq, head_cols(n, dh)), (dk, head_cols(n, dh)), (dv, head_cols(n, dh)),
         (pre, head_cols(n, dh)), (br, head_cols(n + HALO, dh)), (ogg, head_cols(n, dh)), (dskip, head_cols(n, dh)),
         (small, head_lead(8, dh)), (wqk, head_lead(dh // 128, 384, 256)), (wv, head_lead(dh // 128, 384, 128)),
         (gw, head_lead(3, dh, 128)), (w_all, head_lead(d, 2 * dh)),
         (dng, head_lead(d, dh)), (sums, head_lead(8, dh))],
        [(sds((H, d, 3 * dh), BF16), head_lead(d, 3 * dh)), (sds((n, d), F32), whole((n, d))),
         (sds((HALO, d), F32), whole((HALO, d))), (sds((H, 72, dh), F32), whole((H, 72, dh)))],
        [pltpu.VMEM((n + HALO, d), F32), pltpu.VMEM((n + 2 * HALO, dh), F32), pltpu.VMEM((n + HALO, dh), F32),
         pltpu.VMEM((n, 2 * dh), BF16), pltpu.VMEM((n, dh), BF16), pltpu.VMEM((n, 2 * dh), BF16),
         pltpu.VMEM((n, dh), BF16)],
    )

    ing = ing.at[n - HALO :].add(shifted(corr, -1))

    minor = minor.at[:, 66, 0].set(bsum[0, H : 2 * H])
    total, minor = scattered(grads, minor)
    return (
        output, ing, minor[64 : 64 + d // dh].reshape(d), total[:, 0 : 2 * dh].reshape(up_weight.shape),
        minor[0:TAPS], minor[TAPS], minor[16:40].reshape(3, 8, dh // 4, 4)[:, 0:4].transpose(0, 2, 3, 1),
        minor[40:64].reshape(3, 8, dh)[:, 0 : 2 * H].transpose(0, 2, 1),
        jnp.stack([minor[10, 0:1], minor[66, 0:1]]), minor[8], minor[9], total[:, 2 * dh :].T,
    )


def solution(mesh):
    rows = P(("dp", "head"), None)
    small = (P(None, "head"), P("head"), P(None, "head", None, None), P(None, "head", None), P(None, "head"))
    return jax.shard_map(
        local,
        mesh=mesh,
        in_specs=(rows, P("dp"), P(), P("dp", None, "head"), *small, P("head"), P("head"), P("head", "dp"), rows),
        out_specs=(rows, rows, P(), P("dp", None, "head"), *small, P("head"), P("head"), P("head", "dp")),
        check_vma=False,
    )
```

```python
import math
from functools import partial

import jax
import jax.numpy as jnp
from jax import lax
from jax.experimental import pallas as pl
from jax.experimental.pallas import tpu as pltpu
from jax.sharding import PartitionSpec as P

EPS = 1e-05
NEG = -10000.0
CH = 256
HALO = 16
TAPS = 4
F32, BF16 = jnp.float32, jnp.bfloat16
HIGHEST = lax.Precision.HIGHEST


def nn(a, b, **kw):
    return lax.dot_general(a, b, (((1,), (0,)), ((), ())), preferred_element_type=F32, **kw)


def nt(a, b, **kw):
    return lax.dot_general(a, b, (((1,), (1,)), ((), ())), preferred_element_type=F32, **kw)


def tn(a, b, **kw):
    return lax.dot_general(a, b, (((0,), (0,)), ((), ())), preferred_element_type=F32, **kw)


def sigmoid(u):
    return 0.5 * jnp.tanh(0.5 * u) + 0.5


def log_sigmoid(u):
    return jnp.minimum(u, 0.0) - jnp.log(1.0 + jnp.exp(-jnp.abs(u)))


def iota(shape, dim):
    return lax.broadcasted_iota(jnp.int32, shape, dim)


def pick(block, lane):
    return jnp.sum(jnp.where(iota(block.shape, 1) == lane, block, 0.0), axis=1, keepdims=True)


def normalised(rows):
    centred = rows - jnp.mean(rows, axis=1, keepdims=True)
    inv_std = lax.rsqrt(jnp.mean(centred * centred, axis=1, keepdims=True) + EPS)
    return centred * inv_std, inv_std


def row_chunks(total, size):
    return [(r, min(size, total - r)) for r in range(0, total, size)]


def maps_of(pack_ref, cols, rest):
    rows = pack_ref[0, 8:24, cols]
    high = rows.astype(BF16)
    parts = [high]
    if rest:
        parts.append((rows - high.astype(F32)).astype(BF16))
    diagonal = iota((128, 128), 0) // 4 == iota((128, 128), 1) // 4
    made = []
    for part in parts:
        made.append([])
        for m in range(3):
            chosen = jnp.where(iota((16, 128), 0) == 4 * m + iota((16, 128), 1) % 4, 1.0, 0.0).astype(BF16)
            made[-1].append(jnp.where(diagonal, tn(part, chosen), 0.0).astype(BF16))
    return made


def gate_maps(pack_ref, into):
    for m in range(3):
        rows = pack_ref[0, 24 + 8 * m : 32 + 8 * m]
        into[m, 0:16] = jnp.concatenate([rows, jnp.zeros_like(rows)], axis=0).astype(BF16)


def lift_kernel(n_heads, x_ref, halo_ref, gain_ref, seg_ref, pack_ref, w_ref,
                q_ref, k_ref, va_ref, pre_ref, br_ref, og_ref, gates_ref, normt_ref, flags_ref,
                normed, ext, wqk, wv, gw):
    h = pl.program_id(0)
    n, dh = q_ref.shape
    me = lax.axis_index("head")

    @pl.when(h == 0)
    def _():
        gain = jnp.concatenate([gain_ref[j : j + 1] for j in range(gain_ref.shape[0])], axis=1)
        unit, _ = normalised(halo_ref[...].astype(F32))
        normed[0:HALO] = (unit * gain).astype(BF16)
        for r, rows in row_chunks(n, CH):
            unit, _ = normalised(x_ref[r : r + rows].astype(F32))
            scaled = unit * gain
            normed[HALO + r : HALO + r + rows] = scaled.astype(BF16)
            normt_ref[:, r : r + rows] = scaled.T.astype(BF16)
        gates_ref[...] = jnp.zeros_like(gates_ref)
        gw[...] = jnp.zeros_like(gw)
        token = iota(seg_ref.shape, 0) * 128 + iota(seg_ref.shape, 1)

        def segment(at):
            found = jnp.where(token == at, seg_ref[...], 0).astype(F32)
            return jnp.sum(jnp.sum(found, axis=1, keepdims=True), axis=0, keepdims=True)

        own = segment(me * n)
        before = jnp.where((segment(me * n - 1) == own) & (me > 0), 1.0, 0.0)
        after = jnp.where((segment(me * n + n) == own) & (me < n_heads - 1), 1.0, 0.0)
        flags_ref[0:8] = jnp.broadcast_to(before, (8, 128))
        flags_ref[8:16] = jnp.broadcast_to(after, (8, 128))

    gate_maps(pack_ref, gw)
    for b in range(dh // 128):
        (q_high, k_high, v_high), (q_rest, k_rest, v_rest) = maps_of(pack_ref, slice(128 * b, 128 * b + 128), True)
        for at, high, rest in ((0, q_high, q_rest), (128, k_high, k_rest)):
            wqk[b, 0:128, at : at + 128] = high
            wqk[b, 128:256, at : at + 128] = high
            wqk[b, 256:384, at : at + 128] = rest
        wv[b, 0:128] = v_high
        wv[b, 128:256] = v_high
        wv[b, 256:384] = v_rest
    lane = iota((1, 128), 1)
    bias = jnp.where(lane == h, pack_ref[0, 7:8, 0:1], 0.0) + jnp.where(lane == n_heads + h, pack_ref[0, 7:8, 1:2], 0.0)

    w = w_ref.at[0]
    halo = nn(normed[0:HALO], w[:, 0:dh]) * flags_ref[0:1, 0:1]
    ext[0:HALO] = halo
    br_ref[0:HALO] = halo.astype(BF16)
    for r, rows in row_chunks(n, 512):
        lifted = nn(normed[HALO + r : HALO + r + rows], w[...])
        branch = lifted[:, 0:dh]
        ext[HALO + r : HALO + r + rows] = branch
        og_ref[r : r + rows] = lifted[:, dh:].astype(BF16)
        branch_b = branch.astype(BF16)
        br_ref[HALO + r : HALO + r + rows] = branch_b
        pre = pack_ref[0, TAPS : TAPS + 1] + pack_ref[0, 0:1] * branch
        for j in range(1, TAPS):
            pre = pre + pack_ref[0, j : j + 1] * ext[HALO + r - j : HALO + r - j + rows]
        pre_ref[r : r + rows] = pre.astype(BF16)
        conv = pre * sigmoid(pre)
        conv_b = conv.astype(BF16)
        conv_rest = (conv - conv_b.astype(F32)).astype(BF16)
        branch_rest = (branch - branch_b.astype(F32)).astype(BF16)
        for b in range(dh // 128):
            cols = slice(128 * b, 128 * b + 128)
            parts = [conv_b[:, cols], conv_rest[:, cols], conv_b[:, cols]]
            qk = nn(jnp.concatenate(parts, axis=1), wqk[b]).astype(BF16)
            q_ref[r : r + rows, cols] = qk[:, 0:128]
            k_ref[r : r + rows, cols] = qk[:, 128:256]
            parts = [branch_b[:, cols], branch_rest[:, cols], branch_b[:, cols]]
            va_ref[0, r : r + rows, cols] = nn(jnp.concatenate(parts, axis=1), wv[b]).astype(BF16)
        va_ref[0, r : r + rows, dh : dh + 128] = jnp.where(
            iota((rows, 128), 1) == 0, 1.0, 0.0
        ).astype(BF16)
        gates_ref[r : r + rows] += (
            nt(q_ref[r : r + rows], gw[0])
            + nt(k_ref[r : r + rows], gw[1])
            + nt(va_ref[0, r : r + rows, 0:dh], gw[2])
            + bias
        )


def states(h, n_heads, gates_ref, k_ref, va_ref, gcol_ref, grow_ref, sloc, leaving, retain, st, ns):
    n, dh = k_ref.shape

    @pl.when(h == 0)
    def _():
        lower = jnp.where(iota((CH, CH), 0) >= iota((CH, CH), 1), 1.0, 0.0)
        for r, rows in row_chunks(n, CH):
            pre = gates_ref[r : r + rows]
            cum = nn(lower, log_sigmoid(pre), precision=HIGHEST)
            cum = pltpu.roll(cum, 128 - n_heads, 1)
            after = pltpu.roll(pre - cum, n_heads, 1)
            lane = iota((rows, 128), 1)
            both = jnp.where(lane < n_heads, cum, jnp.where(lane < 2 * n_heads, after, 0.0))
            gcol_ref[r : r + rows] = both
            grow_ref[:, r : r + rows] = both.T[0 : grow_ref.shape[0]]

    st[...] = jnp.zeros_like(st)
    ns[...] = jnp.zeros_like(ns)
    chunks = row_chunks(n, CH)
    whole_total = jnp.zeros((1, 1), F32)
    for c, (r, rows) in enumerate(chunks):
        block = gcol_ref[r : r + rows]
        total = pick(block[rows - 8 : rows], h)[7:8]
        whole_total = whole_total + total
        ending = jnp.exp(total + pick(block, n_heads + h))
        weighted = k_ref[r : r + rows].astype(F32) * ending
        st[...] = jnp.exp(total) * st[...] + tn(va_ref[0, r : r + rows, 0:dh], weighted.astype(BF16))
        ns[...] = jnp.exp(total) * ns[...] + jnp.sum(weighted, axis=0, keepdims=True)
        last = c == len(chunks) - 1
        to = leaving.at[h] if last else sloc.at[h, c]
        to[0:dh] = st[...].astype(BF16)
        to[dh : dh + 16] = jnp.where(iota((16, dh), 0) == 0, ns[0:1], 0.0).astype(BF16)
    retain[h] = jnp.broadcast_to(jnp.exp(whole_total), retain.shape[1:])


def decay_of(block, grow_ref, h, n_heads, r, rows, log_scale):
    cum = pick(block, h)
    after = grow_ref[pl.ds(n_heads + h, 1), r : r + rows]
    exponent = jnp.where(
        iota((rows, rows), 0) >= iota((rows, rows), 1), (cum + log_scale) + after, NEG
    )
    return jnp.exp(exponent), cum


def forward_kernel(n_heads, log_scale,
                   x_ref, og_all_ref, gates_ref, flags_ref, q_ref, k_ref, va_ref, gate_ref, pre_ref, pack_ref, w_ref,
                   out_ref, gcol_ref, grow_ref, retain_ref, dng_ref, sttot_ref, gloc_ref, gend_ref, gaug_ref, ogg_ref,
                   dskip_ref, sums_ref,
                   acc, ogt, numer, mixed_s, stb, gt, gn, sloc, leaving, landed, retain, ss, rs):
    step = pl.program_id(0)
    chain = Chain(1, retain, flags_ref[0:1, 0:1], leaving, landed, (ss, rs))
    place = chain.place

    @pl.when(step == 0)
    def _():
        chain.greet()

    @pl.when(step < n_heads)
    def _():
        states(step, n_heads, gates_ref, k_ref, va_ref, gcol_ref, grow_ref, sloc, leaving, retain, gt, gn)

        @pl.when(place == 0)
        def _():
            chain.pump(step)

        @pl.when((place == 1) & (step > 0))
        def _():
            chain.pump(step - 1)

    @pl.when(step >= n_heads)
    def _():
        h = step - n_heads

        @pl.when((place == 1) & (h == 0))
        def _():
            chain.pump(n_heads - 1)

        @pl.when((place > 1) & (h > 0) & (2 * h - 1 < n_heads))
        def _():
            chain.pump(2 * h - 1)

        for c, (r, rows) in enumerate(row_chunks(q_ref.shape[0], CH)):
            span = slice(r, r + rows)
            decay, _ = decay_of(gcol_ref[span], grow_ref, h, n_heads, r, rows, log_scale)
            weights = (nt(q_ref[span], k_ref[span]) * decay).astype(BF16)
            numer[span] = nn(weights, va_ref[0, span])

        @pl.when((place > 1) & (2 * h < n_heads))
        def _():
            chain.pump(2 * h)

        mix(h, n_heads, log_scale, x_ref, og_all_ref, gcol_ref, q_ref, sloc, landed, gate_ref, pre_ref, pack_ref, w_ref,
            out_ref, dng_ref, sttot_ref, gloc_ref, gend_ref, gaug_ref, ogg_ref, dskip_ref, sums_ref,
            acc, ogt, numer, mixed_s, stb, gt, gn)

    @pl.when(step == 2 * n_heads - 1)
    def _():
        retain_ref[...] = retain[...]
        chain.finish()


def mix(h, n_heads, log_scale,
        x_ref, og_all_ref, gcol_ref, q_ref, sloc, landed, gate_ref, pre_ref, pack_ref, w_ref,
        out_ref, dng_ref, sttot_ref, gloc_ref, gend_ref, gaug_ref, ogg_ref, dskip_ref, sums_ref,
        acc, ogt, numer, mixed_s, stb, gt, gn):
    n, dh = q_ref.shape
    gain = pack_ref[0, TAPS + 1 : TAPS + 2]
    skip = pack_ref[0, TAPS + 2 : TAPS + 3]
    down_t = w_ref.at[0]

    @pl.when(h == 0)
    def _():
        acc[...] = jnp.zeros_like(acc)
        for r, rows in row_chunks(n, CH):
            ogt[:, r : r + rows] = og_all_ref[r : r + rows].astype(F32).T.astype(BF16)
        stb[dh + 16 :] = jnp.zeros((stb.shape[0] - dh - 16, dh), BF16)

    prefix = jnp.zeros((1, 1), F32)
    gain_sum = jnp.zeros((1, dh), F32)
    skip_sum = jnp.zeros((1, dh), F32)
    pair_sum = jnp.zeros((1, 1), F32)
    for c, (r, rows) in enumerate(row_chunks(n, CH)):
        span = slice(r, r + rows)
        block = gcol_ref[span]
        total = pick(block[rows - 8 : rows], h)[7:8]
        state = landed[h].astype(F32) * jnp.exp(prefix)
        if c > 0:
            state = state + sloc[h, c - 1].astype(F32)
        prefix = prefix + total
        state_b = state.astype(BF16)
        sttot_ref[0, c] = state_b
        stb[0 : dh + 16] = state_b
        factor = jnp.exp(pick(block, h) + log_scale)
        both = numer[span] + factor * nt(q_ref[span], stb[...])
        denom = both[:, dh : dh + 1]
        r_inv = lax.rsqrt(denom * denom + 1.0)
        unit, inv_std = normalised(both[:, 0:dh] * r_inv)
        gate = gate_ref[span].astype(F32)
        sg = sigmoid(gate)
        silu_gate = gate * sg
        pre = pre_ref[span].astype(F32)
        conv = pre * sigmoid(pre)
        inner = unit * gain + skip * conv
        mixed = (inner * silu_gate).astype(BF16)
        mixed_s[span] = mixed
        acc[span] += nt(mixed, down_t[...])
        mixed_grad = nn(og_all_ref[span], down_t[...])
        hskip = mixed_grad * silu_gate
        ogg_ref[span] = (mixed_grad * inner * (sg * (1.0 + gate * (1.0 - sg)))).astype(BF16)
        dskip_ref[span] = (hskip * skip).astype(BF16)
        skip_sum = skip_sum + jnp.sum(hskip * conv, axis=0, keepdims=True)
        gain_sum = gain_sum + jnp.sum(hskip * unit, axis=0, keepdims=True)
        dhh = hskip * gain
        along = jnp.mean(dhh * unit, axis=1, keepdims=True)
        grad = (inv_std * r_inv) * (dhh - jnp.mean(dhh, axis=1, keepdims=True) - unit * along)
        radial = dh * EPS * along * inv_std * inv_std
        gaug_ref[0, span, 0:dh] = grad.astype(BF16)
        gaug_ref[0, span, dh : dh + 128] = jnp.where(
            iota((rows, 128), 1) == 0, -radial * denom * r_inv * r_inv, 0.0
        ).astype(BF16)
        pair_sum = pair_sum + jnp.sum(radial * r_inv * r_inv, axis=0, keepdims=True)
    sums_ref[0, 0:1] = gain_sum
    sums_ref[0, 1:2] = skip_sum
    sums_ref[0, 2:3] = jnp.broadcast_to(pair_sum, (1, dh))
    sums_ref[0, 3:8] = jnp.zeros((5, dh), F32)

    @pl.when(h == n_heads - 1)
    def _():
        for r, rows in row_chunks(n, CH):
            out_ref[r : r + rows] = (x_ref[r : r + rows].astype(F32) + acc[r : r + rows]).astype(BF16)

    dng_ref[0] = nn(ogt[...], mixed_s[...]).astype(BF16)

    gt[...] = jnp.zeros_like(gt)
    gn[...] = jnp.zeros_like(gn)
    for c, (r, rows) in reversed(list(enumerate(row_chunks(n, CH)))):
        span = slice(r, r + rows)
        block = gcol_ref[span]
        cum = pick(block, h)
        keep = jnp.exp(pick(block[rows - 8 : rows], h)[7:8])
        weighted = q_ref[span].astype(F32) * jnp.exp(cum + log_scale)
        side = gaug_ref[0, span, dh : dh + 128].astype(F32)[:, 0:1]
        gt[...] = keep * gt[...] + tn(gaug_ref[0, span, 0:dh], weighted.astype(BF16))
        gn[...] = keep * gn[...] + jnp.sum(weighted * side, axis=0, keepdims=True)
        to = gloc_ref.at[0, c - 1] if c else gend_ref.at[0]
        to[0:dh] = gt[...].astype(BF16)
        to[dh : dh + 16] = jnp.where(iota((16, dh), 0) == 0, gn[0:1], 0.0).astype(BF16)


def memory_back(h, n_heads, log_scale, chain,
                gates_ref, gcol_ref, grow_ref, q_ref, k_ref, va_ref, gaug_ref, sttot_ref, gloc_ref,
                dq_s, dk_s, dv_s, pg_s, bsum, dk_near, dv_near, stb, gtb, cols, rowsb, across):
    n, dh = q_ref.shape
    chunks = row_chunks(n, CH)

    @pl.when(h == 0)
    def _():
        stb[dh + 16 :] = jnp.zeros((stb.shape[0] - dh - 16, dh), BF16)
        gtb[dh + 16 :] = jnp.zeros((gtb.shape[0] - dh - 16, dh), BF16)
        cols[...] = jnp.zeros_like(cols)
        rowsb[...] = jnp.zeros_like(rowsb)
        across[...] = jnp.zeros_like(across)

    for c, (r, rows) in enumerate(chunks):
        span = slice(r, r + rows)
        stb[0 : dh + 16] = sttot_ref[0, c]
        q, k, va, gaug = q_ref[span], k_ref[span], va_ref[0, span], gaug_ref[0, span]
        decay, cum = decay_of(gcol_ref[span], grow_ref, h, n_heads, r, rows, log_scale)
        weights = nt(q, k) * decay
        wg = nt(gaug, va)
        d_scores = (wg * decay).astype(BF16)
        pair = wg * weights
        dq_far = jnp.exp(cum + log_scale) * nn(gaug, stb[...])
        dq_s[h, span] = (nn(d_scores, k) + dq_far).astype(BF16)
        dk_near[span] = tn(d_scores, q)
        dv_near[span] = tn(weights.astype(BF16), gaug[:, 0:dh])
        row_sum = jnp.sum(pair, axis=1, keepdims=True) + jnp.sum(dq_far * q.astype(F32), axis=1, keepdims=True)
        cols[span] = jnp.where(iota((rows, 128), 1) == h, row_sum, cols[span])
        rowsb[pl.ds(h, 1), span] = jnp.sum(pair, axis=0, keepdims=True)

    @pl.when((chain.place == 1) & (h == 0))
    def _():
        for i in range(1, n_heads):
            chain.pump(i)

    @pl.when(chain.place > 1)
    def _():
        chain.pump(h)

    suffix = jnp.zeros((1, 1), F32)
    for c, (r, rows) in reversed(list(enumerate(chunks))):
        span = slice(r, r + rows)
        block = gcol_ref[span]
        total = pick(block[rows - 8 : rows], h)[7:8]
        after_col = pick(block, n_heads + h)
        grad_state = chain.landed[h].astype(F32) * jnp.exp(suffix)
        if c < len(chunks) - 1:
            grad_state = grad_state + gloc_ref[0, c].astype(F32)
        suffix = suffix + total
        gtb[0 : dh + 16] = grad_state.astype(BF16)
        through = jnp.exp(total) * jnp.sum(
            jnp.sum(sttot_ref[0, c].astype(F32) * grad_state, axis=1, keepdims=True), axis=0, keepdims=True
        )
        k = k_ref[span]
        ending = jnp.exp(total + after_col)
        dk_far = ending * nn(va_ref[0, span], gtb[...])
        dk_s[h, span] = (dk_near[span] + dk_far).astype(BF16)
        dv_s[h, span] = (dv_near[span] + ending * nt(k, gtb[...])[:, 0:dh]).astype(BF16)
        col_far = jnp.sum(dk_far * k.astype(F32), axis=1, keepdims=True)
        cols[span] = jnp.where(iota((rows, 128), 1) == n_heads + h, col_far, cols[span])
        across[c : c + 1] = jnp.where(iota((1, 128), 1) == h, through, across[c : c + 1])

    @pl.when(h == n_heads - 1)
    def _():
        upper = jnp.where(iota((CH, CH), 0) <= iota((CH, CH), 1), 1.0, 0.0)
        strict = jnp.where(iota((CH, CH), 0) > iota((CH, CH), 1), 1.0, 0.0)
        lane = iota((CH, 128), 1)
        bias_sum = jnp.zeros((1, 128), F32)
        for c, (r, rows) in enumerate(chunks):
            span = slice(r, r + rows)
            near_col = rowsb[:, span].T
            far = pltpu.roll(cols[span], 128 - n_heads, 1)
            forget = (
                nn(upper, cols[span] - near_col, precision=HIGHEST)
                + nn(strict, far, precision=HIGHEST)
                + across[c : c + 1]
            )
            pre = gates_ref[span]
            forget = pltpu.roll(forget, n_heads, 1) * sigmoid(-pre)
            grads = jnp.where(
                lane < n_heads, near_col + far, jnp.where(lane < 2 * n_heads, forget, 0.0)
            )
            bias_sum = bias_sum + jnp.sum(grads, axis=0, keepdims=True)
            pg_s[span] = grads.astype(BF16)
        bsum[...] = jnp.where(iota((8, 128), 0) == 0, bias_sum, 0.0)


def lower(h, n_heads,
          x_ref, halo_ref, gain_ref, flags_ref, og_all_ref, normt_ref, pg_ref, bsum_ref, q_ref, k_ref, va_ref,
          dq_s, dk_s, dv_s, pre_ref, br_ref, ogg_ref, dskip_ref,
          pack_ref, w_ref, dng_ref, sums_ref,
          upg_ref, ing_ref, corr_ref, minor_ref,
          nacc, pext, brx, lifted, conv_s, wqk, wv, gw):
    n, dh = q_ref.shape
    link = flags_ref[0:1, 0:1]
    w = w_ref.at[0]

    minor_out = minor_ref
    minor_ref = minor_out.at[pl.ds(h, 1)]
    minor_ref[0, 64:] = jnp.zeros((minor_ref.shape[1] - 64, dh), F32)

    @pl.when(h == 0)
    def _():
        nacc[...] = jnp.zeros_like(nacc)
        ing_ref[...] = jnp.zeros_like(ing_ref)
        pext[0:HALO] = jnp.zeros((HALO, dh), F32)
        pext[HALO + n :] = jnp.zeros((HALO, dh), F32)
        gw[...] = jnp.zeros_like(gw)

    gate_maps(pack_ref, gw)
    for b in range(dh // 128):
        [(q_high, k_high, v_high)] = maps_of(pack_ref, slice(128 * b, 128 * b + 128), False)
        wqk[b, :, 0:128] = q_high
        wqk[b, :, 128:256] = k_high
        wv[b] = v_high

    for r, rows in row_chunks(n + HALO, 208):
        brx[r : r + rows] = br_ref[r : r + rows].astype(F32)

    taps = [jnp.zeros((1, dh), F32) for _ in range(TAPS)]
    bias_sum = jnp.zeros((1, dh), F32)
    for r, rows in row_chunks(n, CH):
        span = slice(r, r + rows)
        pg = pg_ref[span]
        dqt = (dq_s[h, span].astype(F32) + nn(pg, gw[0])).astype(BF16)
        dkt = (dk_s[h, span].astype(F32) + nn(pg, gw[1])).astype(BF16)
        dvt = (dv_s[h, span].astype(F32) + nn(pg, gw[2])).astype(BF16)
        pre = pre_ref[span].astype(F32)
        sg = sigmoid(pre)
        conv_s[span] = (pre * sg).astype(BF16)
        slope = sg * (1.0 + pre * (1.0 - sg))
        dq_s[h, span] = dqt
        dk_s[h, span] = dkt
        dv_s[h, span] = dvt
        for b in range(dh // 128):
            at = slice(128 * b, 128 * b + 128)
            both = jnp.concatenate([dqt[:, at], dkt[:, at]], axis=1)
            conv_grad = nt(both, wqk[b]) + dskip_ref[span, at].astype(F32)
            pext[HALO + r : HALO + r + rows, at] = conv_grad * slope[:, at]
        pre_grad = pext[HALO + r : HALO + r + rows]
        bias_sum = bias_sum + jnp.sum(pre_grad, axis=0, keepdims=True)
        for j in range(TAPS):
            taps[j] = taps[j] + jnp.sum(
                pre_grad * brx[HALO + r - j : HALO + r - j + rows], axis=0, keepdims=True
            )
    for j in range(TAPS):
        minor_ref[0, j : j + 1] = taps[j]
    minor_ref[0, TAPS : TAPS + 1] = bias_sum
    minor_ref[0, TAPS + 1 : 8] = jnp.zeros((8 - TAPS - 1, dh), F32)
    minor_ref[0, 8:16] = sums_ref[0]
    upg_ref[0, :, 2 * dh : 3 * dh] = dng_ref[0]

    halo_grad = jnp.zeros((HALO, dh), F32)
    for j in range(1, TAPS):
        halo_grad = halo_grad + pack_ref[0, j : j + 1] * pext[j : HALO + j]
    halo_b = (halo_grad * link).astype(BF16)
    nacc[0:HALO] += nt(halo_b, w[:, 0:dh])
    for r, rows in row_chunks(n, CH):
        span = slice(r, r + rows)
        grad = jnp.zeros((rows, dh), F32)
        for j in range(TAPS):
            grad = grad + pack_ref[0, j : j + 1] * pext[HALO + r + j : HALO + r + j + rows]
        for b in range(dh // 128):
            at = slice(128 * b, 128 * b + 128)
            lifted[span, at] = (grad[:, at] + nt(dv_s[h, span, at], wv[b])).astype(BF16)
        lifted[span, dh : 2 * dh] = ogg_ref[span]
        ing_ref[span] += nt(lifted[span], w[...])

    unit_halo, std_halo = normalised(halo_ref[...].astype(F32))
    gain = jnp.concatenate([gain_ref[j : j + 1] for j in range(gain_ref.shape[0])], axis=1)
    upg = nn(normt_ref[...], lifted[...])
    upg_ref[0, :, dh : 2 * dh] = upg[:, dh:].astype(BF16)
    upg_ref[0, :, 0:dh] = (upg[:, 0:dh] + tn((unit_halo * gain).astype(BF16), halo_b)).astype(BF16)

    fold = jnp.where(iota((8, 128), 1) % 4 == iota((8, 128), 0), 1.0, 0.0)
    diagonal = iota((128, 128), 0) // 4 == iota((128, 128), 1) // 4
    for b in range(dh // 128):
        at = slice(128 * b, 128 * b + 128)
        qk_grad = tn(conv_s[:, at], jnp.concatenate([dq_s[h, :, at], dk_s[h, :, at]], axis=1))
        v_grad = tn(brx[HALO:, at].astype(BF16), dv_s[h, :, at])
        for m, full in enumerate((qk_grad[:, 0:128], qk_grad[:, 128:256], v_grad)):
            minor_ref[0, 16 + 8 * m : 24 + 8 * m, at] = nt(fold, jnp.where(diagonal, full, 0.0), precision=HIGHEST)
    minor_ref[0, 40:48] = tn(pg_ref[...], q_ref[...])[0:8]
    minor_ref[0, 48:56] = tn(pg_ref[...], k_ref[...])[0:8]
    minor_ref[0, 56:64] = tn(pg_ref[...], va_ref[0, :, 0:dh])[0:8]

    @pl.when(h == n_heads - 1)
    def _():
        def back(normed_grad, unit, inv_std):
            scaled = normed_grad * gain
            return inv_std * (
                scaled
                - jnp.mean(scaled, axis=1, keepdims=True)
                - unit * jnp.mean(scaled * unit, axis=1, keepdims=True)
            )

        corr_ref[...] = back(nacc[0:HALO], unit_halo, std_halo)
        total = jnp.sum(nacc[0:HALO] * unit_halo, axis=0, keepdims=True)
        for r, rows in row_chunks(n, CH):
            unit, inv_std = normalised(x_ref[r : r + rows].astype(F32))
            grads = ing_ref[r : r + rows]
            total = total + jnp.sum(grads * unit, axis=0, keepdims=True)
            ing_ref[r : r + rows] = og_all_ref[r : r + rows].astype(F32) + back(grads, unit, inv_std)
        for i in range(n_heads):
            minor_out[i, 66:67] = jnp.broadcast_to(bsum_ref[0:1, n_heads + i : n_heads + i + 1], (1, dh))
            for j in range(total.shape[1] // dh):
                minor_out[i, 64 + j : 65 + j] = total[:, dh * j : dh * j + dh]


def backward_kernel(n_heads, log_scale,
                    x_ref, halo_ref, gain_ref, flags_ref, og_all_ref, normt_ref, gates_ref, gcol_ref, grow_ref, retain_ref,
                    gend_ref, q_ref, k_ref, va_ref, gaug_ref, sttot_ref, gloc_ref, pre_ref, br_ref, ogg_ref, dskip_ref,
                    pack_ref, w_ref, dng_ref, sums_ref,
                    upg_ref, ing_ref, corr_ref, minor_ref,
                    dq_s, dk_s, dv_s, pg_s, bsum, stb, gtb, cols, rowsb, across,
                    nacc, pext, brx, lifted, conv_s, wqk, wv, gw, leaving, landed, ss, rs):
    step = pl.program_id(0)
    chain = Chain(-1, retain_ref, flags_ref[8:9, 0:1], leaving, landed, (ss, rs))

    @pl.when(step == 0)
    def _():
        chain.greet()
        leaving[...] = gend_ref[...]

        @pl.when(chain.place == 0)
        def _():
            for i in range(n_heads):
                chain.pump(i)

        @pl.when(chain.place == 1)
        def _():
            chain.pump(0)

    dh = q_ref.shape[1]
    near_k, near_v = ing_ref.at[:, 0:dh], ing_ref.at[:, dh : 2 * dh]

    @pl.when(step < n_heads)
    def _():
        memory_back(step, n_heads, log_scale, chain, gates_ref, gcol_ref, grow_ref, q_ref, k_ref, va_ref, gaug_ref,
                    sttot_ref, gloc_ref, dq_s, dk_s, dv_s, pg_s, bsum, near_k, near_v, stb, gtb, cols, rowsb, across)

    @pl.when(step >= n_heads)
    def _():
        lower(step - n_heads, n_heads, x_ref, halo_ref, gain_ref, flags_ref, og_all_ref, normt_ref, pg_s, bsum, q_ref,
              k_ref, va_ref, dq_s, dk_s, dv_s, pre_ref, br_ref, ogg_ref, dskip_ref, pack_ref, w_ref, dng_ref, sums_ref,
              upg_ref, ing_ref, corr_ref, minor_ref, nacc, pext, brx, lifted, conv_s, wqk, wv, gw)

    @pl.when(step == 2 * n_heads - 1)
    def _():
        chain.finish()


class Specs:
    def __init__(self, heads, rounds=2):
        self.heads, self.steps = heads, heads * rounds
        self.index = dict(
            both=lambda s: lax.rem(s, heads),
            first=lambda s: jnp.minimum(s, heads - 1),
            second=lambda s: jnp.maximum(s - heads, 0),
        )

    def whole(self, *shape):
        return pl.BlockSpec(shape, lambda s: (0,) * len(shape), pipeline_mode=pl.Buffered(1))

    def cols(self, when, rows, cols):
        index = self.index[when]
        return pl.BlockSpec((None, rows, cols), lambda s: (index(s), 0, 0))

    def lead(self, when, *shape, last=0):
        index = self.index[when]
        return pl.BlockSpec((1, *shape), lambda s: (index(s),) + (0,) * (len(shape) - 1) + (last,))


def params(**kw):
    return pltpu.CompilerParams(dimension_semantics=("arbitrary",), vmem_limit_bytes=62 << 20, **kw)


def sds(shape, dtype):
    return jax.ShapeDtypeStruct(shape, dtype)


def shifted(x, by):
    heads = lax.axis_size("head")
    pairs = [(i, i + by) for i in range(heads) if 0 <= i + by < heads]
    return lax.ppermute(x, "head", pairs)


MESH = pl.DeviceIdType.MESH


class Place:
    def __init__(self):
        dp, head = lax.axis_index("dp"), lax.axis_index("head")
        self.z, self.y = lax.div(dp, 2), lax.rem(dp, 2)
        self.x, self.c = lax.div(head, 2), lax.rem(head, 2)

    def along_z(self, k):
        z = self.z
        return (z, z + 1 - 2 * lax.rem(z, 2), lax.rem(z + 2, 4), 3 - z)[k]

    def device(self, k=0, fy=0, fx=0, fc=0):
        y, x, c = (1 - v if f else v for v, f in ((self.y, fy), (self.x, fx), (self.c, fc)))
        return (self.along_z(k) * 2 + y, x * 2 + c)

    def head(self, fx=0, fc=0):
        return (1 - self.x if fx else self.x) * 2 + (1 - self.c if fc else self.c)

    def rows(self, k, fy, size):
        y = 1 - self.y if fy else self.y
        return pl.multiple_of((self.along_z(k) * 2 + y) * size, 16)


NEIGHBOURS = (dict(fc=1), dict(fx=1), dict(fx=1, fc=1), dict(fy=1), dict(k=1), dict(k=2), dict(k=3))


def greet(devices):
    barrier = pltpu.get_barrier_semaphore()
    for device in devices:
        pl.semaphore_signal(barrier, inc=1, device_id=device, device_id_type=MESH)
    pl.semaphore_wait(barrier, len(devices))


def remote(src, dst, sems, at, device):
    send, recv = sems
    return pltpu.make_async_remote_copy(
        src_ref=src, dst_ref=dst, send_sem=send.at[at], recv_sem=recv.at[at], device_id=device, device_id_type=MESH
    )


class Gather:
    SEMAPHORES = ((2, 3), (2, 3), (2, 4), (2, 4), (2, 4, 2), (2, 4, 2), (2, 4, 4), (2, 4, 4))
    FLIPS = ((dict(fx=1), dict(fy=1)), (dict(fy=1), dict(fx=1)))

    def __init__(self, here, shard, w, sems):
        self.here, self.shard, self.w = here, shard, w
        self.z, self.f, self.s, self.d = (tuple(sems[i : i + 2]) for i in (0, 2, 4, 6))
        self.rows = shard.shape[0]
        self.started = []

    def block(self, p, k=0, fy=0, fx=0, fc=0):
        half = self.rows // 2
        return self.w.at[self.here.head(fx, fc), pl.ds(self.here.rows(k, fy, self.rows) + half * p, half)]

    def send(self, src, dst, sems, at, to):
        copy = remote(src, dst, sems, at, self.here.device(**to))
        copy.start()
        self.started.append(copy)

    def arrived(self, dst, sems, at):
        remote(dst, dst, sems, at, self.here.device(fc=1)).wait_recv()

    def begin(self):
        half = self.rows // 2
        for p in (0, 1):
            mine = self.shard.at[pl.ds(half * p, half)]
            first, second = self.FLIPS[p]
            self.send(mine, self.block(p), self.z, (p, 0), dict(k=1))
            self.send(mine, self.block(p), self.f, (p, 0), first)
        for p in (0, 1):
            mine = self.shard.at[pl.ds(half * p, half)]
            first, second = self.FLIPS[p]
            for k in (2, 3):
                self.send(mine, self.block(p), self.z, (p, k - 1), dict(k=k))
            self.send(mine, self.block(p), self.s, (p, 0, 0), second)
            self.send(mine, self.block(p), self.d, (p, 0, 0), dict(fc=1))

    def from_z(self, k):
        for p in (0, 1):
            first, second = self.FLIPS[p]
            block = self.block(p, k)
            self.arrived(block, self.z, (p, k - 1))
            self.send(block, block, self.f, (p, k), first)
            self.send(block, block, self.s, (p, k, 0), second)
            self.send(block, block, self.d, (p, k, 0), dict(fc=1))

    def from_first(self, k):
        for p in (0, 1):
            first, second = self.FLIPS[p]
            block = self.block(p, k, **first)
            self.arrived(block, self.f, (p, k))
            self.send(block, block, self.s, (p, k, 1), second)
            self.send(block, block, self.d, (p, k, 1), dict(fc=1))

    def from_second(self, k):
        for i in (0, 1):
            for p in (0, 1):
                first, second = self.FLIPS[p]
                block = self.block(p, k, **(dict(**first, **second) if i else second))
                self.arrived(block, self.s, (p, k, i))
                self.send(block, block, self.d, (p, k, 2 + i), dict(fc=1))

    def from_core(self, k):
        for p in (0, 1):
            first, second = self.FLIPS[p]
            for i, over in enumerate((dict(), first, second, dict(**first, **second))):
                self.arrived(self.block(p, k, fc=1, **over), self.d, (p, k, i))

    def run(self):
        self.begin()
        self.from_first(0)
        for k in (1, 2, 3):
            self.from_z(k)
            self.from_second(k - 1)
            self.from_first(k)
        self.from_second(3)
        for k in range(4):
            self.from_core(k)
        for copy in self.started:
            copy.wait_send()


def gather_kernel(up_raw, down, taps, conv_bias, group, skip, gate_bias, maps, gates, x, w, pack_all, halo,
                  shard, pack, rows_s, local_sem, ms, mr, *sems):
    here = Place()
    n = x.shape[0]
    dh = pack.shape[1]
    rows = shard.shape[0]
    shard[:, 0:dh] = up_raw[:, 0]
    shard[:, dh : 2 * dh] = up_raw[:, 1]
    shard[:, 2 * dh :] = down[...]
    fill_pack(taps, conv_bias, group, skip, gate_bias, maps, gates, pack, rows_s)
    copies = [pltpu.make_async_copy(pack, pack_all.at[here.head()], local_sem.at[0]),
              pltpu.make_async_copy(shard, w.at[here.head(), pl.ds(here.rows(0, 0, rows), rows)], local_sem.at[1])]
    for copy in copies:
        copy.start()
    greet([here.device(**to) for to in NEIGHBOURS])
    small = []
    for i, to in enumerate(NEIGHBOURS[:3]):
        small.append(remote(pack, pack_all.at[here.head()], (ms, mr), i, here.device(**to)))
    after = (here.z * 2 + here.y, lax.rem(here.head() + 1, 4))
    small.append(remote(x.at[pl.ds(n - HALO, HALO)], halo, (ms, mr), 3, after))
    for copy in small:
        copy.start()
    Gather(here, shard, w, sems).run()
    for i, to in enumerate(NEIGHBOURS[:3]):
        from_them = pack_all.at[here.head(to.get("fx", 0), to.get("fc", 0))]
        remote(from_them, from_them, (ms, mr), i, here.device(fc=1)).wait_recv()
    remote(halo, halo, (ms, mr), 3, here.device(fc=1)).wait_recv()
    for copy in small:
        copy.wait_send()
    for copy in copies:
        copy.wait()


def fill_pack(taps, conv_bias, group, skip, gate_bias, maps, gates, pack, rows_s):
    dh = pack.shape[1]
    pack[0:TAPS] = taps[...]
    for i, ref in enumerate((conv_bias, group, skip)):
        for j in range(dh // 128):
            pack[TAPS + i : TAPS + i + 1, 128 * j : 128 * j + 128] = ref[j : j + 1]
    lane = iota((1, dh), 1)
    pack[7:8] = jnp.where(lane == 0, gate_bias[0:1, 0:1], jnp.where(lane == 1, gate_bias[0:1, 1:2], 0.0))
    rows_s[...] = jnp.zeros_like(rows_s)
    for m in range(3):
        for i in range(4):
            rows_s[16 * m + 4 * i : 16 * m + 4 * i + 4, 0 : dh // 4] = maps[m, i]
        pack[24 + 8 * m : 32 + 8 * m] = gates[m].astype(F32)
    wide = nn(rows_s[...], jnp.where(iota((128, dh), 1) // 4 == iota((128, dh), 0), 1.0, 0.0), precision=HIGHEST)
    for m in range(3):
        rows = jnp.zeros((4, dh), F32)
        for i in range(4):
            rows = jnp.where(iota((4, dh), 1) % 4 == i, wide[16 * m + 4 * i : 16 * m + 4 * i + 4], rows)
        pack[8 + 4 * m : 12 + 4 * m] = rows
    pack[20:24] = jnp.zeros((4, dh), F32)


def gathered(up_weight, down, small, x, heads):
    dp = lax.axis_size("dp")
    n, d = x.shape
    vmem = pl.BlockSpec(memory_space=pltpu.VMEM)
    rows, _, dh = up_weight.shape
    if not by_hand(rows):
        up = up_weight.reshape(rows, 2 * dh)
        pack = pl.pallas_call(
            fill_pack, out_shape=sds((48, dh), F32), in_specs=[vmem] * 7, out_specs=vmem,
            scratch_shapes=[pltpu.VMEM((48, 128), F32)], name="pack",
        )(*small)

        def all_of(shard):
            w = lax.all_gather(shard, ("dp", "head"), axis=0)
            w = w.reshape(dp, heads, *shard.shape).transpose(1, 0, 2, 3)
            return w.reshape(heads, dp * shard.shape[0], shard.shape[1])

        w = all_of(jnp.concatenate([up, down], axis=1))
        return w, lax.all_gather(pack, "head", axis=0), shifted(x[n - HALO :], 1)
    sem = pltpu.SemaphoreType.DMA
    anywhere = pl.BlockSpec(memory_space=pl.ANY)
    return pl.pallas_call(
        gather_kernel,
        out_shape=[sds((heads, dp * rows, 3 * dh), BF16), sds((heads, 48, dh), F32), sds((HALO, d), BF16)],
        in_specs=[vmem, vmem, *[vmem] * 7, anywhere],
        out_specs=[anywhere] * 3,
        scratch_shapes=[pltpu.VMEM((rows, 3 * dh), BF16), pltpu.VMEM((48, dh), F32), pltpu.VMEM((48, 128), F32),
                        sem((2,)), sem((4,)), sem((4,)), *(sem(shape) for shape in Gather.SEMAPHORES)],
        compiler_params=pltpu.CompilerParams(collective_id=0, has_side_effects=True),
        name="gather",
    )(up_weight, down, *small, x)


def by_hand(rows):
    return lax.axis_size("dp") == 8 and lax.axis_size("head") == 4 and rows % 32 == 0


def scatter_kernel(part, minor, corr, total, minor_total, corr_in,
                   own, r0, r1a, r1b, r2, r3, m0, m1, n0, n1,
                   load, s0, t0, s1, t1, s2, t2, s3, t3, ms, mr):
    here = Place()
    rows = total.shape[0]
    half = rows // 2
    spans = (pl.ds(0, half), pl.ds(half, half))
    order = (1, 2, 3, 0)
    corners = ((1, 1), (1, 0), (0, 1), (0, 0))

    def block(k, fx, fy, fc):
        return part.at[here.head(fx, fc), pl.ds(here.rows(k, fy, rows), rows)]

    loads = {}
    for k in order:
        for fx, fy in corners:
            loads[k, fx, fy] = pltpu.make_async_copy(block(k, fx, fy, 0), own.at[fx, k, fy], load.at[fx, k, fy])
            loads[k, fx, fy].start()
    small = [pltpu.make_async_copy(minor.at[here.head(fx)], m0.at[fx], load.at[fx, 4, 0]) for fx in (0, 1)]
    for copy in small:
        copy.start()
    greet([here.device(**to) for to in NEIGHBOURS])
    started = []

    def send(src, dst, sems, at, to):
        copy = remote(src, dst, sems, at, to if isinstance(to, tuple) else here.device(**to))
        copy.start()
        started.append(copy)

    def arrived(dst, sems, at):
        remote(dst, dst, sems, at, here.device(fc=1)).wait_recv()

    def add(into, other):
        into[...] = (into[...].astype(F32) + other[...].astype(F32)).astype(into.dtype)

    def first(k):
        for fx, fy in corners:
            loads[k, fx, fy].wait()
            arrived(r0.at[fx, k, fy], (s0, t0), (fx, k, fy))
            add(own.at[fx, k, fy], r0.at[fx, k, fy])
            if fy:
                send(own.at[fx, k, 1, spans[0]], r1a.at[fx, k], (s1, t1), (0, fx, k), dict(fy=1))
            if fx:
                send(own.at[1, k, fy, spans[1]], r1b.at[fy, k], (s1, t1), (1, fy, k), dict(fx=1))

    def second(k):
        for f in (1, 0):
            arrived(r1a.at[f, k], (s1, t1), (0, f, k))
            add(own.at[f, k, 0, spans[0]], r1a.at[f, k])
            if f:
                send(own.at[1, k, 0, spans[0]], r2.at[0, k], (s2, t2), (0, k), dict(fx=1))
            arrived(r1b.at[f, k], (s1, t1), (1, f, k))
            add(own.at[0, k, f, spans[1]], r1b.at[f, k])
            if f:
                send(own.at[0, k, 1, spans[1]], r2.at[1, k], (s2, t2), (1, k), dict(fy=1))

    def third(k):
        for p in (0, 1):
            arrived(r2.at[p, k], (s2, t2), (p, k))
            add(own.at[0, k, 0, spans[p]], r2.at[p, k])
            if k:
                send(own.at[0, k, 0, spans[p]], r3.at[p, k - 1], (s3, t3), (p, k - 1), dict(k=k))

    send(corr, corr_in, (ms, mr), 6, (here.z * 2 + here.y, lax.rem(here.head() + 3, 4)))
    for fx in (0, 1):
        send(minor.at[here.head(fx, 1)], n0.at[fx], (ms, mr), fx, dict(fc=1))
    for k in order:
        for fx, fy in corners:
            send(block(k, fx, fy, 1), r0.at[fx, k, fy], (s0, t0), (fx, k, fy), dict(fc=1))
    for fx in (0, 1):
        small[fx].wait()
        arrived(n0.at[fx], (ms, mr), fx)
        add(m0.at[fx], n0.at[fx])
    send(m0.at[1], n1.at[0], (ms, mr), 2, dict(fx=1))
    first(1)
    first(2)
    second(1)
    arrived(n1.at[0], (ms, mr), 2)
    m1[0] = m0[0] + n1[0]
    send(m1.at[0], n1.at[1], (ms, mr), 3, dict(fy=1))
    first(3)
    second(2)
    third(1)
    arrived(n1.at[1], (ms, mr), 3)
    m1[1] = m1[0] + n1[1]
    send(m1.at[1], n1.at[2], (ms, mr), 4, dict(k=1))
    first(0)
    second(3)
    third(2)
    arrived(n1.at[2], (ms, mr), 4)
    m1[2] = m1[1] + n1[2]
    send(m1.at[2], n1.at[3], (ms, mr), 5, dict(k=2))
    second(0)
    third(3)
    third(0)
    for p in (0, 1):
        summed = own[0, 0, 0, spans[p]].astype(F32)
        for k in range(3):
            arrived(r3.at[p, k], (s3, t3), (p, k))
            summed = summed + r3[p, k].astype(F32)
        total[spans[p]] = summed
    arrived(n1.at[3], (ms, mr), 5)
    minor_total[...] = m1[2] + n1[3]
    arrived(corr_in, (ms, mr), 6)
    for copy in started:
        copy.wait_send()


def scattered(part, minor, corr):
    dp = lax.axis_size("dp")
    heads, d, cols = part.shape
    rows = d // dp
    if not by_hand(rows):
        part = lax.psum_scatter(part, "head", scatter_dimension=0, tiled=True)
        part = lax.psum_scatter(part, "dp", scatter_dimension=1, tiled=True)[0].astype(F32)
        minor = lax.psum(lax.psum_scatter(minor, "head", scatter_dimension=0, tiled=True), "dp")[0]
        return part, minor, shifted(corr, -1)
    sem = pltpu.SemaphoreType.DMA
    half = rows // 2
    lines = minor.shape[1:]
    vmem = pl.BlockSpec(memory_space=pltpu.VMEM)
    return pl.pallas_call(
        scatter_kernel,
        out_shape=[sds((rows, cols), F32), sds(lines, F32), sds(corr.shape, F32)],
        in_specs=[pl.BlockSpec(memory_space=pl.ANY)] * 3,
        out_specs=[vmem] * 3,
        scratch_shapes=[
            pltpu.VMEM((2, 4, 2, rows, cols), BF16), pltpu.VMEM((2, 4, 2, rows, cols), BF16),
            pltpu.VMEM((2, 4, half, cols), BF16), pltpu.VMEM((2, 4, half, cols), BF16),
            pltpu.VMEM((2, 4, half, cols), BF16), pltpu.VMEM((2, 3, half, cols), BF16),
            pltpu.VMEM((2, *lines), F32), pltpu.VMEM((3, *lines), F32),
            pltpu.VMEM((2, *lines), F32), pltpu.VMEM((4, *lines), F32),
            sem((2, 5, 2)), sem((2, 4, 2)), sem((2, 4, 2)), sem((2, 2, 4)), sem((2, 2, 4)), sem((2, 4)), sem((2, 4)),
            sem((2, 3)), sem((2, 3)), sem((7,)), sem((7,)),
        ],
        compiler_params=pltpu.CompilerParams(collective_id=1, has_side_effects=True, vmem_limit_bytes=60 << 20),
        name="scatter",
    )(part, minor, corr)


def finish_kernel(n_heads, total, minor, corr, ing, output, up, down, conv_w, conv_b, maps, gate_w, gate_b, group, skip, gain, ing_out, out):
    dh = minor.shape[1]
    up[:, 0] = total[:, 0:dh]
    up[:, 1] = total[:, dh : 2 * dh]
    down[...] = total[:, 2 * dh :]
    conv_w[...] = minor[0:TAPS]
    for j in range(dh // 128):
        at = slice(128 * j, 128 * j + 128)
        for ref, row in ((conv_b, TAPS), (group, 8), (skip, 9)):
            ref[j : j + 1] = minor[row : row + 1, at]
        for i in range(gain.shape[0] * 128 // dh):
            gain[dh // 128 * i + j : dh // 128 * i + j + 1] = minor[64 + i : 65 + i, at]
    for m in range(3):
        gate_w[m] = minor[40 + 8 * m : 48 + 8 * m]
    for i in range(4):
        chosen = jnp.where(iota((dh, 128), 0) == 4 * iota((dh, 128), 1) + i, 1.0, 0.0)
        rows = nn(minor[16:40], chosen, precision=HIGHEST)
        for m in range(3):
            maps[m, i] = rows[8 * m : 8 * m + 4, 0 : dh // 4]
    gate_b[0:1, 0:1] = minor[10:11, 0:1]
    gate_b[0:1, 1:2] = minor[66:67, 0:1]
    last = lax.axis_index("head") == n_heads - 1
    ing_out[...] = ing[...] + jnp.where(last, 0.0, corr[...])


class Chain:
    def __init__(self, by, retain, linked, leaving, landed, sems):
        self.dp, head = lax.axis_index("dp"), lax.axis_index("head")
        self.heads = lax.axis_size("head")
        self.ahead, self.behind = lax.rem(head + 1, self.heads), lax.rem(head + self.heads - 1, self.heads)
        self.place = head if by > 0 else self.heads - 1 - head
        self.to = (self.dp, self.ahead if by > 0 else self.behind)
        self.retain, self.linked, self.leaving, self.landed, self.sems = retain, linked, leaving, landed, sems

    def greet(self):
        greet([(self.dp, self.ahead), (self.dp, self.behind)])

    def copy(self, i):
        return remote(self.leaving.at[i], self.landed.at[i], self.sems, i, self.to)

    def pump(self, i):
        @pl.when(self.place != 0)
        def _():
            self.copy(i).wait_recv()
            entering = self.landed[i].astype(F32) * self.linked
            self.landed[i] = entering.astype(BF16)
            self.leaving[i] = (self.leaving[i].astype(F32) + entering * self.retain[i, 0:1, 0:1]).astype(BF16)

        @pl.when(self.place == 0)
        def _():
            self.landed[i] = jnp.zeros(self.landed.shape[1:], BF16)

        @pl.when(self.place != self.heads - 1)
        def _():
            self.copy(i).start()

    def finish(self):
        @pl.when(self.place != self.heads - 1)
        def _():
            for i in range(self.heads):
                self.copy(i).wait_send()


def local(inputs, segment_ids, norm_gain, up_weight, conv_weight, conv_bias, qkv_weight,
          gate_weight, gate_bias, group_gain, skip_gain, down_weight, out_grad):
    H = lax.axis_size("head")
    n, d = inputs.shape
    dh = up_weight.shape[2]
    srows = dh + 16
    nch = n // CH
    log_scale = -0.5 * math.log(dh)

    small = (conv_weight, conv_bias.reshape(-1, 128), group_gain.reshape(-1, 128), skip_gain.reshape(-1, 128), gate_bias.T,
             qkv_weight.transpose(0, 2, 3, 1), gate_weight.transpose(0, 2, 1))
    w_all, pack, halo = gathered(up_weight, down_weight.T, small, inputs, H)
    gain = norm_gain.reshape(-1, 128)
    seg = segment_ids.reshape(-1, 128)

    def call(kernel, name, rounds, ins, outs, scratch, **kw):
        return pl.pallas_call(
            kernel, grid=(H * rounds,), out_shape=[o[0] for o in outs], in_specs=[i[1] for i in ins],
            out_specs=[o[1] for o in outs], scratch_shapes=scratch, compiler_params=params(**kw), name=name,
        )(*[i[0] for i in ins])

    sp = Specs(H, 1)
    per_head = sp.lead("both", *pack.shape[1:])
    cols_b = (sds((H, n, dh), BF16), sp.cols("both", n, dh))
    whole = lambda a: (a, sp.whole(*a.shape))
    q, k, va, pre, br, og, gates, normt, flags = call(
        partial(lift_kernel, H), "lift", 1,
        [whole(inputs), whole(halo), whole(gain), whole(seg), (pack, per_head), (w_all, sp.lead("both", d, 2 * dh))],
        [cols_b, cols_b, (sds((H, n, dh + 128), BF16), sp.lead("both", n, dh + 128)), cols_b,
         (sds((H, n + HALO, dh), BF16), sp.cols("both", n + HALO, dh)), cols_b,
         whole(sds((n, 128), F32)), whole(sds((d, n), BF16)), whole(sds((16, 128), F32))],
        [pltpu.VMEM((n + HALO, d), BF16), pltpu.VMEM((n + HALO, dh), F32), pltpu.VMEM((dh // 128, 384, 256), BF16),
         pltpu.VMEM((dh // 128, 384, 128), BF16), pltpu.VMEM((3, 128, dh), BF16)],
    )

    sp = Specs(H)
    sem = pltpu.SemaphoreType.DMA((H,))
    state = pltpu.VMEM((H, srows, dh), BF16)
    late = lambda a: (a, sp.cols("second", n, dh))
    output, gcol, grow, retain, dng, sttot, gloc, gend, gaug, ogg, dskip, sums = call(
        partial(forward_kernel, H, log_scale), "forward", 2,
        [whole(inputs), whole(out_grad), whole(gates), whole(flags), late(q), (k, sp.cols("both", n, dh)),
         (va, sp.lead("both", n, dh + 128)), late(og), late(pre), (pack, sp.lead("second", *pack.shape[1:])),
         (w_all, sp.lead("second", d, dh, last=2))],
        [whole(sds((n, d), BF16)), whole(sds((n, 128), F32)), whole(sds((8, n), F32)), whole(sds((H, 8, 128), F32)),
         (sds((H, d, dh), BF16), sp.lead("second", d, dh)),
         (sds((H, nch, srows, dh), BF16), sp.lead("second", nch, srows, dh)),
         (sds((H, nch - 1, srows, dh), BF16), sp.lead("second", nch - 1, srows, dh)),
         (sds((H, srows, dh), BF16), sp.lead("second", srows, dh)),
         (sds((H, n, dh + 128), BF16), sp.lead("second", n, dh + 128)), late(sds((H, n, dh), BF16)),
         late(sds((H, n, dh), BF16)), (sds((H, 8, dh), F32), sp.lead("second", 8, dh))],
        [pltpu.VMEM((n, d), F32), pltpu.VMEM((d, n), BF16), pltpu.VMEM((n, dh + 128), F32), pltpu.VMEM((n, dh), BF16),
         pltpu.VMEM((dh + 128, dh), BF16), pltpu.VMEM((dh, dh), F32), pltpu.VMEM((1, dh), F32),
         pltpu.VMEM((H, nch - 1, srows, dh), BF16), state, state, pltpu.VMEM((H, 8, 128), F32), sem, sem],
        collective_id=2, has_side_effects=True,
    )

    early = lambda a, *shape: (a, sp.lead("first", *shape))
    grads, ing, corr, minor = call(
        partial(backward_kernel, H, log_scale), "backward", 2,
        [whole(inputs), whole(halo), whole(gain), whole(flags), whole(out_grad), whole(normt), whole(gates), whole(gcol),
         whole(grow), whole(retain), whole(gend), (q, sp.cols("both", n, dh)), (k, sp.cols("both", n, dh)),
         (va, sp.lead("both", n, dh + 128)), early(gaug, n, dh + 128), early(sttot, nch, srows, dh),
         early(gloc, nch - 1, srows, dh), late(pre), (br, sp.cols("second", n + HALO, dh)), late(ogg), late(dskip),
         (pack, sp.lead("second", *pack.shape[1:])), (w_all, sp.lead("second", d, 2 * dh)),
         (dng, sp.lead("second", d, dh)), (sums, sp.lead("second", 8, dh))],
        [(sds((H, d, 3 * dh), BF16), sp.lead("second", d, 3 * dh)), whole(sds((n, d), F32)), whole(sds((HALO, d), F32)),
         whole(sds((H, 72, dh), F32))],
        [pltpu.VMEM((H, n, dh), BF16), pltpu.VMEM((H, n, dh), BF16), pltpu.VMEM((H, n, dh), BF16),
         pltpu.VMEM((n, 128), BF16), pltpu.VMEM((8, 128), F32),
         pltpu.VMEM((dh + 128, dh), BF16), pltpu.VMEM((dh + 128, dh), BF16), pltpu.VMEM((n, 128), F32),
         pltpu.VMEM((128, n), F32), pltpu.VMEM((8, 128), F32),
         pltpu.VMEM((HALO, d), F32), pltpu.VMEM((n + 2 * HALO, dh), F32), pltpu.VMEM((n + HALO, dh), F32),
         pltpu.VMEM((n, 2 * dh), BF16), pltpu.VMEM((n, dh), BF16), pltpu.VMEM((dh // 128, 128, 256), BF16), pltpu.VMEM((dh // 128, 128, 128), BF16),
         pltpu.VMEM((3, 128, dh), BF16), state, state, sem, sem],
        collective_id=3, has_side_effects=True,
    )

    total, minor, corr = scattered(grads, minor, corr)
    rows = total.shape[0]
    once = lambda *shape: pl.BlockSpec(shape, lambda i: (0,) * len(shape))
    tail = pl.BlockSpec((HALO, d), lambda i: (n // HALO - 1, 0))
    lines = (dh // 128, 128)
    shapes = [(rows, 2, dh), (rows, dh), (TAPS, dh), lines, (3, 4, 4, dh // 4), (3, 2 * H, dh), (1, 2), lines, lines,
              (d // 128, 128)]
    anywhere = pl.BlockSpec(memory_space=pl.ANY)
    up, down, conv_w, conv_b, maps, gate_w, gate_b, group, skip, gain, ing, output = pl.pallas_call(
        partial(finish_kernel, H),
        grid=(1,),
        out_shape=[*(sds(shape, F32) for shape in shapes), sds((n, d), F32), sds((n, d), BF16)],
        in_specs=[once(*total.shape), once(*minor.shape), once(*corr.shape), tail, anywhere],
        out_specs=[*(once(*shape) for shape in shapes), tail, anywhere],
        input_output_aliases={3: 10, 4: 11},
        name="finish",
    )(total, minor, corr, ing, output)
    return (output, ing, gain.reshape(d), up, conv_w, conv_b.reshape(dh), maps.transpose(0, 3, 1, 2),
            gate_w.transpose(0, 2, 1), gate_b.T, group.reshape(dh), skip.reshape(dh), down.T)


def solution(mesh):
    rows = P(("dp", "head"), None)
    small = (P(None, "head"), P("head"), P(None, "head", None, None), P(None, "head", None), P(None, "head"))
    return jax.shard_map(
        local,
        mesh=mesh,
        in_specs=(rows, P("dp"), P(), P("dp", None, "head"), *small, P("head"), P("head"), P("head", "dp"), rows),
        out_specs=(rows, rows, P(), P("dp", None, "head"), *small, P("head"), P("head"), P("head", "dp")),
        check_vma=False,
    )
```

```python
import math
from functools import partial

import jax
import jax.numpy as jnp
from jax import lax
from jax.experimental import pallas as pl
from jax.experimental.pallas import tpu as pltpu
from jax.sharding import PartitionSpec as P

EPS = 1e-05
NEG = -10000.0
CH = 256
HALO = 16
TAPS = 4
F32, BF16 = jnp.float32, jnp.bfloat16
HIGHEST = lax.Precision.HIGHEST


def nn(a, b, **kw):
    return lax.dot_general(a, b, (((1,), (0,)), ((), ())), preferred_element_type=F32, **kw)


def nt(a, b, **kw):
    return lax.dot_general(a, b, (((1,), (1,)), ((), ())), preferred_element_type=F32, **kw)


def tn(a, b, **kw):
    return lax.dot_general(a, b, (((0,), (0,)), ((), ())), preferred_element_type=F32, **kw)


def sigmoid(u):
    return 0.5 * jnp.tanh(0.5 * u) + 0.5


def log_sigmoid(u):
    return jnp.minimum(u, 0.0) - jnp.log(1.0 + jnp.exp(-jnp.abs(u)))


def iota(shape, dim):
    return lax.broadcasted_iota(jnp.int32, shape, dim)


def pick(block, lane):
    return jnp.sum(jnp.where(iota(block.shape, 1) == lane, block, 0.0), axis=1, keepdims=True)


def normalised(rows):
    centred = rows - jnp.mean(rows, axis=1, keepdims=True)
    inv_std = lax.rsqrt(jnp.mean(centred * centred, axis=1, keepdims=True) + EPS)
    return centred * inv_std, inv_std


def row_chunks(total, size):
    return [(r, min(size, total - r)) for r in range(0, total, size)]


def maps_of(pack_ref, cols, rest):
    rows = pack_ref[0, 8:24, cols]
    high = rows.astype(BF16)
    parts = [high]
    if rest:
        parts.append((rows - high.astype(F32)).astype(BF16))
    diagonal = iota((128, 128), 0) // 4 == iota((128, 128), 1) // 4
    made = []
    for part in parts:
        made.append([])
        for m in range(3):
            chosen = jnp.where(iota((16, 128), 0) == 4 * m + iota((16, 128), 1) % 4, 1.0, 0.0).astype(BF16)
            made[-1].append(jnp.where(diagonal, tn(part, chosen), 0.0).astype(BF16))
    return made


def gate_maps(pack_ref, into):
    for m in range(3):
        rows = pack_ref[0, 24 + 8 * m : 32 + 8 * m]
        into[m, 0:16] = jnp.concatenate([rows, jnp.zeros_like(rows)], axis=0).astype(BF16)


def lift_kernel(n_heads, x_ref, halo_ref, gain_ref, seg_ref, pack_ref, w_ref,
                q_ref, k_ref, va_ref, pre_ref, br_ref, og_ref, gates_ref, normt_ref, flags_ref,
                normed, ext, wqk, wv, gw):
    h = pl.program_id(0)
    n, dh = q_ref.shape
    me = lax.axis_index("head")

    @pl.when(h == 0)
    def _():
        gain = jnp.concatenate([gain_ref[j : j + 1] for j in range(gain_ref.shape[0])], axis=1)
        unit, _ = normalised(halo_ref[...].astype(F32))
        normed[0:HALO] = (unit * gain).astype(BF16)
        for r, rows in row_chunks(n, CH):
            unit, _ = normalised(x_ref[r : r + rows].astype(F32))
            scaled = unit * gain
            normed[HALO + r : HALO + r + rows] = scaled.astype(BF16)
            normt_ref[:, r : r + rows] = scaled.T.astype(BF16)
        gates_ref[...] = jnp.zeros_like(gates_ref)
        gw[...] = jnp.zeros_like(gw)
        token = iota(seg_ref.shape, 0) * 128 + iota(seg_ref.shape, 1)

        def segment(at):
            found = jnp.where(token == at, seg_ref[...], 0).astype(F32)
            return jnp.sum(jnp.sum(found, axis=1, keepdims=True), axis=0, keepdims=True)

        own = segment(me * n)
        before = jnp.where((segment(me * n - 1) == own) & (me > 0), 1.0, 0.0)
        after = jnp.where((segment(me * n + n) == own) & (me < n_heads - 1), 1.0, 0.0)
        flags_ref[0:8] = jnp.broadcast_to(before, (8, 128))
        flags_ref[8:16] = jnp.broadcast_to(after, (8, 128))

    gate_maps(pack_ref, gw)
    for b in range(dh // 128):
        (q_high, k_high, v_high), (q_rest, k_rest, v_rest) = maps_of(pack_ref, slice(128 * b, 128 * b + 128), True)
        for at, high, rest in ((0, q_high, q_rest), (128, k_high, k_rest)):
            wqk[b, 0:128, at : at + 128] = high
            wqk[b, 128:256, at : at + 128] = high
            wqk[b, 256:384, at : at + 128] = rest
        wv[b, 0:128] = v_high
        wv[b, 128:256] = v_high
        wv[b, 256:384] = v_rest
    lane = iota((1, 128), 1)
    bias = jnp.where(lane == h, pack_ref[0, 7:8, 0:1], 0.0) + jnp.where(lane == n_heads + h, pack_ref[0, 7:8, 1:2], 0.0)

    w = w_ref.at[0]
    halo = nn(normed[0:HALO], w[:, 0:dh]) * flags_ref[0:1, 0:1]
    ext[0:HALO] = halo
    br_ref[0:HALO] = halo.astype(BF16)
    for r, rows in row_chunks(n, 512):
        lifted = nn(normed[HALO + r : HALO + r + rows], w[...])
        branch = lifted[:, 0:dh]
        ext[HALO + r : HALO + r + rows] = branch
        og_ref[r : r + rows] = lifted[:, dh:].astype(BF16)
        branch_b = branch.astype(BF16)
        br_ref[HALO + r : HALO + r + rows] = branch_b
        pre = pack_ref[0, TAPS : TAPS + 1] + pack_ref[0, 0:1] * branch
        for j in range(1, TAPS):
            pre = pre + pack_ref[0, j : j + 1] * ext[HALO + r - j : HALO + r - j + rows]
        pre_ref[r : r + rows] = pre.astype(BF16)
        conv = pre * sigmoid(pre)
        conv_b = conv.astype(BF16)
        conv_rest = (conv - conv_b.astype(F32)).astype(BF16)
        branch_rest = (branch - branch_b.astype(F32)).astype(BF16)
        for b in range(dh // 128):
            cols = slice(128 * b, 128 * b + 128)
            parts = [conv_b[:, cols], conv_rest[:, cols], conv_b[:, cols]]
            qk = nn(jnp.concatenate(parts, axis=1), wqk[b]).astype(BF16)
            q_ref[r : r + rows, cols] = qk[:, 0:128]
            k_ref[r : r + rows, cols] = qk[:, 128:256]
            parts = [branch_b[:, cols], branch_rest[:, cols], branch_b[:, cols]]
            va_ref[0, r : r + rows, cols] = nn(jnp.concatenate(parts, axis=1), wv[b]).astype(BF16)
        va_ref[0, r : r + rows, dh : dh + 128] = jnp.where(
            iota((rows, 128), 1) == 0, 1.0, 0.0
        ).astype(BF16)
        gates_ref[r : r + rows] += (
            nt(q_ref[r : r + rows], gw[0])
            + nt(k_ref[r : r + rows], gw[1])
            + nt(va_ref[0, r : r + rows, 0:dh], gw[2])
            + bias
        )


def states(h, n_heads, gates_ref, k_ref, va_ref, gcol_ref, grow_ref, sloc, leaving, retain, st, ns):
    n, dh = k_ref.shape

    @pl.when(h == 0)
    def _():
        lower = jnp.where(iota((CH, CH), 0) >= iota((CH, CH), 1), 1.0, 0.0)
        for r, rows in row_chunks(n, CH):
            pre = gates_ref[r : r + rows]
            cum = nn(lower, log_sigmoid(pre), precision=HIGHEST)
            cum = pltpu.roll(cum, 128 - n_heads, 1)
            after = pltpu.roll(pre - cum, n_heads, 1)
            lane = iota((rows, 128), 1)
            both = jnp.where(lane < n_heads, cum, jnp.where(lane < 2 * n_heads, after, 0.0))
            gcol_ref[r : r + rows] = both
            grow_ref[:, r : r + rows] = both.T[0 : grow_ref.shape[0]]

    st[...] = jnp.zeros_like(st)
    ns[...] = jnp.zeros_like(ns)
    chunks = row_chunks(n, CH)
    whole_total = jnp.zeros((1, 1), F32)
    for c, (r, rows) in enumerate(chunks):
        block = gcol_ref[r : r + rows]
        total = pick(block[rows - 8 : rows], h)[7:8]
        whole_total = whole_total + total
        ending = jnp.exp(total + pick(block, n_heads + h))
        weighted = k_ref[r : r + rows].astype(F32) * ending
        st[...] = jnp.exp(total) * st[...] + tn(va_ref[0, r : r + rows, 0:dh], weighted.astype(BF16))
        ns[...] = jnp.exp(total) * ns[...] + jnp.sum(weighted, axis=0, keepdims=True)
        last = c == len(chunks) - 1
        to = leaving.at[h] if last else sloc.at[h, c]
        to[0:dh] = st[...].astype(BF16)
        to[dh : dh + 16] = jnp.where(iota((16, dh), 0) == 0, ns[0:1], 0.0).astype(BF16)
    retain[h] = jnp.broadcast_to(jnp.exp(whole_total), retain.shape[1:])


def decay_of(block, grow_ref, h, n_heads, r, rows, log_scale):
    cum = pick(block, h)
    after = grow_ref[pl.ds(n_heads + h, 1), r : r + rows]
    exponent = jnp.where(
        iota((rows, rows), 0) >= iota((rows, rows), 1), (cum + log_scale) + after, NEG
    )
    return jnp.exp(exponent), cum


def forward_kernel(n_heads, log_scale,
                   x_ref, og_all_ref, gates_ref, flags_ref, q_ref, k_ref, va_ref, gate_ref, pre_ref, pack_ref, w_ref,
                   out_ref, gcol_ref, grow_ref, retain_ref, dng_ref, sttot_ref, gloc_ref, gend_ref, gaug_ref, ogg_ref,
                   dskip_ref, sums_ref, gin_ref,
                   acc, ogt, numer, mixed_s, stb, gt, gn, sloc, leaving, landed, retain, ss, rs,
                   back_leaving, back_landed, back_ss, back_rs):
    step = pl.program_id(0)
    chain = Chain(1, retain, flags_ref[0:1, 0:1], leaving, landed, (ss, rs))
    place = chain.place
    early = range(back_landed.shape[0])
    back = Chain(-1, retain, flags_ref[8:9, 0:1], back_leaving, back_landed, (back_ss, back_rs), early)

    @pl.when(step == 0)
    def _():
        chain.greet()

    @pl.when(step < n_heads)
    def _():
        states(step, n_heads, gates_ref, k_ref, va_ref, gcol_ref, grow_ref, sloc, leaving, retain, gt, gn)

        @pl.when(place == 0)
        def _():
            chain.pump(step)

        @pl.when((place == 1) & (step > 0))
        def _():
            chain.pump(step - 1)

    @pl.when(step >= n_heads)
    def _():
        h = step - n_heads

        @pl.when((place == 1) & (h == 0))
        def _():
            chain.pump(n_heads - 1)

        @pl.when((place > 1) & (h > 0) & (2 * h - 1 < n_heads))
        def _():
            chain.pump(2 * h - 1)

        for c, (r, rows) in enumerate(row_chunks(q_ref.shape[0], CH)):
            span = slice(r, r + rows)
            decay, _ = decay_of(gcol_ref[span], grow_ref, h, n_heads, r, rows, log_scale)
            weights = (nt(q_ref[span], k_ref[span]) * decay).astype(BF16)
            numer[span] = nn(weights, va_ref[0, span])

        @pl.when((place > 1) & (2 * h < n_heads))
        def _():
            chain.pump(2 * h)

        mix(h, n_heads, log_scale, x_ref, og_all_ref, gcol_ref, q_ref, sloc, landed, gate_ref, pre_ref, pack_ref, w_ref,
            out_ref, dng_ref, sttot_ref, gloc_ref, gend_ref, gaug_ref, ogg_ref, dskip_ref, sums_ref,
            acc, ogt, numer, mixed_s, stb, gt, gn)

        for i in early:

            @pl.when(h == i)
            def _():
                back_leaving[i] = gend_ref[0]

        for i in early:

            @pl.when(h == jnp.minimum(back.place + i, n_heads - 1))
            def _():
                back.pump(i)

    @pl.when(step == 2 * n_heads - 1)
    def _():
        retain_ref[...] = retain[...]
        gin_ref[...] = back_landed[...]
        chain.finish()
        back.finish()


def mix(h, n_heads, log_scale,
        x_ref, og_all_ref, gcol_ref, q_ref, sloc, landed, gate_ref, pre_ref, pack_ref, w_ref,
        out_ref, dng_ref, sttot_ref, gloc_ref, gend_ref, gaug_ref, ogg_ref, dskip_ref, sums_ref,
        acc, ogt, numer, mixed_s, stb, gt, gn):
    n, dh = q_ref.shape
    gain = pack_ref[0, TAPS + 1 : TAPS + 2]
    skip = pack_ref[0, TAPS + 2 : TAPS + 3]
    down_t = w_ref.at[0]

    @pl.when(h == 0)
    def _():
        acc[...] = jnp.zeros_like(acc)
        for r, rows in row_chunks(n, CH):
            ogt[:, r : r + rows] = og_all_ref[r : r + rows].astype(F32).T.astype(BF16)
        stb[dh + 16 :] = jnp.zeros((stb.shape[0] - dh - 16, dh), BF16)

    prefix = jnp.zeros((1, 1), F32)
    gain_sum = jnp.zeros((1, dh), F32)
    skip_sum = jnp.zeros((1, dh), F32)
    pair_sum = jnp.zeros((1, 1), F32)
    for c, (r, rows) in enumerate(row_chunks(n, CH)):
        span = slice(r, r + rows)
        block = gcol_ref[span]
        total = pick(block[rows - 8 : rows], h)[7:8]
        state = landed[h].astype(F32) * jnp.exp(prefix)
        if c > 0:
            state = state + sloc[h, c - 1].astype(F32)
        prefix = prefix + total
        state_b = state.astype(BF16)
        sttot_ref[0, c] = state_b
        stb[0 : dh + 16] = state_b
        factor = jnp.exp(pick(block, h) + log_scale)
        both = numer[span] + factor * nt(q_ref[span], stb[...])
        denom = both[:, dh : dh + 1]
        r_inv = lax.rsqrt(denom * denom + 1.0)
        unit, inv_std = normalised(both[:, 0:dh] * r_inv)
        gate = gate_ref[span].astype(F32)
        sg = sigmoid(gate)
        silu_gate = gate * sg
        pre = pre_ref[span].astype(F32)
        conv = pre * sigmoid(pre)
        inner = unit * gain + skip * conv
        mixed = (inner * silu_gate).astype(BF16)
        mixed_s[span] = mixed
        acc[span] += nt(mixed, down_t[...])
        mixed_grad = nn(og_all_ref[span], down_t[...])
        hskip = mixed_grad * silu_gate
        ogg_ref[span] = (mixed_grad * inner * (sg * (1.0 + gate * (1.0 - sg)))).astype(BF16)
        dskip_ref[span] = (hskip * skip).astype(BF16)
        skip_sum = skip_sum + jnp.sum(hskip * conv, axis=0, keepdims=True)
        gain_sum = gain_sum + jnp.sum(hskip * unit, axis=0, keepdims=True)
        dhh = hskip * gain
        along = jnp.mean(dhh * unit, axis=1, keepdims=True)
        grad = (inv_std * r_inv) * (dhh - jnp.mean(dhh, axis=1, keepdims=True) - unit * along)
        radial = dh * EPS * along * inv_std * inv_std
        gaug_ref[0, span, 0:dh] = grad.astype(BF16)
        gaug_ref[0, span, dh : dh + 128] = jnp.where(
            iota((rows, 128), 1) == 0, -radial * denom * r_inv * r_inv, 0.0
        ).astype(BF16)
        pair_sum = pair_sum + jnp.sum(radial * r_inv * r_inv, axis=0, keepdims=True)
    sums_ref[0, 0:1] = gain_sum
    sums_ref[0, 1:2] = skip_sum
    sums_ref[0, 2:3] = jnp.broadcast_to(pair_sum, (1, dh))
    sums_ref[0, 3:8] = jnp.zeros((5, dh), F32)

    @pl.when(h == n_heads - 1)
    def _():
        for r, rows in row_chunks(n, CH):
            out_ref[r : r + rows] = (x_ref[r : r + rows].astype(F32) + acc[r : r + rows]).astype(BF16)

    dng_ref[0] = nn(ogt[...], mixed_s[...]).astype(BF16)

    gt[...] = jnp.zeros_like(gt)
    gn[...] = jnp.zeros_like(gn)
    for c, (r, rows) in reversed(list(enumerate(row_chunks(n, CH)))):
        span = slice(r, r + rows)
        block = gcol_ref[span]
        cum = pick(block, h)
        keep = jnp.exp(pick(block[rows - 8 : rows], h)[7:8])
        weighted = q_ref[span].astype(F32) * jnp.exp(cum + log_scale)
        side = gaug_ref[0, span, dh : dh + 128].astype(F32)[:, 0:1]
        gt[...] = keep * gt[...] + tn(gaug_ref[0, span, 0:dh], weighted.astype(BF16))
        gn[...] = keep * gn[...] + jnp.sum(weighted * side, axis=0, keepdims=True)
        to = gloc_ref.at[0, c - 1] if c else gend_ref.at[0]
        to[0:dh] = gt[...].astype(BF16)
        to[dh : dh + 16] = jnp.where(iota((16, dh), 0) == 0, gn[0:1], 0.0).astype(BF16)


def memory_back(h, n_heads, log_scale, chain,
                gates_ref, gcol_ref, grow_ref, q_ref, k_ref, va_ref, gaug_ref, sttot_ref, gloc_ref,
                dq_s, dk_s, dv_s, pg_s, bsum, dk_near, dv_near, stb, gtb, cols, rowsb, across):
    n, dh = q_ref.shape
    chunks = row_chunks(n, CH)

    @pl.when(h == 0)
    def _():
        stb[dh + 16 :] = jnp.zeros((stb.shape[0] - dh - 16, dh), BF16)
        gtb[dh + 16 :] = jnp.zeros((gtb.shape[0] - dh - 16, dh), BF16)
        cols[...] = jnp.zeros_like(cols)
        rowsb[...] = jnp.zeros_like(rowsb)
        across[...] = jnp.zeros_like(across)

    for c, (r, rows) in enumerate(chunks):
        span = slice(r, r + rows)
        stb[0 : dh + 16] = sttot_ref[0, c]
        q, k, va, gaug = q_ref[span], k_ref[span], va_ref[0, span], gaug_ref[0, span]
        decay, cum = decay_of(gcol_ref[span], grow_ref, h, n_heads, r, rows, log_scale)
        weights = nt(q, k) * decay
        wg = nt(gaug, va)
        d_scores = (wg * decay).astype(BF16)
        pair = wg * weights
        dq_far = jnp.exp(cum + log_scale) * nn(gaug, stb[...])
        dq_s[h, span] = (nn(d_scores, k) + dq_far).astype(BF16)
        dk_near[span] = tn(d_scores, q)
        dv_near[span] = tn(weights.astype(BF16), gaug[:, 0:dh])
        row_sum = jnp.sum(pair, axis=1, keepdims=True) + jnp.sum(dq_far * q.astype(F32), axis=1, keepdims=True)
        cols[span] = jnp.where(iota((rows, 128), 1) == h, row_sum, cols[span])
        rowsb[pl.ds(h, 1), span] = jnp.sum(pair, axis=0, keepdims=True)

    @pl.when((chain.place == 1) & (h == 0))
    def _():
        for i in chain.carried:
            chain.pump(i)

    @pl.when((chain.place > 2) & (h >= chain.carried[0]))
    def _():
        chain.pump(h)

    suffix = jnp.zeros((1, 1), F32)
    for c, (r, rows) in reversed(list(enumerate(chunks))):
        span = slice(r, r + rows)
        block = gcol_ref[span]
        total = pick(block[rows - 8 : rows], h)[7:8]
        after_col = pick(block, n_heads + h)
        grad_state = chain.landed[h].astype(F32) * jnp.exp(suffix)
        if c < len(chunks) - 1:
            grad_state = grad_state + gloc_ref[0, c].astype(F32)
        suffix = suffix + total
        gtb[0 : dh + 16] = grad_state.astype(BF16)
        through = jnp.exp(total) * jnp.sum(
            jnp.sum(sttot_ref[0, c].astype(F32) * grad_state, axis=1, keepdims=True), axis=0, keepdims=True
        )
        k = k_ref[span]
        ending = jnp.exp(total + after_col)
        dk_far = ending * nn(va_ref[0, span], gtb[...])
        dk_s[h, span] = (dk_near[span] + dk_far).astype(BF16)
        dv_s[h, span] = (dv_near[span] + ending * nt(k, gtb[...])[:, 0:dh]).astype(BF16)
        col_far = jnp.sum(dk_far * k.astype(F32), axis=1, keepdims=True)
        cols[span] = jnp.where(iota((rows, 128), 1) == n_heads + h, col_far, cols[span])
        across[c : c + 1] = jnp.where(iota((1, 128), 1) == h, through, across[c : c + 1])

    @pl.when(h == n_heads - 1)
    def _():
        upper = jnp.where(iota((CH, CH), 0) <= iota((CH, CH), 1), 1.0, 0.0)
        strict = jnp.where(iota((CH, CH), 0) > iota((CH, CH), 1), 1.0, 0.0)
        lane = iota((CH, 128), 1)
        bias_sum = jnp.zeros((1, 128), F32)
        for c, (r, rows) in enumerate(chunks):
            span = slice(r, r + rows)
            near_col = rowsb[:, span].T
            far = pltpu.roll(cols[span], 128 - n_heads, 1)
            forget = (
                nn(upper, cols[span] - near_col, precision=HIGHEST)
                + nn(strict, far, precision=HIGHEST)
                + across[c : c + 1]
            )
            pre = gates_ref[span]
            forget = pltpu.roll(forget, n_heads, 1) * sigmoid(-pre)
            grads = jnp.where(
                lane < n_heads, near_col + far, jnp.where(lane < 2 * n_heads, forget, 0.0)
            )
            bias_sum = bias_sum + jnp.sum(grads, axis=0, keepdims=True)
            pg_s[span] = grads.astype(BF16)
        bsum[...] = jnp.where(iota((8, 128), 0) == 0, bias_sum, 0.0)


def lower(h, n_heads,
          halo_ref, gain_ref, flags_ref, normt_ref, pg_ref, bsum_ref, q_ref, k_ref, va_ref,
          dq_s, dk_s, dv_s, pre_ref, br_ref, ogg_ref, dskip_ref,
          pack_ref, w_ref, sums_ref,
          upg_ref, ng_ref, corr_ref, minor_ref,
          pext, lifted, conv_s, wqk, wv, gw, gacc, first, last):
    n, dh = q_ref.shape
    link = flags_ref[0:1, 0:1]
    w = w_ref.at[0]

    minor_out = minor_ref
    minor_ref = minor_out.at[pl.ds(h, 1)]
    minor_ref[0, 67:] = jnp.zeros((minor_ref.shape[1] - 67, dh), F32)

    @pl.when(first)
    def _():
        corr_ref[...] = jnp.zeros_like(corr_ref)
        ng_ref[...] = jnp.zeros_like(ng_ref)
        gacc[...] = jnp.zeros_like(gacc)
        pext[0:HALO] = jnp.zeros((HALO, dh), F32)
        pext[HALO + n :] = jnp.zeros((HALO, dh), F32)
        gw[...] = jnp.zeros_like(gw)

    gate_maps(pack_ref, gw)
    for b in range(dh // 128):
        [(q_high, k_high, v_high)] = maps_of(pack_ref, slice(128 * b, 128 * b + 128), False)
        wqk[b, :, 0:128] = q_high
        wqk[b, :, 128:256] = k_high
        wv[b] = v_high

    taps = [jnp.zeros((1, dh), F32) for _ in range(TAPS)]
    bias_sum = jnp.zeros((1, dh), F32)
    for r, rows in row_chunks(n, CH):
        span = slice(r, r + rows)
        pg = pg_ref[span]
        dqt = (dq_s[h, span].astype(F32) + nn(pg, gw[0])).astype(BF16)
        dkt = (dk_s[h, span].astype(F32) + nn(pg, gw[1])).astype(BF16)
        dvt = (dv_s[h, span].astype(F32) + nn(pg, gw[2])).astype(BF16)
        pre = pre_ref[span].astype(F32)
        sg = sigmoid(pre)
        conv_s[span] = (pre * sg).astype(BF16)
        slope = sg * (1.0 + pre * (1.0 - sg))
        dq_s[h, span] = dqt
        dk_s[h, span] = dkt
        dv_s[h, span] = dvt
        for b in range(dh // 128):
            at = slice(128 * b, 128 * b + 128)
            both = jnp.concatenate([dqt[:, at], dkt[:, at]], axis=1)
            conv_grad = nt(both, wqk[b]) + dskip_ref[span, at].astype(F32)
            pext[HALO + r : HALO + r + rows, at] = conv_grad * slope[:, at]
        pre_grad = pext[HALO + r : HALO + r + rows]
        bias_sum = bias_sum + jnp.sum(pre_grad, axis=0, keepdims=True)
        branch = br_ref[r : r + rows + HALO].astype(F32)
        for j in range(TAPS):
            taps[j] = taps[j] + jnp.sum(pre_grad * branch[HALO - j : HALO - j + rows], axis=0, keepdims=True)
    for j in range(TAPS):
        minor_ref[0, j : j + 1] = taps[j]
    minor_ref[0, TAPS : TAPS + 1] = bias_sum
    minor_ref[0, TAPS + 1 : 8] = jnp.zeros((8 - TAPS - 1, dh), F32)
    minor_ref[0, 8:16] = sums_ref[0]

    halo_grad = jnp.zeros((HALO, dh), F32)
    for j in range(1, TAPS):
        halo_grad = halo_grad + pack_ref[0, j : j + 1] * pext[j : HALO + j]
    halo_b = (halo_grad * link).astype(BF16)
    corr_ref[...] += nt(halo_b, w[:, 0:dh])
    for r, rows in row_chunks(n, CH):
        span = slice(r, r + rows)
        grad = jnp.zeros((rows, dh), F32)
        for j in range(TAPS):
            grad = grad + pack_ref[0, j : j + 1] * pext[HALO + r + j : HALO + r + j + rows]
        for b in range(dh // 128):
            at = slice(128 * b, 128 * b + 128)
            lifted[span, at] = (grad[:, at] + nt(dv_s[h, span, at], wv[b])).astype(BF16)
        lifted[span, dh : 2 * dh] = ogg_ref[span]
        ng_ref[span] += nt(lifted[span], w[...])

    unit_halo, _ = normalised(halo_ref[...].astype(F32))
    gain = jnp.concatenate([gain_ref[j : j + 1] for j in range(gain_ref.shape[0])], axis=1)
    normed_halo = (unit_halo * gain).astype(BF16)
    d = normt_ref.shape[0]
    for r, rows in row_chunks(d, d // 2):
        span = slice(r, r + rows)
        upg = nn(normt_ref[span], lifted[...])
        upg = jnp.concatenate([upg[:, 0:dh] + tn(normed_halo[:, span], halo_b), upg[:, dh:]], axis=1)
        upg_ref[span] = upg.astype(BF16)
        along = upg * w[span].astype(F32)
        part = along[:, 0:128]
        for at in range(128, 2 * dh, 128):
            part = part + along[:, at : at + 128]
        gacc[span] += part

    fold = jnp.where(iota((8, 128), 1) % 4 == iota((8, 128), 0), 1.0, 0.0)
    diagonal = iota((128, 128), 0) // 4 == iota((128, 128), 1) // 4
    for b in range(dh // 128):
        at = slice(128 * b, 128 * b + 128)
        qk_grad = tn(conv_s[:, at], jnp.concatenate([dq_s[h, :, at], dk_s[h, :, at]], axis=1))
        v_grad = tn(br_ref[HALO:, at], dv_s[h, :, at])
        for m, full in enumerate((qk_grad[:, 0:128], qk_grad[:, 128:256], v_grad)):
            minor_ref[0, 16 + 8 * m : 24 + 8 * m, at] = nt(fold, jnp.where(diagonal, full, 0.0), precision=HIGHEST)
    minor_ref[0, 40:48] = tn(pg_ref[...], q_ref[...])[0:8]
    minor_ref[0, 48:56] = tn(pg_ref[...], k_ref[...])[0:8]
    minor_ref[0, 56:64] = tn(pg_ref[...], va_ref[0, :, 0:dh])[0:8]

    @pl.when(last)
    def _():
        total = nt(jnp.ones((8, 128), F32), gacc[...], precision=HIGHEST)[0:1] / gain
        for i in range(n_heads):
            minor_out[i, 66:67] = jnp.broadcast_to(bsum_ref[0:1, n_heads + i : n_heads + i + 1], (1, dh))
            for j in range(d // dh):
                minor_out[i, 64 + j : 65 + j] = total[:, dh * j : dh * j + dh]


def backward_kernel(inside, n_heads, log_scale,
                    halo_ref, gain_ref, flags_ref, normt_ref, gates_ref, gcol_ref, grow_ref, retain_ref,
                    gend_ref, gin_ref, q_ref, k_ref, va_ref, gaug_ref, sttot_ref, gloc_ref, pre_ref, br_ref, ogg_ref,
                    dskip_ref, pack_ref, w_ref, sums_ref, *rest):
    if inside:
        dng, up_total, down_total, minor_total, corr_in, ng_ref, *rest = rest
    else:
        upg_ref, minor_ref, corr_ref, ng_ref, *rest = rest
    (dq_s, dk_s, dv_s, pg_s, bsum, stb, gtb, cols, rowsb, across, pext, lifted, conv_s, wqk, wv, gw, gacc,
     leaving, landed, ss, rs, *rest) = rest
    step = pl.program_id(0)
    done = gin_ref.shape[0]
    chain = Chain(-1, retain_ref, flags_ref[8:9, 0:1], leaving, landed, (ss, rs), range(done, n_heads))
    dh = q_ref.shape[1]
    near_k, near_v = ng_ref.at[:, 0:dh], ng_ref.at[:, dh : 2 * dh]
    if inside:
        here = Place()
        upg_ref, minor_ref, corr_ref, landing, m0, m1, n0, n1, load, ms, mr, *rest = rest
        many = len(rest) // 2
        up = Scatter(here, *rest[:many])
        down = Scatter(here, *rest[many:])

    @pl.when(step == 0)
    def _():
        if inside:
            greet([here.device(**to) for to in NEIGHBOURS])
        else:
            chain.greet()
        leaving[...] = gend_ref[...]
        landed[0:done] = gin_ref[...]

        @pl.when(chain.place == 0)
        def _():
            for i in chain.carried:
                chain.pump(i)

    @pl.when((step >= done) & (step < n_heads) & (chain.place == 2))
    def _():
        chain.pump(step)

    @pl.when(step < n_heads)
    def _():
        memory_back(step, n_heads, log_scale, chain, gates_ref, gcol_ref, grow_ref, q_ref, k_ref, va_ref, gaug_ref,
                    sttot_ref, gloc_ref, dq_s, dk_s, dv_s, pg_s, bsum, near_k, near_v, stb, gtb, cols, rowsb, across)

    if inside:

        @pl.when(step == n_heads + 1)
        def _():
            up.given(1)

        @pl.when(step == n_heads + 3)
        def _():
            up.given(0)

    @pl.when(step >= n_heads)
    def _():
        i = step - n_heads
        lower(turned(i), n_heads, halo_ref, gain_ref, flags_ref, normt_ref, pg_s, bsum, q_ref,
              k_ref, va_ref, dq_s, dk_s, dv_s, pre_ref, br_ref, ogg_ref, dskip_ref, pack_ref, w_ref, sums_ref,
              upg_ref, ng_ref, corr_ref, minor_ref, pext, lifted, conv_s, wqk, wv, gw, gacc, i == 0, i == n_heads - 1)

    if inside:
        loads = [pltpu.make_async_copy(dng.at[here.head(fx, 0)], down.own.at[fx], load.at[fx]) for fx in (0, 1)]

        def at_end_of(number):
            return pl.when(step == number)

        @at_end_of(1)
        def _():
            for fx in (1, 0):
                loads[fx].start()
                down.give(dng.at[here.head(fx, 1)], fx)

        @at_end_of(2)
        def _():
            for fx in (1, 0):
                loads[fx].wait()
                for k in ORDER:
                    down.first(fx, k)

        @at_end_of(3)
        def _():
            for k in ORDER:
                down.away(k)

        @at_end_of(4)
        def _():
            up.give(upg_ref, 1)
            for k in ORDER:
                down.home(k)

        @at_end_of(5)
        def _():
            up.own[1] = upg_ref[...]
            for k in ORDER:
                up.first(1, k)
            for k in ORDER:
                down.third(k)

        @at_end_of(6)
        def _():
            up.give(upg_ref, 0)
            for k in ORDER:
                up.away(k)
            down.final(down_total)

        @at_end_of(7)
        def _():
            up.own[0] = upg_ref[...]
            before = (here.z * 2 + here.y, lax.rem(here.head() + 3, 4))
            sent = [remote(corr_ref, landing, (ms, mr), 6, before)]
            sent[0].start()

            def send(src, dst, at, to):
                copy = remote(src, dst, (ms, mr), at, here.device(**to))
                copy.start()
                sent.append(copy)

            def arrived(dst, at):
                remote(dst, dst, (ms, mr), at, here.device(fc=1)).wait_recv()

            for fx in (0, 1):
                send(minor_ref.at[here.head(fx, 1)], n0.at[fx], fx, dict(fc=1))
            up.first(0, 1)
            up.first(0, 2)
            for fx in (1, 0):
                arrived(n0.at[fx], fx)
                m0[fx] = minor_ref[here.head(fx, 0)] + n0[fx]
            send(m0.at[1], n1.at[0], 2, dict(fx=1))
            up.home(1)
            up.first(0, 3)
            up.first(0, 0)
            up.home(2)
            arrived(n1.at[0], 2)
            m1[0] = m0[0] + n1[0]
            send(m1.at[0], n1.at[1], 3, dict(fy=1))
            up.third(1)
            up.home(3)
            up.third(2)
            arrived(n1.at[1], 3)
            m1[1] = m1[0] + n1[1]
            send(m1.at[1], n1.at[2], 4, dict(k=1))
            up.home(0)
            up.third(3)
            arrived(n1.at[2], 4)
            m1[2] = m1[1] + n1[2]
            send(m1.at[2], n1.at[3], 5, dict(k=2))
            up.third(0)
            up.final(up_total)
            arrived(n1.at[3], 5)
            minor_total[...] = m1[2] + n1[3]
            arrived(landing, 6)
            corr_in[...] = landing[...]
            for copy in sent:
                copy.wait_send()
            down.given(1)
            down.given(0)
            up.finish()
            down.finish()

    @pl.when(step == 2 * n_heads - 1)
    def _():
        chain.finish()


ORDER = (1, 2, 3, 0)


class Scatter:
    SEMAPHORES = ((2, 4), (2, 4), (2, 2, 4), (2, 2, 4), (2, 4), (2, 4), (2, 3), (2, 3))

    @staticmethod
    def scratch(d, rows, cols):
        half = rows // 2
        sem = pltpu.SemaphoreType.DMA
        return [pltpu.VMEM((2, d, cols), BF16), pltpu.VMEM((2, d, cols), BF16), pltpu.VMEM((2, 4, half, cols), BF16),
                pltpu.VMEM((2, 4, half, cols), BF16), pltpu.VMEM((2, 4, half, cols), BF16),
                pltpu.VMEM((2, 3, half, cols), BF16), *(sem(shape) for shape in Scatter.SEMAPHORES)]

    def __init__(self, here, own, r0, r1a, r1b, r2, r3, *sems):
        self.here, self.own, self.r0, self.r1a, self.r1b, self.r2, self.r3 = here, own, r0, r1a, r1b, r2, r3
        self.s0, self.s1, self.s2, self.s3 = (tuple(sems[i : i + 2]) for i in (0, 2, 4, 6))
        self.half = r3.shape[2]

    def piece(self, fx, k, fy, p):
        return self.own.at[fx, pl.ds(self.here.rows(k, fy, 2 * self.half) + self.half * p, self.half)]

    def pair(self, k):
        return pl.ds(pl.multiple_of(self.here.along_z(k) * 4 * self.half, 16), 4 * self.half)

    def send(self, src, dst, sems, at, to):
        remote(src, dst, sems, at, self.here.device(**to)).start()

    def arrived(self, dst, sems, at):
        remote(dst, dst, sems, at, self.here.device(fc=1)).wait_recv()

    def sent(self, src, sems, at):
        remote(src, src, sems, at, self.here.device(fc=1)).wait_send()

    def add(self, into, other):
        into[...] = (into[...].astype(F32) + other[...].astype(F32)).astype(BF16)

    def give(self, src, fx):
        for k in ORDER:
            self.send(src.at[self.pair(k)], self.r0.at[fx, self.pair(k)], self.s0, (fx, k), dict(fc=1))

    def given(self, fx):
        for k in range(4):
            self.sent(self.r0.at[fx, self.pair(k)], self.s0, (fx, k))

    def first(self, fx, k):
        self.arrived(self.r0.at[fx, self.pair(k)], self.s0, (fx, k))
        self.add(self.own.at[fx, self.pair(k)], self.r0.at[fx, self.pair(k)])
        self.send(self.piece(fx, k, 1, 0), self.r1a.at[fx, k], self.s1, (0, fx, k), dict(fy=1))
        if fx:
            for fy in (1, 0):
                self.send(self.piece(1, k, fy, 1), self.r1b.at[fy, k], self.s1, (1, fy, k), dict(fx=1))

    def away(self, k):
        self.arrived(self.r1a.at[1, k], self.s1, (0, 1, k))
        self.add(self.piece(1, k, 0, 0), self.r1a.at[1, k])
        self.send(self.piece(1, k, 0, 0), self.r2.at[0, k], self.s2, (0, k), dict(fx=1))

    def home(self, k):
        self.arrived(self.r1a.at[0, k], self.s1, (0, 0, k))
        self.add(self.piece(0, k, 0, 0), self.r1a.at[0, k])
        for f in (1, 0):
            self.arrived(self.r1b.at[f, k], self.s1, (1, f, k))
            self.add(self.piece(0, k, f, 1), self.r1b.at[f, k])
            if f:
                self.send(self.piece(0, k, 1, 1), self.r2.at[1, k], self.s2, (1, k), dict(fy=1))

    def third(self, k):
        for p in (0, 1):
            self.arrived(self.r2.at[p, k], self.s2, (p, k))
            self.add(self.piece(0, k, 0, p), self.r2.at[p, k])
            if k:
                self.send(self.piece(0, k, 0, p), self.r3.at[p, k - 1], self.s3, (p, k - 1), dict(k=k))

    def final(self, total):
        for p in (0, 1):
            summed = self.piece(0, 0, 0, p)[...].astype(F32)
            for k in range(3):
                self.arrived(self.r3.at[p, k], self.s3, (p, k))
                summed = summed + self.r3[p, k].astype(F32)
            total[self.half * p : self.half * p + self.half] = summed

    def finish(self):
        for k in range(4):
            for f in (0, 1):
                self.sent(self.r1a.at[f, k], self.s1, (0, f, k))
                self.sent(self.r1b.at[f, k], self.s1, (1, f, k))
                self.sent(self.r2.at[f, k], self.s2, (f, k))
                if k < 3:
                    self.sent(self.r3.at[f, k], self.s3, (f, k))


def turned(i):
    head = lax.axis_index("head")
    x, c = lax.div(head, 2), lax.rem(head, 2)
    fx, fc = 1 - lax.div(i, 2), 1 - lax.rem(i, 2)
    return (x + fx - 2 * x * fx) * 2 + (c + fc - 2 * c * fc)


class Specs:
    def __init__(self, heads, rounds=2):
        self.heads, self.steps = heads, heads * rounds
        self.index = dict(
            both=lambda s: lax.rem(s, heads),
            first=lambda s: jnp.minimum(s, heads - 1),
            second=lambda s: jnp.maximum(s - heads, 0),
            turned=lambda s: turned(jnp.maximum(s - heads, 0)),
            mixed=lambda s: jnp.where(s < heads, s, turned(jnp.maximum(s - heads, 0))),
        )

    def whole(self, *shape):
        return pl.BlockSpec(shape, lambda s: (0,) * len(shape), pipeline_mode=pl.Buffered(1))

    def cols(self, when, rows, cols):
        index = self.index[when]
        return pl.BlockSpec((None, rows, cols), lambda s: (index(s), 0, 0))

    def lead(self, when, *shape, last=0):
        index = self.index[when]
        return pl.BlockSpec((1, *shape), lambda s: (index(s),) + (0,) * (len(shape) - 1) + (last,))


def params(**kw):
    return pltpu.CompilerParams(dimension_semantics=("arbitrary",), vmem_limit_bytes=62 << 20, **kw)


def sds(shape, dtype):
    return jax.ShapeDtypeStruct(shape, dtype)


def shifted(x, by):
    heads = lax.axis_size("head")
    pairs = [(i, i + by) for i in range(heads) if 0 <= i + by < heads]
    return lax.ppermute(x, "head", pairs)


MESH = pl.DeviceIdType.MESH


class Place:
    def __init__(self):
        dp, head = lax.axis_index("dp"), lax.axis_index("head")
        self.z, self.y = lax.div(dp, 2), lax.rem(dp, 2)
        self.x, self.c = lax.div(head, 2), lax.rem(head, 2)

    def along_z(self, k):
        z = self.z
        return (z, z + 1 - 2 * lax.rem(z, 2), lax.rem(z + 2, 4), 3 - z)[k]

    def device(self, k=0, fy=0, fx=0, fc=0):
        y, x, c = (1 - v if f else v for v, f in ((self.y, fy), (self.x, fx), (self.c, fc)))
        return (self.along_z(k) * 2 + y, x * 2 + c)

    def head(self, fx=0, fc=0):
        return (1 - self.x if fx else self.x) * 2 + (1 - self.c if fc else self.c)

    def rows(self, k, fy, size):
        y = 1 - self.y if fy else self.y
        return pl.multiple_of((self.along_z(k) * 2 + y) * size, 16)


NEIGHBOURS = (dict(fc=1), dict(fx=1), dict(fx=1, fc=1), dict(fy=1), dict(k=1), dict(k=2), dict(k=3))


def greet(devices):
    barrier = pltpu.get_barrier_semaphore()
    for device in devices:
        pl.semaphore_signal(barrier, inc=1, device_id=device, device_id_type=MESH)
    pl.semaphore_wait(barrier, len(devices))


def remote(src, dst, sems, at, device):
    send, recv = sems
    return pltpu.make_async_remote_copy(
        src_ref=src, dst_ref=dst, send_sem=send.at[at], recv_sem=recv.at[at], device_id=device, device_id_type=MESH
    )


class Gather:
    SEMAPHORES = ((2, 3), (2, 3), (2, 4), (2, 4), (2, 4, 2), (2, 4, 2), (2, 4, 4), (2, 4, 4))
    FLIPS = ((dict(fx=1), dict(fy=1)), (dict(fy=1), dict(fx=1)))

    def __init__(self, here, shard, w, sems):
        self.here, self.shard, self.w = here, shard, w
        self.z, self.f, self.s, self.d = (tuple(sems[i : i + 2]) for i in (0, 2, 4, 6))
        self.rows = shard.shape[0]
        self.started = []

    def block(self, p, k=0, fy=0, fx=0, fc=0):
        half = self.rows // 2
        return self.w.at[self.here.head(fx, fc), pl.ds(self.here.rows(k, fy, self.rows) + half * p, half)]

    def send(self, src, dst, sems, at, to):
        copy = remote(src, dst, sems, at, self.here.device(**to))
        copy.start()
        self.started.append(copy)

    def arrived(self, dst, sems, at):
        remote(dst, dst, sems, at, self.here.device(fc=1)).wait_recv()

    def begin(self):
        half = self.rows // 2
        for p in (0, 1):
            mine = self.shard.at[pl.ds(half * p, half)]
            first, second = self.FLIPS[p]
            self.send(mine, self.block(p), self.z, (p, 0), dict(k=1))
            self.send(mine, self.block(p), self.f, (p, 0), first)
        for p in (0, 1):
            mine = self.shard.at[pl.ds(half * p, half)]
            first, second = self.FLIPS[p]
            for k in (2, 3):
                self.send(mine, self.block(p), self.z, (p, k - 1), dict(k=k))
            self.send(mine, self.block(p), self.s, (p, 0, 0), second)
            self.send(mine, self.block(p), self.d, (p, 0, 0), dict(fc=1))

    def from_z(self, k):
        for p in (0, 1):
            first, second = self.FLIPS[p]
            block = self.block(p, k)
            self.arrived(block, self.z, (p, k - 1))
            self.send(block, block, self.f, (p, k), first)
            self.send(block, block, self.s, (p, k, 0), second)
            self.send(block, block, self.d, (p, k, 0), dict(fc=1))

    def from_first(self, k):
        for p in (0, 1):
            first, second = self.FLIPS[p]
            block = self.block(p, k, **first)
            self.arrived(block, self.f, (p, k))
            self.send(block, block, self.s, (p, k, 1), second)
            self.send(block, block, self.d, (p, k, 1), dict(fc=1))

    def from_second(self, k):
        for i in (0, 1):
            for p in (0, 1):
                first, second = self.FLIPS[p]
                block = self.block(p, k, **(dict(**first, **second) if i else second))
                self.arrived(block, self.s, (p, k, i))
                self.send(block, block, self.d, (p, k, 2 + i), dict(fc=1))

    def from_core(self, k):
        for p in (0, 1):
            first, second = self.FLIPS[p]
            for i, over in enumerate((dict(), first, second, dict(**first, **second))):
                self.arrived(self.block(p, k, fc=1, **over), self.d, (p, k, i))

    def run(self):
        self.begin()
        self.from_first(0)
        for k in (1, 2, 3):
            self.from_z(k)
            self.from_second(k - 1)
            self.from_first(k)
        self.from_second(3)
        for k in range(4):
            self.from_core(k)
        for copy in self.started:
            copy.wait_send()


def gather_kernel(up_raw, down, taps, conv_bias, group, skip, gate_bias, maps, gates, x, w, pack_all, halo,
                  shard, pack, rows_s, local_sem, ms, mr, *sems):
    here = Place()
    n = x.shape[0]
    dh = pack.shape[1]
    rows = shard.shape[0]
    shard[:, 0:dh] = up_raw[:, 0]
    shard[:, dh : 2 * dh] = up_raw[:, 1]
    shard[:, 2 * dh :] = down[...]
    fill_pack(taps, conv_bias, group, skip, gate_bias, maps, gates, pack, rows_s)
    copies = [pltpu.make_async_copy(pack, pack_all.at[here.head()], local_sem.at[0]),
              pltpu.make_async_copy(shard, w.at[here.head(), pl.ds(here.rows(0, 0, rows), rows)], local_sem.at[1])]
    for copy in copies:
        copy.start()
    greet([here.device(**to) for to in NEIGHBOURS])
    small = []
    for i, to in enumerate(NEIGHBOURS[:3]):
        small.append(remote(pack, pack_all.at[here.head()], (ms, mr), i, here.device(**to)))
    after = (here.z * 2 + here.y, lax.rem(here.head() + 1, 4))
    small.append(remote(x.at[pl.ds(n - HALO, HALO)], halo, (ms, mr), 3, after))
    for copy in small:
        copy.start()
    Gather(here, shard, w, sems).run()
    for i, to in enumerate(NEIGHBOURS[:3]):
        from_them = pack_all.at[here.head(to.get("fx", 0), to.get("fc", 0))]
        remote(from_them, from_them, (ms, mr), i, here.device(fc=1)).wait_recv()
    remote(halo, halo, (ms, mr), 3, here.device(fc=1)).wait_recv()
    for copy in small:
        copy.wait_send()
    for copy in copies:
        copy.wait()


def fill_pack(taps, conv_bias, group, skip, gate_bias, maps, gates, pack, rows_s):
    dh = pack.shape[1]
    pack[0:TAPS] = taps[...]
    for i, ref in enumerate((conv_bias, group, skip)):
        for j in range(dh // 128):
            pack[TAPS + i : TAPS + i + 1, 128 * j : 128 * j + 128] = ref[j : j + 1]
    lane = iota((1, dh), 1)
    pack[7:8] = jnp.where(lane == 0, gate_bias[0:1, 0:1], jnp.where(lane == 1, gate_bias[0:1, 1:2], 0.0))
    rows_s[...] = jnp.zeros_like(rows_s)
    for m in range(3):
        for i in range(4):
            rows_s[16 * m + 4 * i : 16 * m + 4 * i + 4, 0 : dh // 4] = maps[m, i]
        pack[24 + 8 * m : 32 + 8 * m] = gates[m].astype(F32)
    wide = nn(rows_s[...], jnp.where(iota((128, dh), 1) // 4 == iota((128, dh), 0), 1.0, 0.0), precision=HIGHEST)
    for m in range(3):
        rows = jnp.zeros((4, dh), F32)
        for i in range(4):
            rows = jnp.where(iota((4, dh), 1) % 4 == i, wide[16 * m + 4 * i : 16 * m + 4 * i + 4], rows)
        pack[8 + 4 * m : 12 + 4 * m] = rows
    pack[20:24] = jnp.zeros((4, dh), F32)


def gathered(up_weight, down, small, x, heads):
    dp = lax.axis_size("dp")
    n, d = x.shape
    vmem = pl.BlockSpec(memory_space=pltpu.VMEM)
    rows, _, dh = up_weight.shape
    if not by_hand(rows):
        up = up_weight.reshape(rows, 2 * dh)
        pack = pl.pallas_call(
            fill_pack, out_shape=sds((48, dh), F32), in_specs=[vmem] * 7, out_specs=vmem,
            scratch_shapes=[pltpu.VMEM((48, 128), F32)], name="pack",
        )(*small)

        def all_of(shard):
            w = lax.all_gather(shard, ("dp", "head"), axis=0)
            w = w.reshape(dp, heads, *shard.shape).transpose(1, 0, 2, 3)
            return w.reshape(heads, dp * shard.shape[0], shard.shape[1])

        w = all_of(jnp.concatenate([up, down], axis=1))
        return w, lax.all_gather(pack, "head", axis=0), shifted(x[n - HALO :], 1)
    sem = pltpu.SemaphoreType.DMA
    anywhere = pl.BlockSpec(memory_space=pl.ANY)
    return pl.pallas_call(
        gather_kernel,
        out_shape=[sds((heads, dp * rows, 3 * dh), BF16), sds((heads, 48, dh), F32), sds((HALO, d), BF16)],
        in_specs=[vmem, vmem, *[vmem] * 7, anywhere],
        out_specs=[anywhere] * 3,
        scratch_shapes=[pltpu.VMEM((rows, 3 * dh), BF16), pltpu.VMEM((48, dh), F32), pltpu.VMEM((48, 128), F32),
                        sem((2,)), sem((4,)), sem((4,)), *(sem(shape) for shape in Gather.SEMAPHORES)],
        compiler_params=pltpu.CompilerParams(collective_id=0, has_side_effects=True),
        name="gather",
    )(up_weight, down, *small, x)


def by_hand(rows):
    return lax.axis_size("dp") == 8 and lax.axis_size("head") == 4 and rows % 32 == 0


def finish_kernel(n_heads, x, og, norm_gain, up_total, down_total, minor, corr, ng, output,
                  up, down, conv_w, conv_b, maps, gate_w, gate_b, group, skip, gain, ing, out):
    step = pl.program_id(0)
    rows = x.shape[0]
    out[...] = output[...]
    unit, inv_std = normalised(x[...].astype(F32))
    follows = jnp.where((lax.axis_index("head") < n_heads - 1) & (step == pl.num_programs(0) - 1), 1.0, 0.0)
    grads = ng[...] + jnp.concatenate([jnp.zeros((rows - HALO, x.shape[1]), F32), corr[...] * follows], axis=0)
    scaled = grads * jnp.concatenate([norm_gain[j : j + 1] for j in range(norm_gain.shape[0])], axis=1)
    ing[...] = og[...].astype(F32) + inv_std * (
        scaled - jnp.mean(scaled, axis=1, keepdims=True) - unit * jnp.mean(scaled * unit, axis=1, keepdims=True)
    )

    @pl.when(step == 0)
    def _():
        finish_small(up_total, down_total, minor, up, down, conv_w, conv_b, maps, gate_w, gate_b, group, skip, gain)


def finish_small(up_total, down_total, minor, up, down, conv_w, conv_b, maps, gate_w, gate_b, group, skip, gain):
    dh = minor.shape[1]
    up[:, 0] = up_total[:, 0:dh]
    up[:, 1] = up_total[:, dh : 2 * dh]
    down[...] = down_total[...]
    conv_w[...] = minor[0:TAPS]
    for j in range(dh // 128):
        at = slice(128 * j, 128 * j + 128)
        for ref, row in ((conv_b, TAPS), (group, 8), (skip, 9)):
            ref[j : j + 1] = minor[row : row + 1, at]
        for i in range(gain.shape[0] * 128 // dh):
            gain[dh // 128 * i + j : dh // 128 * i + j + 1] = minor[64 + i : 65 + i, at]
    for m in range(3):
        gate_w[m] = minor[40 + 8 * m : 48 + 8 * m]
    for i in range(4):
        chosen = jnp.where(iota((dh, 128), 0) == 4 * iota((dh, 128), 1) + i, 1.0, 0.0)
        rows = nn(minor[16:40], chosen, precision=HIGHEST)
        for m in range(3):
            maps[m, i] = rows[8 * m : 8 * m + 4, 0 : dh // 4]
    gate_b[0:1, 0:1] = minor[10:11, 0:1]
    gate_b[0:1, 1:2] = minor[66:67, 0:1]


class Chain:
    def __init__(self, by, retain, linked, leaving, landed, sems, carried=None):
        self.dp, head = lax.axis_index("dp"), lax.axis_index("head")
        self.heads = lax.axis_size("head")
        self.ahead, self.behind = lax.rem(head + 1, self.heads), lax.rem(head + self.heads - 1, self.heads)
        self.place = head if by > 0 else self.heads - 1 - head
        self.to = (self.dp, self.ahead if by > 0 else self.behind)
        self.retain, self.linked, self.leaving, self.landed, self.sems = retain, linked, leaving, landed, sems
        self.carried = carried or range(self.heads)
        self.base = self.carried[0]

    def greet(self):
        greet([(self.dp, self.ahead), (self.dp, self.behind)])

    def copy(self, i):
        return remote(self.leaving.at[i - self.base], self.landed.at[i], self.sems, i, self.to)

    def pump(self, i):
        @pl.when(self.place != 0)
        def _():
            self.copy(i).wait_recv()
            entering = self.landed[i].astype(F32) * self.linked
            self.landed[i] = entering.astype(BF16)
            own = self.leaving[i - self.base].astype(F32)
            self.leaving[i - self.base] = (own + entering * self.retain[i, 0:1, 0:1]).astype(BF16)

        @pl.when(self.place == 0)
        def _():
            self.landed[i] = jnp.zeros(self.landed.shape[1:], BF16)

        @pl.when(self.place != self.heads - 1)
        def _():
            self.copy(i).start()

    def finish(self):
        @pl.when(self.place != self.heads - 1)
        def _():
            for i in self.carried:
                self.copy(i).wait_send()


def local(inputs, segment_ids, norm_gain, up_weight, conv_weight, conv_bias, qkv_weight,
          gate_weight, gate_bias, group_gain, skip_gain, down_weight, out_grad):
    H = lax.axis_size("head")
    n, d = inputs.shape
    dh = up_weight.shape[2]
    srows = dh + 16
    nch = n // CH
    log_scale = -0.5 * math.log(dh)

    small = (conv_weight, conv_bias.reshape(-1, 128), group_gain.reshape(-1, 128), skip_gain.reshape(-1, 128), gate_bias.T,
             qkv_weight.transpose(0, 2, 3, 1), gate_weight.transpose(0, 2, 1))
    w_all, pack, halo = gathered(up_weight, down_weight.T, small, inputs, H)
    gain = norm_gain.reshape(-1, 128)
    seg = segment_ids.reshape(-1, 128)

    def call(kernel, name, rounds, ins, outs, scratch, **kw):
        return pl.pallas_call(
            kernel, grid=(H * rounds,), out_shape=[o[0] for o in outs], in_specs=[i[1] for i in ins],
            out_specs=[o[1] for o in outs], scratch_shapes=scratch, compiler_params=params(**kw), name=name,
        )(*[i[0] for i in ins])

    sp = Specs(H, 1)
    per_head = sp.lead("both", *pack.shape[1:])
    cols_b = (sds((H, n, dh), BF16), sp.cols("both", n, dh))
    whole = lambda a: (a, sp.whole(*a.shape))
    q, k, va, pre, br, og, gates, normt, flags = call(
        partial(lift_kernel, H), "lift", 1,
        [whole(inputs), whole(halo), whole(gain), whole(seg), (pack, per_head), (w_all, sp.lead("both", d, 2 * dh))],
        [cols_b, cols_b, (sds((H, n, dh + 128), BF16), sp.lead("both", n, dh + 128)), cols_b,
         (sds((H, n + HALO, dh), BF16), sp.cols("both", n + HALO, dh)), cols_b,
         whole(sds((n, 128), F32)), whole(sds((d, n), BF16)), whole(sds((16, 128), F32))],
        [pltpu.VMEM((n + HALO, d), BF16), pltpu.VMEM((n + HALO, dh), F32), pltpu.VMEM((dh // 128, 384, 256), BF16),
         pltpu.VMEM((dh // 128, 384, 128), BF16), pltpu.VMEM((3, 128, dh), BF16)],
    )

    sp = Specs(H)
    sem = pltpu.SemaphoreType.DMA((H,))
    state = pltpu.VMEM((H, srows, dh), BF16)
    late = lambda a: (a, sp.cols("second", n, dh))
    first = H // 2
    output, gcol, grow, retain, dng, sttot, gloc, gend, gaug, ogg, dskip, sums, gin = call(
        partial(forward_kernel, H, log_scale), "forward", 2,
        [whole(inputs), whole(out_grad), whole(gates), whole(flags), late(q), (k, sp.cols("both", n, dh)),
         (va, sp.lead("both", n, dh + 128)), late(og), late(pre), (pack, sp.lead("second", *pack.shape[1:])),
         (w_all, sp.lead("second", d, dh, last=2))],
        [whole(sds((n, d), BF16)), whole(sds((n, 128), F32)), whole(sds((8, n), F32)), whole(sds((H, 8, 128), F32)),
         (sds((H, d, dh), BF16), sp.lead("second", d, dh)),
         (sds((H, nch, srows, dh), BF16), sp.lead("second", nch, srows, dh)),
         (sds((H, nch - 1, srows, dh), BF16), sp.lead("second", nch - 1, srows, dh)),
         (sds((H, srows, dh), BF16), sp.lead("second", srows, dh)),
         (sds((H, n, dh + 128), BF16), sp.lead("second", n, dh + 128)), late(sds((H, n, dh), BF16)),
         late(sds((H, n, dh), BF16)), (sds((H, 8, dh), F32), sp.lead("second", 8, dh)),
         whole(sds((first, srows, dh), BF16))],
        [pltpu.VMEM((n, d), F32), pltpu.VMEM((d, n), BF16), pltpu.VMEM((n, dh + 128), F32), pltpu.VMEM((n, dh), BF16),
         pltpu.VMEM((dh + 128, dh), BF16), pltpu.VMEM((dh, dh), F32), pltpu.VMEM((1, dh), F32),
         pltpu.VMEM((H, nch - 1, srows, dh), BF16), state, state, pltpu.VMEM((H, 8, 128), F32), sem, sem,
         pltpu.VMEM((first, srows, dh), BF16), pltpu.VMEM((first, srows, dh), BF16), pltpu.SemaphoreType.DMA((first,)),
         pltpu.SemaphoreType.DMA((first,))],
        collective_id=2, has_side_effects=True,
    )

    early = lambda a, *shape: (a, sp.lead("first", *shape))
    turn = lambda a, *shape: (a, sp.lead("turned", *shape))
    late = lambda a: (a, sp.cols("turned", *a.shape[1:]))
    rows = up_weight.shape[0]
    inside = by_hand(rows)
    anywhere = pl.BlockSpec(memory_space=pl.ANY)
    vmem = pltpu.VMEM
    ins = [whole(halo), whole(gain), whole(flags), whole(normt), whole(gates), whole(gcol), whole(grow), whole(retain),
           (gend, pl.BlockSpec((H - first, srows, dh), lambda s: (1, 0, 0), pipeline_mode=pl.Buffered(1))), whole(gin), (q, sp.cols("mixed", n, dh)), (k, sp.cols("mixed", n, dh)), (va, sp.lead("mixed", n, dh + 128)),
           early(gaug, n, dh + 128), early(sttot, nch, srows, dh), early(gloc, nch - 1, srows, dh),
           late(pre), late(br), late(ogg), late(dskip), turn(pack, *pack.shape[1:]), turn(w_all, d, 2 * dh),
           turn(sums, 8, dh)]
    sums_here = [sds((H, 72, dh), F32), sds((HALO, d), F32)]
    scratch = [vmem((H, n, dh), BF16), vmem((H, n, dh), BF16), vmem((H, n, dh), BF16), vmem((n, 128), BF16),
               vmem((8, 128), F32), vmem((dh + 128, dh), BF16), vmem((dh + 128, dh), BF16), vmem((n, 128), F32),
               vmem((128, n), F32), vmem((8, 128), F32), vmem((n + 2 * HALO, dh), F32), vmem((n, 2 * dh), BF16),
               vmem((n, dh), BF16), vmem((dh // 128, 128, 256), BF16), vmem((dh // 128, 128, 128), BF16),
               vmem((3, 128, dh), BF16), vmem((d, 128), F32), vmem((H - first, srows, dh), BF16), state, sem, sem]
    if inside:
        ins.append((dng, anywhere))
        outs = [sds((rows, 2 * dh), F32), sds((rows, dh), F32), sds((72, dh), F32), sds((HALO, d), F32), sds((n, d), F32)]
        small = lambda count: vmem((count, 72, dh), F32)
        dma = pltpu.SemaphoreType.DMA
        scratch += [vmem((d, 2 * dh), BF16), vmem((H, 72, dh), F32), vmem((HALO, d), F32), vmem((HALO, d), F32), small(2), small(3), small(2),
                    small(4), dma((2,)), dma((7,)), dma((7,)), *Scatter.scratch(d, rows, 2 * dh),
                    *Scatter.scratch(d, rows, dh)]
        outs = [whole(o) for o in outs]
    else:
        outs = [(sds((H, d, 2 * dh), BF16), sp.cols("turned", d, 2 * dh)), *(whole(o) for o in sums_here),
                whole(sds((n, d), F32))]
    made = call(partial(backward_kernel, inside, H, log_scale), "backward", 2, ins, outs, scratch,
                collective_id=3, has_side_effects=True)
    if inside:
        up_total, down_total, minor, corr, ng = made
    else:
        upg, minor, corr, ng = made

        def summed(part):
            part = lax.psum_scatter(part, "head", scatter_dimension=0, tiled=True)
            return lax.psum_scatter(part, "dp", scatter_dimension=1, tiled=True)[0].astype(F32)

        up_total, down_total = summed(upg), summed(dng)
        minor = lax.psum(lax.psum_scatter(minor, "head", scatter_dimension=0, tiled=True), "dp")[0]
        corr = shifted(corr, -1)

    once = lambda *shape: pl.BlockSpec(shape, lambda i: (0,) * len(shape))
    chunk = pl.BlockSpec((CH, d), lambda i: (i, 0))
    lines = (dh // 128, 128)
    shapes = [(rows, 2, dh), (rows, dh), (TAPS, dh), lines, (3, 4, 4, dh // 4), (3, 2 * H, dh), (1, 2), lines, lines,
              (d // 128, 128)]
    up, down, conv_w, conv_b, maps, gate_w, gate_b, group, skip, norm, ing, output = pl.pallas_call(
        partial(finish_kernel, H),
        grid=(n // CH,),
        out_shape=[*(sds(shape, F32) for shape in shapes), sds((n, d), F32), sds((n, d), BF16)],
        in_specs=[chunk, chunk, *(once(*a.shape) for a in (gain, up_total, down_total, minor, corr)), chunk, chunk],
        out_specs=[*(once(*shape) for shape in shapes), chunk, chunk],
        compiler_params=params(),
        name="finish",
    )(inputs, out_grad, gain, up_total, down_total, minor, corr, ng, output)
    return (output, ing, norm.reshape(d), up, conv_w, conv_b.reshape(dh), maps.transpose(0, 3, 1, 2),
            gate_w.transpose(0, 2, 1), gate_b.T, group.reshape(dh), skip.reshape(dh), down.T)


def solution(mesh):
    rows = P(("dp", "head"), None)
    small = (P(None, "head"), P("head"), P(None, "head", None, None), P(None, "head", None), P(None, "head"))
    return jax.shard_map(
        local,
        mesh=mesh,
        in_specs=(rows, P("dp"), P(), P("dp", None, "head"), *small, P("head"), P("head"), P("head", "dp"), rows),
        out_specs=(rows, rows, P(), P("dp", None, "head"), *small, P("head"), P("head"), P("head", "dp")),
        check_vma=False,
    )
```

```python
import math
from functools import partial

import jax
import jax.numpy as jnp
from jax import lax
from jax.experimental import pallas as pl
from jax.experimental.pallas import tpu as pltpu
from jax.sharding import PartitionSpec as P

EPS = 1e-05
NEG = -10000.0
CH = 256
HALO = 16
TAPS = 4
F32, BF16 = jnp.float32, jnp.bfloat16
HIGHEST = lax.Precision.HIGHEST


def nn(a, b, **kw):
    return lax.dot_general(a, b, (((1,), (0,)), ((), ())), preferred_element_type=F32, **kw)


def nt(a, b, **kw):
    return lax.dot_general(a, b, (((1,), (1,)), ((), ())), preferred_element_type=F32, **kw)


def tn(a, b, **kw):
    return lax.dot_general(a, b, (((0,), (0,)), ((), ())), preferred_element_type=F32, **kw)


def sigmoid(u):
    return 0.5 * jnp.tanh(0.5 * u) + 0.5


def log_sigmoid(u):
    return jnp.minimum(u, 0.0) - jnp.log(1.0 + jnp.exp(-jnp.abs(u)))


def iota(shape, dim):
    return lax.broadcasted_iota(jnp.int32, shape, dim)


def pick(block, lane):
    return jnp.sum(jnp.where(iota(block.shape, 1) == lane, block, 0.0), axis=1, keepdims=True)


def normalised(rows):
    centred = rows - jnp.mean(rows, axis=1, keepdims=True)
    inv_std = lax.rsqrt(jnp.mean(centred * centred, axis=1, keepdims=True) + EPS)
    return centred * inv_std, inv_std


def row_chunks(total, size):
    return [(r, min(size, total - r)) for r in range(0, total, size)]


def maps_of(pack_ref, cols, rest):
    rows = pack_ref[0, 8:24, cols]
    high = rows.astype(BF16)
    parts = [high]
    if rest:
        parts.append((rows - high.astype(F32)).astype(BF16))
    diagonal = iota((128, 128), 0) // 4 == iota((128, 128), 1) // 4
    made = []
    for part in parts:
        made.append([])
        for m in range(3):
            chosen = jnp.where(iota((16, 128), 0) == 4 * m + iota((16, 128), 1) % 4, 1.0, 0.0).astype(BF16)
            made[-1].append(jnp.where(diagonal, tn(part, chosen), 0.0).astype(BF16))
    return made


def gate_maps(pack_ref, into):
    for m in range(3):
        rows = pack_ref[0, 24 + 8 * m : 32 + 8 * m]
        into[m, 0:16] = jnp.concatenate([rows, jnp.zeros_like(rows)], axis=0).astype(BF16)


def lift_kernel(n_heads, x_ref, halo_ref, gain_ref, seg_ref, pack_ref, w_ref,
                q_ref, k_ref, va_ref, pre_ref, br_ref, og_ref, gates_ref, normt_ref, flags_ref,
                normed, ext, wqk, wv, gw):
    h = pl.program_id(0)
    n, dh = q_ref.shape
    me = lax.axis_index("head")

    @pl.when(h == 0)
    def _():
        gain = jnp.concatenate([gain_ref[j : j + 1] for j in range(gain_ref.shape[0])], axis=1)
        unit, _ = normalised(halo_ref[...].astype(F32))
        normed[0:HALO] = (unit * gain).astype(BF16)
        for r, rows in row_chunks(n, CH):
            unit, _ = normalised(x_ref[r : r + rows].astype(F32))
            scaled = unit * gain
            normed[HALO + r : HALO + r + rows] = scaled.astype(BF16)
            normt_ref[:, r : r + rows] = scaled.T.astype(BF16)
        gates_ref[...] = jnp.zeros_like(gates_ref)
        gw[...] = jnp.zeros_like(gw)
        token = iota(seg_ref.shape, 0) * 128 + iota(seg_ref.shape, 1)

        def segment(at):
            found = jnp.where(token == at, seg_ref[...], 0).astype(F32)
            return jnp.sum(jnp.sum(found, axis=1, keepdims=True), axis=0, keepdims=True)

        own = segment(me * n)
        before = jnp.where((segment(me * n - 1) == own) & (me > 0), 1.0, 0.0)
        after = jnp.where((segment(me * n + n) == own) & (me < n_heads - 1), 1.0, 0.0)
        flags_ref[0:8] = jnp.broadcast_to(before, (8, 128))
        flags_ref[8:16] = jnp.broadcast_to(after, (8, 128))

    gate_maps(pack_ref, gw)
    for b in range(dh // 128):
        (q_high, k_high, v_high), (q_rest, k_rest, v_rest) = maps_of(pack_ref, slice(128 * b, 128 * b + 128), True)
        for at, high, rest in ((0, q_high, q_rest), (128, k_high, k_rest)):
            wqk[b, 0:128, at : at + 128] = high
            wqk[b, 128:256, at : at + 128] = high
            wqk[b, 256:384, at : at + 128] = rest
        wv[b, 0:128] = v_high
        wv[b, 128:256] = v_high
        wv[b, 256:384] = v_rest
    lane = iota((1, 128), 1)
    bias = jnp.where(lane == h, pack_ref[0, 7:8, 0:1], 0.0) + jnp.where(lane == n_heads + h, pack_ref[0, 7:8, 1:2], 0.0)

    w = w_ref.at[0]
    halo = nn(normed[0:HALO], w[:, 0:dh]) * flags_ref[0:1, 0:1]
    ext[0:HALO] = halo
    br_ref[0:HALO] = halo.astype(BF16)
    for r, rows in row_chunks(n, 512):
        lifted = nn(normed[HALO + r : HALO + r + rows], w[...])
        branch = lifted[:, 0:dh]
        ext[HALO + r : HALO + r + rows] = branch
        og_ref[r : r + rows] = lifted[:, dh:].astype(BF16)
        branch_b = branch.astype(BF16)
        br_ref[HALO + r : HALO + r + rows] = branch_b
        pre = pack_ref[0, TAPS : TAPS + 1] + pack_ref[0, 0:1] * branch
        for j in range(1, TAPS):
            pre = pre + pack_ref[0, j : j + 1] * ext[HALO + r - j : HALO + r - j + rows]
        pre_ref[r : r + rows] = pre.astype(BF16)
        conv = pre * sigmoid(pre)
        conv_b = conv.astype(BF16)
        conv_rest = (conv - conv_b.astype(F32)).astype(BF16)
        branch_rest = (branch - branch_b.astype(F32)).astype(BF16)
        for b in range(dh // 128):
            cols = slice(128 * b, 128 * b + 128)
            parts = [conv_b[:, cols], conv_rest[:, cols], conv_b[:, cols]]
            qk = nn(jnp.concatenate(parts, axis=1), wqk[b]).astype(BF16)
            q_ref[r : r + rows, cols] = qk[:, 0:128]
            k_ref[r : r + rows, cols] = qk[:, 128:256]
            parts = [branch_b[:, cols], branch_rest[:, cols], branch_b[:, cols]]
            va_ref[0, r : r + rows, cols] = nn(jnp.concatenate(parts, axis=1), wv[b]).astype(BF16)
        va_ref[0, r : r + rows, dh : dh + 128] = jnp.where(
            iota((rows, 128), 1) == 0, 1.0, 0.0
        ).astype(BF16)
        gates_ref[r : r + rows] += (
            nt(q_ref[r : r + rows], gw[0])
            + nt(k_ref[r : r + rows], gw[1])
            + nt(va_ref[0, r : r + rows, 0:dh], gw[2])
            + bias
        )


def states(h, n_heads, gates_ref, k_ref, va_ref, gcol_ref, grow_ref, sloc, leaving, retain, st, ns):
    n, dh = k_ref.shape

    @pl.when(h == 0)
    def _():
        lower = jnp.where(iota((CH, CH), 0) >= iota((CH, CH), 1), 1.0, 0.0)
        for r, rows in row_chunks(n, CH):
            pre = gates_ref[r : r + rows]
            cum = nn(lower, log_sigmoid(pre), precision=HIGHEST)
            cum = pltpu.roll(cum, 128 - n_heads, 1)
            after = pltpu.roll(pre - cum, n_heads, 1)
            lane = iota((rows, 128), 1)
            both = jnp.where(lane < n_heads, cum, jnp.where(lane < 2 * n_heads, after, 0.0))
            gcol_ref[r : r + rows] = both
            grow_ref[:, r : r + rows] = both.T[0 : grow_ref.shape[0]]

    st[...] = jnp.zeros_like(st)
    ns[...] = jnp.zeros_like(ns)
    chunks = row_chunks(n, CH)
    whole_total = jnp.zeros((1, 1), F32)
    for c, (r, rows) in enumerate(chunks):
        block = gcol_ref[r : r + rows]
        total = pick(block[rows - 8 : rows], h)[7:8]
        whole_total = whole_total + total
        ending = jnp.exp(total + pick(block, n_heads + h))
        weighted = k_ref[r : r + rows].astype(F32) * ending
        st[...] = jnp.exp(total) * st[...] + tn(va_ref[0, r : r + rows, 0:dh], weighted.astype(BF16))
        ns[...] = jnp.exp(total) * ns[...] + jnp.sum(weighted, axis=0, keepdims=True)
        last = c == len(chunks) - 1
        to = leaving.at[h] if last else sloc.at[h, c]
        to[0:dh] = st[...].astype(BF16)
        to[dh : dh + 16] = jnp.where(iota((16, dh), 0) == 0, ns[0:1], 0.0).astype(BF16)
    retain[h] = jnp.broadcast_to(jnp.exp(whole_total), retain.shape[1:])


def decay_of(block, grow_ref, h, n_heads, r, rows, log_scale):
    cum = pick(block, h)
    after = grow_ref[pl.ds(n_heads + h, 1), r : r + rows]
    exponent = jnp.where(
        iota((rows, rows), 0) >= iota((rows, rows), 1), (cum + log_scale) + after, NEG
    )
    return jnp.exp(exponent), cum


def forward_kernel(n_heads, log_scale,
                   x_ref, og_all_ref, gates_ref, flags_ref, q_ref, k_ref, va_ref, gate_ref, pre_ref, pack_ref, w_ref,
                   out_ref, gcol_ref, grow_ref, retain_ref, dng_ref, sttot_ref, gloc_ref, gend_ref, gaug_ref, ogg_ref,
                   dskip_ref, sums_ref, gin_ref,
                   acc, ogt, numer, mixed_s, stb, gt, gn, sloc, leaving, landed, retain, ss, rs,
                   back_leaving, back_landed, back_ss, back_rs):
    step = pl.program_id(0)
    chain = Chain(1, retain, flags_ref[0:1, 0:1], leaving, landed, (ss, rs))
    place = chain.place
    early = range(back_landed.shape[0])
    back = Chain(-1, retain, flags_ref[8:9, 0:1], back_leaving, back_landed, (back_ss, back_rs), early)

    @pl.when(step == 0)
    def _():
        chain.signal()

    @pl.when(step < n_heads)
    def _():
        states(step, n_heads, gates_ref, k_ref, va_ref, gcol_ref, grow_ref, sloc, leaving, retain, gt, gn)

        @pl.when(step == 0)
        def _():
            pl.semaphore_wait(pltpu.get_barrier_semaphore(), 2)

        @pl.when(place == 0)
        def _():
            chain.pump(step)

        @pl.when((place == 1) & (step > 0))
        def _():
            chain.pump(step - 1)

    @pl.when(step >= n_heads)
    def _():
        h = step - n_heads

        @pl.when((place == 1) & (h == 0))
        def _():
            chain.pump(n_heads - 1)

        @pl.when((place > 1) & (h > 0) & (2 * h - 1 < n_heads))
        def _():
            chain.pump(2 * h - 1)

        for c, (r, rows) in enumerate(row_chunks(q_ref.shape[0], CH)):
            span = slice(r, r + rows)
            decay, _ = decay_of(gcol_ref[span], grow_ref, h, n_heads, r, rows, log_scale)
            weights = (nt(q_ref[span], k_ref[span]) * decay).astype(BF16)
            numer[span] = nn(weights, va_ref[0, span])

        @pl.when((place > 1) & (2 * h < n_heads))
        def _():
            chain.pump(2 * h)

        mix(h, n_heads, log_scale, x_ref, og_all_ref, gcol_ref, q_ref, sloc, landed, gate_ref, pre_ref, pack_ref, w_ref,
            out_ref, dng_ref, sttot_ref, gloc_ref, gend_ref, gaug_ref, ogg_ref, dskip_ref, sums_ref,
            acc, ogt, numer, mixed_s, stb, gt, gn)

        for i in early:

            @pl.when(h == i)
            def _():
                back_leaving[i] = gend_ref[0]

        for i in early:

            @pl.when(h == jnp.minimum(back.place + i, n_heads - 1))
            def _():
                back.pump(i)

    @pl.when(step == 2 * n_heads - 1)
    def _():
        retain_ref[...] = retain[...]
        gin_ref[...] = back_landed[...]
        chain.finish()
        back.finish()


def mix(h, n_heads, log_scale,
        x_ref, og_all_ref, gcol_ref, q_ref, sloc, landed, gate_ref, pre_ref, pack_ref, w_ref,
        out_ref, dng_ref, sttot_ref, gloc_ref, gend_ref, gaug_ref, ogg_ref, dskip_ref, sums_ref,
        acc, ogt, numer, mixed_s, stb, gt, gn):
    n, dh = q_ref.shape
    gain = pack_ref[0, TAPS + 1 : TAPS + 2]
    skip = pack_ref[0, TAPS + 2 : TAPS + 3]
    down_t = w_ref.at[0]

    @pl.when(h == 0)
    def _():
        acc[...] = jnp.zeros_like(acc)
        for r, rows in row_chunks(n, CH):
            ogt[:, r : r + rows] = og_all_ref[r : r + rows].astype(F32).T.astype(BF16)
        stb[dh + 16 :] = jnp.zeros((stb.shape[0] - dh - 16, dh), BF16)

    prefix = jnp.zeros((1, 1), F32)
    gain_sum = jnp.zeros((1, dh), F32)
    skip_sum = jnp.zeros((1, dh), F32)
    pair_sum = jnp.zeros((1, 1), F32)
    for c, (r, rows) in enumerate(row_chunks(n, CH)):
        span = slice(r, r + rows)
        block = gcol_ref[span]
        total = pick(block[rows - 8 : rows], h)[7:8]
        state = landed[h].astype(F32) * jnp.exp(prefix)
        if c > 0:
            state = state + sloc[h, c - 1].astype(F32)
        prefix = prefix + total
        state_b = state.astype(BF16)
        sttot_ref[0, c] = state_b
        stb[0 : dh + 16] = state_b
        factor = jnp.exp(pick(block, h) + log_scale)
        both = numer[span] + factor * nt(q_ref[span], stb[...])
        denom = both[:, dh : dh + 1]
        r_inv = lax.rsqrt(denom * denom + 1.0)
        unit, inv_std = normalised(both[:, 0:dh] * r_inv)
        gate = gate_ref[span].astype(F32)
        sg = sigmoid(gate)
        silu_gate = gate * sg
        pre = pre_ref[span].astype(F32)
        conv = pre * sigmoid(pre)
        inner = unit * gain + skip * conv
        mixed = (inner * silu_gate).astype(BF16)
        mixed_s[span] = mixed
        acc[span] += nt(mixed, down_t[...])
        mixed_grad = nn(og_all_ref[span], down_t[...])
        hskip = mixed_grad * silu_gate
        ogg_ref[span] = (mixed_grad * inner * (sg * (1.0 + gate * (1.0 - sg)))).astype(BF16)
        dskip_ref[span] = (hskip * skip).astype(BF16)
        skip_sum = skip_sum + jnp.sum(hskip * conv, axis=0, keepdims=True)
        gain_sum = gain_sum + jnp.sum(hskip * unit, axis=0, keepdims=True)
        dhh = hskip * gain
        along = jnp.mean(dhh * unit, axis=1, keepdims=True)
        grad = (inv_std * r_inv) * (dhh - jnp.mean(dhh, axis=1, keepdims=True) - unit * along)
        radial = dh * EPS * along * inv_std * inv_std
        gaug_ref[0, span, 0:dh] = grad.astype(BF16)
        gaug_ref[0, span, dh : dh + 128] = jnp.where(
            iota((rows, 128), 1) == 0, -radial * denom * r_inv * r_inv, 0.0
        ).astype(BF16)
        pair_sum = pair_sum + jnp.sum(radial * r_inv * r_inv, axis=0, keepdims=True)
    sums_ref[0, 0:1] = gain_sum
    sums_ref[0, 1:2] = skip_sum
    sums_ref[0, 2:3] = jnp.broadcast_to(pair_sum, (1, dh))
    sums_ref[0, 3:8] = jnp.zeros((5, dh), F32)

    @pl.when(h == n_heads - 1)
    def _():
        for r, rows in row_chunks(n, CH):
            out_ref[r : r + rows] = (x_ref[r : r + rows].astype(F32) + acc[r : r + rows]).astype(BF16)

    dng_ref[0] = nn(ogt[...], mixed_s[...]).astype(BF16)

    gt[...] = jnp.zeros_like(gt)
    gn[...] = jnp.zeros_like(gn)
    for c, (r, rows) in reversed(list(enumerate(row_chunks(n, CH)))):
        span = slice(r, r + rows)
        block = gcol_ref[span]
        cum = pick(block, h)
        keep = jnp.exp(pick(block[rows - 8 : rows], h)[7:8])
        weighted = q_ref[span].astype(F32) * jnp.exp(cum + log_scale)
        side = gaug_ref[0, span, dh : dh + 128].astype(F32)[:, 0:1]
        gt[...] = keep * gt[...] + tn(gaug_ref[0, span, 0:dh], weighted.astype(BF16))
        gn[...] = keep * gn[...] + jnp.sum(weighted * side, axis=0, keepdims=True)
        to = gloc_ref.at[0, c - 1] if c else gend_ref.at[0]
        to[0:dh] = gt[...].astype(BF16)
        to[dh : dh + 16] = jnp.where(iota((16, dh), 0) == 0, gn[0:1], 0.0).astype(BF16)


def memory_back(h, n_heads, log_scale, chain,
                gates_ref, gcol_ref, grow_ref, q_ref, k_ref, va_ref, gaug_ref, sttot_ref, gloc_ref,
                dq_s, dk_s, dv_s, pg_s, bsum, dk_near, dv_near, stb, gtb, cols, rowsb, across):
    n, dh = q_ref.shape
    chunks = row_chunks(n, CH)

    @pl.when(h == 0)
    def _():
        stb[dh + 16 :] = jnp.zeros((stb.shape[0] - dh - 16, dh), BF16)
        gtb[dh + 16 :] = jnp.zeros((gtb.shape[0] - dh - 16, dh), BF16)
        cols[...] = jnp.zeros_like(cols)
        rowsb[...] = jnp.zeros_like(rowsb)
        across[...] = jnp.zeros_like(across)

    for c, (r, rows) in enumerate(chunks):
        span = slice(r, r + rows)
        stb[0 : dh + 16] = sttot_ref[0, c]
        q, k, va, gaug = q_ref[span], k_ref[span], va_ref[0, span], gaug_ref[0, span]
        decay, cum = decay_of(gcol_ref[span], grow_ref, h, n_heads, r, rows, log_scale)
        weights = nt(q, k) * decay
        wg = nt(gaug, va)
        d_scores = (wg * decay).astype(BF16)
        pair = wg * weights
        dq_far = jnp.exp(cum + log_scale) * nn(gaug, stb[...])
        dq_s[h, span] = (nn(d_scores, k) + dq_far).astype(BF16)
        dk_near[span] = tn(d_scores, q)
        dv_near[span] = tn(weights.astype(BF16), gaug[:, 0:dh])
        row_sum = jnp.sum(pair, axis=1, keepdims=True) + jnp.sum(dq_far * q.astype(F32), axis=1, keepdims=True)
        cols[span] = jnp.where(iota((rows, 128), 1) == h, row_sum, cols[span])
        rowsb[pl.ds(h, 1), span] = jnp.sum(pair, axis=0, keepdims=True)

    @pl.when((chain.place == 1) & (h == 0))
    def _():
        for i in chain.carried:
            chain.pump(i)

    @pl.when((chain.place > 2) & (h >= chain.carried[0]))
    def _():
        chain.pump(h)

    suffix = jnp.zeros((1, 1), F32)
    for c, (r, rows) in reversed(list(enumerate(chunks))):
        span = slice(r, r + rows)
        block = gcol_ref[span]
        total = pick(block[rows - 8 : rows], h)[7:8]
        after_col = pick(block, n_heads + h)
        grad_state = chain.landed[h].astype(F32) * jnp.exp(suffix)
        if c < len(chunks) - 1:
            grad_state = grad_state + gloc_ref[0, c].astype(F32)
        suffix = suffix + total
        gtb[0 : dh + 16] = grad_state.astype(BF16)
        through = jnp.exp(total) * jnp.sum(
            jnp.sum(sttot_ref[0, c].astype(F32) * grad_state, axis=1, keepdims=True), axis=0, keepdims=True
        )
        k = k_ref[span]
        ending = jnp.exp(total + after_col)
        dk_far = ending * nn(va_ref[0, span], gtb[...])
        dk_s[h, span] = (dk_near[span] + dk_far).astype(BF16)
        dv_s[h, span] = (dv_near[span] + ending * nt(k, gtb[...])[:, 0:dh]).astype(BF16)
        col_far = jnp.sum(dk_far * k.astype(F32), axis=1, keepdims=True)
        cols[span] = jnp.where(iota((rows, 128), 1) == n_heads + h, col_far, cols[span])
        across[c : c + 1] = jnp.where(iota((1, 128), 1) == h, through, across[c : c + 1])

    @pl.when(h == n_heads - 1)
    def _():
        upper = jnp.where(iota((CH, CH), 0) <= iota((CH, CH), 1), 1.0, 0.0)
        strict = jnp.where(iota((CH, CH), 0) > iota((CH, CH), 1), 1.0, 0.0)
        lane = iota((CH, 128), 1)
        bias_sum = jnp.zeros((1, 128), F32)
        for c, (r, rows) in enumerate(chunks):
            span = slice(r, r + rows)
            near_col = rowsb[:, span].T
            far = pltpu.roll(cols[span], 128 - n_heads, 1)
            forget = (
                nn(upper, cols[span] - near_col, precision=HIGHEST)
                + nn(strict, far, precision=HIGHEST)
                + across[c : c + 1]
            )
            pre = gates_ref[span]
            forget = pltpu.roll(forget, n_heads, 1) * sigmoid(-pre)
            grads = jnp.where(
                lane < n_heads, near_col + far, jnp.where(lane < 2 * n_heads, forget, 0.0)
            )
            bias_sum = bias_sum + jnp.sum(grads, axis=0, keepdims=True)
            pg_s[span] = grads.astype(BF16)
        bsum[...] = jnp.where(iota((8, 128), 0) == 0, bias_sum, 0.0)


def lower(h, n_heads,
          halo_ref, gain_ref, flags_ref, normt_ref, pg_ref, bsum_ref, q_ref, k_ref, va_ref,
          dq_s, dk_s, dv_s, pre_ref, br_ref, ogg_ref, dskip_ref,
          pack_ref, w_ref, sums_ref,
          upg_ref, ng_ref, corr_ref, minor_ref,
          pext, lifted, conv_s, wqk, wv, gw, gacc, first, last):
    n, dh = q_ref.shape
    link = flags_ref[0:1, 0:1]
    w = w_ref.at[0]

    minor_out = minor_ref
    minor_ref = minor_out.at[pl.ds(h, 1)]
    minor_ref[0, 67:] = jnp.zeros((minor_ref.shape[1] - 67, dh), F32)

    @pl.when(first)
    def _():
        corr_ref[...] = jnp.zeros_like(corr_ref)
        ng_ref[...] = jnp.zeros_like(ng_ref)
        gacc[...] = jnp.zeros_like(gacc)
        pext[0:HALO] = jnp.zeros((HALO, dh), F32)
        pext[HALO + n :] = jnp.zeros((HALO, dh), F32)
        gw[...] = jnp.zeros_like(gw)

    gate_maps(pack_ref, gw)
    for b in range(dh // 128):
        [(q_high, k_high, v_high)] = maps_of(pack_ref, slice(128 * b, 128 * b + 128), False)
        wqk[b, :, 0:128] = q_high
        wqk[b, :, 128:256] = k_high
        wv[b] = v_high

    taps = [jnp.zeros((1, dh), F32) for _ in range(TAPS)]
    bias_sum = jnp.zeros((1, dh), F32)
    for r, rows in row_chunks(n, CH):
        span = slice(r, r + rows)
        pg = pg_ref[span]
        dqt = (dq_s[h, span].astype(F32) + nn(pg, gw[0])).astype(BF16)
        dkt = (dk_s[h, span].astype(F32) + nn(pg, gw[1])).astype(BF16)
        dvt = (dv_s[h, span].astype(F32) + nn(pg, gw[2])).astype(BF16)
        pre = pre_ref[span].astype(F32)
        sg = sigmoid(pre)
        conv_s[span] = (pre * sg).astype(BF16)
        slope = sg * (1.0 + pre * (1.0 - sg))
        dq_s[h, span] = dqt
        dk_s[h, span] = dkt
        dv_s[h, span] = dvt
        for b in range(dh // 128):
            at = slice(128 * b, 128 * b + 128)
            both = jnp.concatenate([dqt[:, at], dkt[:, at]], axis=1)
            conv_grad = nt(both, wqk[b]) + dskip_ref[span, at].astype(F32)
            pext[HALO + r : HALO + r + rows, at] = conv_grad * slope[:, at]
        pre_grad = pext[HALO + r : HALO + r + rows]
        bias_sum = bias_sum + jnp.sum(pre_grad, axis=0, keepdims=True)
        branch = br_ref[r : r + rows + HALO].astype(F32)
        for j in range(TAPS):
            taps[j] = taps[j] + jnp.sum(pre_grad * branch[HALO - j : HALO - j + rows], axis=0, keepdims=True)
    for j in range(TAPS):
        minor_ref[0, j : j + 1] = taps[j]
    minor_ref[0, TAPS : TAPS + 1] = bias_sum
    minor_ref[0, TAPS + 1 : 8] = jnp.zeros((8 - TAPS - 1, dh), F32)
    minor_ref[0, 8:16] = sums_ref[0]

    halo_grad = jnp.zeros((HALO, dh), F32)
    for j in range(1, TAPS):
        halo_grad = halo_grad + pack_ref[0, j : j + 1] * pext[j : HALO + j]
    halo_b = (halo_grad * link).astype(BF16)
    corr_ref[...] += nt(halo_b, w[:, 0:dh])
    for r, rows in row_chunks(n, CH):
        span = slice(r, r + rows)
        grad = jnp.zeros((rows, dh), F32)
        for j in range(TAPS):
            grad = grad + pack_ref[0, j : j + 1] * pext[HALO + r + j : HALO + r + j + rows]
        for b in range(dh // 128):
            at = slice(128 * b, 128 * b + 128)
            lifted[span, at] = (grad[:, at] + nt(dv_s[h, span, at], wv[b])).astype(BF16)
        lifted[span, dh : 2 * dh] = ogg_ref[span]
        ng_ref[span] += nt(lifted[span], w[...])

    unit_halo, _ = normalised(halo_ref[...].astype(F32))
    gain = jnp.concatenate([gain_ref[j : j + 1] for j in range(gain_ref.shape[0])], axis=1)
    normed_halo = (unit_halo * gain).astype(BF16)
    d = normt_ref.shape[0]
    for r, rows in row_chunks(d, d // 2):
        span = slice(r, r + rows)
        upg = nn(normt_ref[span], lifted[...])
        upg = jnp.concatenate([upg[:, 0:dh] + tn(normed_halo[:, span], halo_b), upg[:, dh:]], axis=1)
        upg_ref[span] = upg.astype(BF16)
        along = upg * w[span].astype(F32)
        part = along[:, 0:128]
        for at in range(128, 2 * dh, 128):
            part = part + along[:, at : at + 128]
        gacc[span] += part

    fold = jnp.where(iota((8, 128), 1) % 4 == iota((8, 128), 0), 1.0, 0.0)
    diagonal = iota((128, 128), 0) // 4 == iota((128, 128), 1) // 4
    for b in range(dh // 128):
        at = slice(128 * b, 128 * b + 128)
        qk_grad = tn(conv_s[:, at], jnp.concatenate([dq_s[h, :, at], dk_s[h, :, at]], axis=1))
        v_grad = tn(br_ref[HALO:, at], dv_s[h, :, at])
        for m, full in enumerate((qk_grad[:, 0:128], qk_grad[:, 128:256], v_grad)):
            minor_ref[0, 16 + 8 * m : 24 + 8 * m, at] = nt(fold, jnp.where(diagonal, full, 0.0), precision=HIGHEST)
    minor_ref[0, 40:48] = tn(pg_ref[...], q_ref[...])[0:8]
    minor_ref[0, 48:56] = tn(pg_ref[...], k_ref[...])[0:8]
    minor_ref[0, 56:64] = tn(pg_ref[...], va_ref[0, :, 0:dh])[0:8]

    @pl.when(last)
    def _():
        total = nt(jnp.ones((8, 128), F32), gacc[...], precision=HIGHEST)[0:1] / gain
        for i in range(n_heads):
            minor_out[i, 66:67] = jnp.broadcast_to(bsum_ref[0:1, n_heads + i : n_heads + i + 1], (1, dh))
            for j in range(d // dh):
                minor_out[i, 64 + j : 65 + j] = total[:, dh * j : dh * j + dh]


def backward_kernel(inside, n_heads, log_scale,
                    halo_ref, gain_ref, flags_ref, normt_ref, gates_ref, gcol_ref, grow_ref, retain_ref,
                    gend_ref, gin_ref, q_ref, k_ref, va_ref, gaug_ref, sttot_ref, gloc_ref, pre_ref, br_ref, ogg_ref,
                    dskip_ref, pack_ref, w_ref, sums_ref, *rest):
    if inside:
        dng, up_total, down_total, minor_total, corr_in, ng_ref, *rest = rest
    else:
        upg_ref, minor_ref, corr_ref, ng_ref, *rest = rest
    (dq_s, dk_s, dv_s, pg_s, bsum, stb, gtb, cols, rowsb, across, pext, lifted, conv_s, wqk, wv, gw, gacc,
     leaving, landed, ss, rs, *rest) = rest
    step = pl.program_id(0)
    done = gin_ref.shape[0]
    chain = Chain(-1, retain_ref, flags_ref[8:9, 0:1], leaving, landed, (ss, rs), range(done, n_heads))
    dh = q_ref.shape[1]
    near_k, near_v = ng_ref.at[:, 0:dh], ng_ref.at[:, dh : 2 * dh]
    if inside:
        here = Place()
        upg_ref, minor_ref, corr_ref, landing, m0, m1, n0, n1, load, ms, mr, *rest = rest
        many = len(rest) // 2
        up = Scatter(here, *rest[:many])
        down = Scatter(here, *rest[many:])

    @pl.when(step == 0)
    def _():
        if inside:
            greet([here.device(**to) for to in NEIGHBOURS])
        else:
            chain.greet()
        leaving[...] = gend_ref[...]
        landed[0:done] = gin_ref[...]

        @pl.when(chain.place == 0)
        def _():
            for i in chain.carried:
                chain.pump(i)

    @pl.when((step >= done) & (step < n_heads) & (chain.place == 2))
    def _():
        chain.pump(step)

    @pl.when(step < n_heads)
    def _():
        memory_back(step, n_heads, log_scale, chain, gates_ref, gcol_ref, grow_ref, q_ref, k_ref, va_ref, gaug_ref,
                    sttot_ref, gloc_ref, dq_s, dk_s, dv_s, pg_s, bsum, near_k, near_v, stb, gtb, cols, rowsb, across)

    if inside:

        @pl.when(step == n_heads + 1)
        def _():
            up.given(1)

        @pl.when(step == n_heads + 3)
        def _():
            up.given(0)

    @pl.when(step >= n_heads)
    def _():
        i = step - n_heads
        lower(turned(i), n_heads, halo_ref, gain_ref, flags_ref, normt_ref, pg_s, bsum, q_ref,
              k_ref, va_ref, dq_s, dk_s, dv_s, pre_ref, br_ref, ogg_ref, dskip_ref, pack_ref, w_ref, sums_ref,
              upg_ref, ng_ref, corr_ref, minor_ref, pext, lifted, conv_s, wqk, wv, gw, gacc, i == 0, i == n_heads - 1)

    if inside:
        loads = [pltpu.make_async_copy(dng.at[here.head(fx, 0)], down.own.at[fx], load.at[fx]) for fx in (0, 1)]

        def at_end_of(number):
            return pl.when(step == number)

        @at_end_of(1)
        def _():
            for fx in (1, 0):
                loads[fx].start()
                down.give(dng.at[here.head(fx, 1)], fx)

        @at_end_of(2)
        def _():
            for fx in (1, 0):
                loads[fx].wait()
                for k in ORDER:
                    down.first(fx, k)

        @at_end_of(3)
        def _():
            for k in ORDER:
                down.away(k)

        @at_end_of(4)
        def _():
            up.give(upg_ref, 1)
            for k in ORDER:
                down.home(k)

        @at_end_of(5)
        def _():
            up.own[1] = upg_ref[...]
            for k in ORDER:
                up.first(1, k)
            for k in ORDER:
                down.third(k)

        @at_end_of(6)
        def _():
            up.give(upg_ref, 0)
            for k in ORDER:
                up.away(k)
            down.final(down_total)

        @at_end_of(7)
        def _():
            up.own[0] = upg_ref[...]
            before = (here.z * 2 + here.y, lax.rem(here.head() + 3, 4))
            sent = [remote(corr_ref, landing, (ms, mr), 6, before)]
            sent[0].start()

            def send(src, dst, at, to):
                copy = remote(src, dst, (ms, mr), at, here.device(**to))
                copy.start()
                sent.append(copy)

            def arrived(dst, at):
                remote(dst, dst, (ms, mr), at, here.device(fc=1)).wait_recv()

            for fx in (0, 1):
                send(minor_ref.at[here.head(fx, 1)], n0.at[fx], fx, dict(fc=1))
            up.first(0, 1)
            up.first(0, 2)
            for fx in (1, 0):
                arrived(n0.at[fx], fx)
                m0[fx] = minor_ref[here.head(fx, 0)] + n0[fx]
            send(m0.at[1], n1.at[0], 2, dict(fx=1))
            up.home(1)
            up.first(0, 3)
            up.first(0, 0)
            up.home(2)
            arrived(n1.at[0], 2)
            m1[0] = m0[0] + n1[0]
            send(m1.at[0], n1.at[1], 3, dict(fy=1))
            up.third(1)
            up.home(3)
            up.third(2)
            arrived(n1.at[1], 3)
            m1[1] = m1[0] + n1[1]
            send(m1.at[1], n1.at[2], 4, dict(k=1))
            up.home(0)
            up.third(3)
            arrived(n1.at[2], 4)
            m1[2] = m1[1] + n1[2]
            send(m1.at[2], n1.at[3], 5, dict(k=2))
            up.third(0)
            up.final(up_total)
            arrived(n1.at[3], 5)
            minor_total[...] = m1[2] + n1[3]
            arrived(landing, 6)
            corr_in[...] = landing[...]
            for copy in sent:
                copy.wait_send()
            down.given(1)
            down.given(0)
            up.finish()
            down.finish()

    @pl.when(step == 2 * n_heads - 1)
    def _():
        chain.finish()


ORDER = (1, 2, 3, 0)


class Scatter:
    SEMAPHORES = ((2, 4), (2, 4), (2, 2, 4), (2, 2, 4), (2, 4), (2, 4), (2, 3), (2, 3))

    @staticmethod
    def scratch(d, rows, cols):
        half = rows // 2
        sem = pltpu.SemaphoreType.DMA
        return [pltpu.VMEM((2, d, cols), BF16), pltpu.VMEM((2, d, cols), BF16), pltpu.VMEM((2, 4, half, cols), BF16),
                pltpu.VMEM((2, 4, half, cols), BF16), pltpu.VMEM((2, 4, half, cols), BF16),
                pltpu.VMEM((2, 3, half, cols), BF16), *(sem(shape) for shape in Scatter.SEMAPHORES)]

    def __init__(self, here, own, r0, r1a, r1b, r2, r3, *sems):
        self.here, self.own, self.r0, self.r1a, self.r1b, self.r2, self.r3 = here, own, r0, r1a, r1b, r2, r3
        self.s0, self.s1, self.s2, self.s3 = (tuple(sems[i : i + 2]) for i in (0, 2, 4, 6))
        self.half = r3.shape[2]

    def piece(self, fx, k, fy, p):
        return self.own.at[fx, pl.ds(self.here.rows(k, fy, 2 * self.half) + self.half * p, self.half)]

    def pair(self, k):
        return pl.ds(pl.multiple_of(self.here.along_z(k) * 4 * self.half, 16), 4 * self.half)

    def send(self, src, dst, sems, at, to):
        remote(src, dst, sems, at, self.here.device(**to)).start()

    def arrived(self, dst, sems, at):
        remote(dst, dst, sems, at, self.here.device(fc=1)).wait_recv()

    def sent(self, src, sems, at):
        remote(src, src, sems, at, self.here.device(fc=1)).wait_send()

    def add(self, into, other):
        into[...] = (into[...].astype(F32) + other[...].astype(F32)).astype(BF16)

    def give(self, src, fx):
        for k in ORDER:
            self.send(src.at[self.pair(k)], self.r0.at[fx, self.pair(k)], self.s0, (fx, k), dict(fc=1))

    def given(self, fx):
        for k in range(4):
            self.sent(self.r0.at[fx, self.pair(k)], self.s0, (fx, k))

    def first(self, fx, k):
        self.arrived(self.r0.at[fx, self.pair(k)], self.s0, (fx, k))
        self.add(self.own.at[fx, self.pair(k)], self.r0.at[fx, self.pair(k)])
        self.send(self.piece(fx, k, 1, 0), self.r1a.at[fx, k], self.s1, (0, fx, k), dict(fy=1))
        if fx:
            for fy in (1, 0):
                self.send(self.piece(1, k, fy, 1), self.r1b.at[fy, k], self.s1, (1, fy, k), dict(fx=1))

    def away(self, k):
        self.arrived(self.r1a.at[1, k], self.s1, (0, 1, k))
        self.add(self.piece(1, k, 0, 0), self.r1a.at[1, k])
        self.send(self.piece(1, k, 0, 0), self.r2.at[0, k], self.s2, (0, k), dict(fx=1))

    def home(self, k):
        self.arrived(self.r1a.at[0, k], self.s1, (0, 0, k))
        self.add(self.piece(0, k, 0, 0), self.r1a.at[0, k])
        for f in (1, 0):
            self.arrived(self.r1b.at[f, k], self.s1, (1, f, k))
            self.add(self.piece(0, k, f, 1), self.r1b.at[f, k])
            if f:
                self.send(self.piece(0, k, 1, 1), self.r2.at[1, k], self.s2, (1, k), dict(fy=1))

    def third(self, k):
        for p in (0, 1):
            self.arrived(self.r2.at[p, k], self.s2, (p, k))
            self.add(self.piece(0, k, 0, p), self.r2.at[p, k])
            if k:
                self.send(self.piece(0, k, 0, p), self.r3.at[p, k - 1], self.s3, (p, k - 1), dict(k=k))

    def final(self, total):
        for p in (0, 1):
            summed = self.piece(0, 0, 0, p)[...].astype(F32)
            for k in range(3):
                self.arrived(self.r3.at[p, k], self.s3, (p, k))
                summed = summed + self.r3[p, k].astype(F32)
            total[self.half * p : self.half * p + self.half] = summed

    def finish(self):
        for k in range(4):
            for f in (0, 1):
                self.sent(self.r1a.at[f, k], self.s1, (0, f, k))
                self.sent(self.r1b.at[f, k], self.s1, (1, f, k))
                self.sent(self.r2.at[f, k], self.s2, (f, k))
                if k < 3:
                    self.sent(self.r3.at[f, k], self.s3, (f, k))


def turned(i):
    head = lax.axis_index("head")
    x, c = lax.div(head, 2), lax.rem(head, 2)
    fx, fc = 1 - lax.div(i, 2), 1 - lax.rem(i, 2)
    return (x + fx - 2 * x * fx) * 2 + (c + fc - 2 * c * fc)


class Specs:
    def __init__(self, heads, rounds=2):
        self.heads, self.steps = heads, heads * rounds
        self.index = dict(
            both=lambda s: lax.rem(s, heads),
            first=lambda s: jnp.minimum(s, heads - 1),
            second=lambda s: jnp.maximum(s - heads, 0),
            turned=lambda s: turned(jnp.maximum(s - heads, 0)),
            mixed=lambda s: jnp.where(s < heads, s, turned(jnp.maximum(s - heads, 0))),
        )

    def whole(self, *shape):
        return pl.BlockSpec(shape, lambda s: (0,) * len(shape), pipeline_mode=pl.Buffered(1))

    def cols(self, when, rows, cols):
        index = self.index[when]
        return pl.BlockSpec((None, rows, cols), lambda s: (index(s), 0, 0))

    def lead(self, when, *shape, last=0):
        index = self.index[when]
        return pl.BlockSpec((1, *shape), lambda s: (index(s),) + (0,) * (len(shape) - 1) + (last,))


def params(**kw):
    return pltpu.CompilerParams(dimension_semantics=("arbitrary",), vmem_limit_bytes=62 << 20, **kw)


def sds(shape, dtype):
    return jax.ShapeDtypeStruct(shape, dtype)


def shifted(x, by):
    heads = lax.axis_size("head")
    pairs = [(i, i + by) for i in range(heads) if 0 <= i + by < heads]
    return lax.ppermute(x, "head", pairs)


MESH = pl.DeviceIdType.MESH


class Place:
    def __init__(self):
        dp, head = lax.axis_index("dp"), lax.axis_index("head")
        self.z, self.y = lax.div(dp, 2), lax.rem(dp, 2)
        self.x, self.c = lax.div(head, 2), lax.rem(head, 2)

    def along_z(self, k):
        z = self.z
        return (z, z + 1 - 2 * lax.rem(z, 2), lax.rem(z + 2, 4), 3 - z)[k]

    def device(self, k=0, fy=0, fx=0, fc=0):
        y, x, c = (1 - v if f else v for v, f in ((self.y, fy), (self.x, fx), (self.c, fc)))
        return (self.along_z(k) * 2 + y, x * 2 + c)

    def head(self, fx=0, fc=0):
        return (1 - self.x if fx else self.x) * 2 + (1 - self.c if fc else self.c)

    def rows(self, k, fy, size):
        y = 1 - self.y if fy else self.y
        return pl.multiple_of((self.along_z(k) * 2 + y) * size, 16)


NEIGHBOURS = (dict(fc=1), dict(fx=1), dict(fx=1, fc=1), dict(fy=1), dict(k=1), dict(k=2), dict(k=3))


def greet(devices, meanwhile=None):
    barrier = pltpu.get_barrier_semaphore()
    for device in devices:
        pl.semaphore_signal(barrier, inc=1, device_id=device, device_id_type=MESH)
    if meanwhile:
        meanwhile()
    pl.semaphore_wait(barrier, len(devices))


def remote(src, dst, sems, at, device):
    send, recv = sems
    return pltpu.make_async_remote_copy(
        src_ref=src, dst_ref=dst, send_sem=send.at[at], recv_sem=recv.at[at], device_id=device, device_id_type=MESH
    )


class Gather:
    SEMAPHORES = ((2, 3), (2, 3), (2, 4), (2, 4), (2, 4, 2), (2, 4, 2), (2, 4, 4), (2, 4, 4))
    FLIPS = ((dict(fx=1), dict(fy=1)), (dict(fy=1), dict(fx=1)))

    def __init__(self, here, shard, w, sems):
        self.here, self.shard, self.w = here, shard, w
        self.z, self.f, self.s, self.d = (tuple(sems[i : i + 2]) for i in (0, 2, 4, 6))
        self.rows = shard.shape[0]
        self.started = []

    def block(self, p, k=0, fy=0, fx=0, fc=0):
        half = self.rows // 2
        return self.w.at[self.here.head(fx, fc), pl.ds(self.here.rows(k, fy, self.rows) + half * p, half)]

    def send(self, src, dst, sems, at, to):
        copy = remote(src, dst, sems, at, self.here.device(**to))
        copy.start()
        self.started.append(copy)

    def arrived(self, dst, sems, at):
        remote(dst, dst, sems, at, self.here.device(fc=1)).wait_recv()

    def begin(self):
        half = self.rows // 2
        for p in (0, 1):
            mine = self.shard.at[pl.ds(half * p, half)]
            first, second = self.FLIPS[p]
            self.send(mine, self.block(p), self.z, (p, 0), dict(k=1))
            self.send(mine, self.block(p), self.f, (p, 0), first)
        for p in (0, 1):
            mine = self.shard.at[pl.ds(half * p, half)]
            first, second = self.FLIPS[p]
            for k in (2, 3):
                self.send(mine, self.block(p), self.z, (p, k - 1), dict(k=k))
            self.send(mine, self.block(p), self.s, (p, 0, 0), second)
            self.send(mine, self.block(p), self.d, (p, 0, 0), dict(fc=1))

    def from_z(self, k):
        for p in (0, 1):
            first, second = self.FLIPS[p]
            block = self.block(p, k)
            self.arrived(block, self.z, (p, k - 1))
            self.send(block, block, self.f, (p, k), first)
            self.send(block, block, self.s, (p, k, 0), second)
            self.send(block, block, self.d, (p, k, 0), dict(fc=1))

    def from_first(self, k):
        for p in (0, 1):
            first, second = self.FLIPS[p]
            block = self.block(p, k, **first)
            self.arrived(block, self.f, (p, k))
            self.send(block, block, self.s, (p, k, 1), second)
            self.send(block, block, self.d, (p, k, 1), dict(fc=1))

    def from_second(self, k):
        for i in (0, 1):
            for p in (0, 1):
                first, second = self.FLIPS[p]
                block = self.block(p, k, **(dict(**first, **second) if i else second))
                self.arrived(block, self.s, (p, k, i))
                self.send(block, block, self.d, (p, k, 2 + i), dict(fc=1))

    def from_core(self, k):
        for p in (0, 1):
            first, second = self.FLIPS[p]
            for i, over in enumerate((dict(), first, second, dict(**first, **second))):
                self.arrived(self.block(p, k, fc=1, **over), self.d, (p, k, i))

    def run(self):
        self.from_first(0)
        for k in (1, 2, 3):
            self.from_z(k)
            self.from_second(k - 1)
            self.from_first(k)
        self.from_second(3)
        for k in range(4):
            self.from_core(k)
        for copy in self.started:
            copy.wait_send()


def gather_kernel(up_raw, down, taps, conv_bias, group, skip, gate_bias, maps, gates, x, w, pack_all, halo,
                  shard, pack, rows_s, local_sem, ms, mr, *sems):
    here = Place()
    n = x.shape[0]
    dh = pack.shape[1]
    rows = shard.shape[0]

    def assemble():
        shard[:, 0:dh] = up_raw[:, 0]
        shard[:, dh : 2 * dh] = up_raw[:, 1]
        shard[:, 2 * dh :] = down[...]

    greet([here.device(**to) for to in NEIGHBOURS], assemble)
    weights = Gather(here, shard, w, sems)
    weights.begin()
    fill_pack(taps, conv_bias, group, skip, gate_bias, maps, gates, pack, rows_s)
    copies = [pltpu.make_async_copy(pack, pack_all.at[here.head()], local_sem.at[0]),
              pltpu.make_async_copy(shard, w.at[here.head(), pl.ds(here.rows(0, 0, rows), rows)], local_sem.at[1])]
    for copy in copies:
        copy.start()
    small = []
    for i, to in enumerate(NEIGHBOURS[:3]):
        small.append(remote(pack, pack_all.at[here.head()], (ms, mr), i, here.device(**to)))
    after = (here.z * 2 + here.y, lax.rem(here.head() + 1, 4))
    small.append(remote(x.at[pl.ds(n - HALO, HALO)], halo, (ms, mr), 3, after))
    for copy in small:
        copy.start()
    weights.run()
    for i, to in enumerate(NEIGHBOURS[:3]):
        from_them = pack_all.at[here.head(to.get("fx", 0), to.get("fc", 0))]
        remote(from_them, from_them, (ms, mr), i, here.device(fc=1)).wait_recv()
    remote(halo, halo, (ms, mr), 3, here.device(fc=1)).wait_recv()
    for copy in small:
        copy.wait_send()
    for copy in copies:
        copy.wait()


def fill_pack(taps, conv_bias, group, skip, gate_bias, maps, gates, pack, rows_s):
    dh = pack.shape[1]
    pack[0:TAPS] = taps[...]
    for i, ref in enumerate((conv_bias, group, skip)):
        for j in range(dh // 128):
            pack[TAPS + i : TAPS + i + 1, 128 * j : 128 * j + 128] = ref[j : j + 1]
    lane = iota((1, dh), 1)
    pack[7:8] = jnp.where(lane == 0, gate_bias[0:1, 0:1], jnp.where(lane == 1, gate_bias[0:1, 1:2], 0.0))
    rows_s[...] = jnp.zeros_like(rows_s)
    for m in range(3):
        for i in range(4):
            rows_s[16 * m + 4 * i : 16 * m + 4 * i + 4, 0 : dh // 4] = maps[m, i]
        pack[24 + 8 * m : 32 + 8 * m] = gates[m].astype(F32)
    wide = nn(rows_s[...], jnp.where(iota((128, dh), 1) // 4 == iota((128, dh), 0), 1.0, 0.0), precision=HIGHEST)
    for m in range(3):
        rows = jnp.zeros((4, dh), F32)
        for i in range(4):
            rows = jnp.where(iota((4, dh), 1) % 4 == i, wide[16 * m + 4 * i : 16 * m + 4 * i + 4], rows)
        pack[8 + 4 * m : 12 + 4 * m] = rows
    pack[20:24] = jnp.zeros((4, dh), F32)


def gathered(up_weight, down, small, x, heads):
    dp = lax.axis_size("dp")
    n, d = x.shape
    vmem = pl.BlockSpec(memory_space=pltpu.VMEM)
    rows, _, dh = up_weight.shape
    if not by_hand(rows):
        up = up_weight.reshape(rows, 2 * dh)
        pack = pl.pallas_call(
            fill_pack, out_shape=sds((48, dh), F32), in_specs=[vmem] * 7, out_specs=vmem,
            scratch_shapes=[pltpu.VMEM((48, 128), F32)], name="pack",
        )(*small)

        def all_of(shard):
            w = lax.all_gather(shard, ("dp", "head"), axis=0)
            w = w.reshape(dp, heads, *shard.shape).transpose(1, 0, 2, 3)
            return w.reshape(heads, dp * shard.shape[0], shard.shape[1])

        w = all_of(jnp.concatenate([up, down], axis=1))
        return w, lax.all_gather(pack, "head", axis=0), shifted(x[n - HALO :], 1)
    sem = pltpu.SemaphoreType.DMA
    anywhere = pl.BlockSpec(memory_space=pl.ANY)
    return pl.pallas_call(
        gather_kernel,
        out_shape=[sds((heads, dp * rows, 3 * dh), BF16), sds((heads, 48, dh), F32), sds((HALO, d), BF16)],
        in_specs=[vmem, vmem, *[vmem] * 7, anywhere],
        out_specs=[anywhere] * 3,
        scratch_shapes=[pltpu.VMEM((rows, 3 * dh), BF16), pltpu.VMEM((48, dh), F32), pltpu.VMEM((48, 128), F32),
                        sem((2,)), sem((4,)), sem((4,)), *(sem(shape) for shape in Gather.SEMAPHORES)],
        compiler_params=pltpu.CompilerParams(collective_id=0, has_side_effects=True),
        name="gather",
    )(up_weight, down, *small, x)


def by_hand(rows):
    return lax.axis_size("dp") == 8 and lax.axis_size("head") == 4 and rows % 32 == 0


def finish_kernel(n_heads, x, og, norm_gain, up_total, down_total, minor, corr, ng, output,
                  up, down, conv_w, conv_b, maps, gate_w, gate_b, group, skip, gain, ing, out):
    step = pl.program_id(0)
    rows = x.shape[0]
    out[...] = output[...]
    unit, inv_std = normalised(x[...].astype(F32))
    follows = jnp.where((lax.axis_index("head") < n_heads - 1) & (step == pl.num_programs(0) - 1), 1.0, 0.0)
    grads = ng[...] + jnp.concatenate([jnp.zeros((rows - HALO, x.shape[1]), F32), corr[...] * follows], axis=0)
    scaled = grads * jnp.concatenate([norm_gain[j : j + 1] for j in range(norm_gain.shape[0])], axis=1)
    ing[...] = og[...].astype(F32) + inv_std * (
        scaled - jnp.mean(scaled, axis=1, keepdims=True) - unit * jnp.mean(scaled * unit, axis=1, keepdims=True)
    )

    @pl.when(step == 0)
    def _():
        finish_small(up_total, down_total, minor, up, down, conv_w, conv_b, maps, gate_w, gate_b, group, skip, gain)


def finish_small(up_total, down_total, minor, up, down, conv_w, conv_b, maps, gate_w, gate_b, group, skip, gain):
    dh = minor.shape[1]
    up[:, 0] = up_total[:, 0:dh]
    up[:, 1] = up_total[:, dh : 2 * dh]
    down[...] = down_total[...]
    conv_w[...] = minor[0:TAPS]
    for j in range(dh // 128):
        at = slice(128 * j, 128 * j + 128)
        for ref, row in ((conv_b, TAPS), (group, 8), (skip, 9)):
            ref[j : j + 1] = minor[row : row + 1, at]
        for i in range(gain.shape[0] * 128 // dh):
            gain[dh // 128 * i + j : dh // 128 * i + j + 1] = minor[64 + i : 65 + i, at]
    for m in range(3):
        gate_w[m] = minor[40 + 8 * m : 48 + 8 * m]
    for i in range(4):
        chosen = jnp.where(iota((dh, 128), 0) == 4 * iota((dh, 128), 1) + i, 1.0, 0.0)
        rows = nn(minor[16:40], chosen, precision=HIGHEST)
        for m in range(3):
            maps[m, i] = rows[8 * m : 8 * m + 4, 0 : dh // 4]
    gate_b[0:1, 0:1] = minor[10:11, 0:1]
    gate_b[0:1, 1:2] = minor[66:67, 0:1]


class Chain:
    def __init__(self, by, retain, linked, leaving, landed, sems, carried=None):
        self.dp, head = lax.axis_index("dp"), lax.axis_index("head")
        self.heads = lax.axis_size("head")
        self.ahead, self.behind = lax.rem(head + 1, self.heads), lax.rem(head + self.heads - 1, self.heads)
        self.place = head if by > 0 else self.heads - 1 - head
        self.to = (self.dp, self.ahead if by > 0 else self.behind)
        self.retain, self.linked, self.leaving, self.landed, self.sems = retain, linked, leaving, landed, sems
        self.carried = carried or range(self.heads)
        self.base = self.carried[0]

    def greet(self):
        self.signal()
        pl.semaphore_wait(pltpu.get_barrier_semaphore(), 2)

    def signal(self):
        for head in (self.ahead, self.behind):
            pl.semaphore_signal(pltpu.get_barrier_semaphore(), inc=1, device_id=(self.dp, head), device_id_type=MESH)

    def copy(self, i):
        return remote(self.leaving.at[i - self.base], self.landed.at[i], self.sems, i, self.to)

    def pump(self, i):
        @pl.when(self.place != 0)
        def _():
            self.copy(i).wait_recv()
            entering = self.landed[i].astype(F32) * self.linked
            self.landed[i] = entering.astype(BF16)
            own = self.leaving[i - self.base].astype(F32)
            self.leaving[i - self.base] = (own + entering * self.retain[i, 0:1, 0:1]).astype(BF16)

        @pl.when(self.place == 0)
        def _():
            self.landed[i] = jnp.zeros(self.landed.shape[1:], BF16)

        @pl.when(self.place != self.heads - 1)
        def _():
            self.copy(i).start()

    def finish(self):
        @pl.when(self.place != self.heads - 1)
        def _():
            for i in self.carried:
                self.copy(i).wait_send()


def local(inputs, segment_ids, norm_gain, up_weight, conv_weight, conv_bias, qkv_weight,
          gate_weight, gate_bias, group_gain, skip_gain, down_weight, out_grad):
    H = lax.axis_size("head")
    n, d = inputs.shape
    dh = up_weight.shape[2]
    srows = dh + 16
    nch = n // CH
    log_scale = -0.5 * math.log(dh)

    small = (conv_weight, conv_bias.reshape(-1, 128), group_gain.reshape(-1, 128), skip_gain.reshape(-1, 128), gate_bias.T,
             qkv_weight.transpose(0, 2, 3, 1), gate_weight.transpose(0, 2, 1))
    w_all, pack, halo = gathered(up_weight, down_weight.T, small, inputs, H)
    gain = norm_gain.reshape(-1, 128)
    seg = segment_ids.reshape(-1, 128)

    def call(kernel, name, rounds, ins, outs, scratch, **kw):
        return pl.pallas_call(
            kernel, grid=(H * rounds,), out_shape=[o[0] for o in outs], in_specs=[i[1] for i in ins],
            out_specs=[o[1] for o in outs], scratch_shapes=scratch, compiler_params=params(**kw), name=name,
        )(*[i[0] for i in ins])

    sp = Specs(H, 1)
    per_head = sp.lead("both", *pack.shape[1:])
    cols_b = (sds((H, n, dh), BF16), sp.cols("both", n, dh))
    whole = lambda a: (a, sp.whole(*a.shape))
    q, k, va, pre, br, og, gates, normt, flags = call(
        partial(lift_kernel, H), "lift", 1,
        [whole(inputs), whole(halo), whole(gain), whole(seg), (pack, per_head), (w_all, sp.lead("both", d, 2 * dh))],
        [cols_b, cols_b, (sds((H, n, dh + 128), BF16), sp.lead("both", n, dh + 128)), cols_b,
         (sds((H, n + HALO, dh), BF16), sp.cols("both", n + HALO, dh)), cols_b,
         whole(sds((n, 128), F32)), whole(sds((d, n), BF16)), whole(sds((16, 128), F32))],
        [pltpu.VMEM((n + HALO, d), BF16), pltpu.VMEM((n + HALO, dh), F32), pltpu.VMEM((dh // 128, 384, 256), BF16),
         pltpu.VMEM((dh // 128, 384, 128), BF16), pltpu.VMEM((3, 128, dh), BF16)],
    )

    sp = Specs(H)
    sem = pltpu.SemaphoreType.DMA((H,))
    state = pltpu.VMEM((H, srows, dh), BF16)
    late = lambda a: (a, sp.cols("second", n, dh))
    first = H // 2
    output, gcol, grow, retain, dng, sttot, gloc, gend, gaug, ogg, dskip, sums, gin = call(
        partial(forward_kernel, H, log_scale), "forward", 2,
        [whole(inputs), whole(out_grad), whole(gates), whole(flags), late(q), (k, sp.cols("both", n, dh)),
         (va, sp.lead("both", n, dh + 128)), late(og), late(pre), (pack, sp.lead("second", *pack.shape[1:])),
         (w_all, sp.lead("second", d, dh, last=2))],
        [whole(sds((n, d), BF16)), whole(sds((n, 128), F32)), whole(sds((8, n), F32)), whole(sds((H, 8, 128), F32)),
         (sds((H, d, dh), BF16), sp.lead("second", d, dh)),
         (sds((H, nch, srows, dh), BF16), sp.lead("second", nch, srows, dh)),
         (sds((H, nch - 1, srows, dh), BF16), sp.lead("second", nch - 1, srows, dh)),
         (sds((H, srows, dh), BF16), sp.lead("second", srows, dh)),
         (sds((H, n, dh + 128), BF16), sp.lead("second", n, dh + 128)), late(sds((H, n, dh), BF16)),
         late(sds((H, n, dh), BF16)), (sds((H, 8, dh), F32), sp.lead("second", 8, dh)),
         whole(sds((first, srows, dh), BF16))],
        [pltpu.VMEM((n, d), F32), pltpu.VMEM((d, n), BF16), pltpu.VMEM((n, dh + 128), F32), pltpu.VMEM((n, dh), BF16),
         pltpu.VMEM((dh + 128, dh), BF16), pltpu.VMEM((dh, dh), F32), pltpu.VMEM((1, dh), F32),
         pltpu.VMEM((H, nch - 1, srows, dh), BF16), state, state, pltpu.VMEM((H, 8, 128), F32), sem, sem,
         pltpu.VMEM((first, srows, dh), BF16), pltpu.VMEM((first, srows, dh), BF16), pltpu.SemaphoreType.DMA((first,)),
         pltpu.SemaphoreType.DMA((first,))],
        collective_id=2, has_side_effects=True,
    )

    early = lambda a, *shape: (a, sp.lead("first", *shape))
    turn = lambda a, *shape: (a, sp.lead("turned", *shape))
    late = lambda a: (a, sp.cols("turned", *a.shape[1:]))
    rows = up_weight.shape[0]
    inside = by_hand(rows)
    anywhere = pl.BlockSpec(memory_space=pl.ANY)
    vmem = pltpu.VMEM
    ins = [whole(halo), whole(gain), whole(flags), whole(normt), whole(gates), whole(gcol), whole(grow), whole(retain),
           (gend, pl.BlockSpec((H - first, srows, dh), lambda s: (1, 0, 0), pipeline_mode=pl.Buffered(1))), whole(gin), (q, sp.cols("mixed", n, dh)), (k, sp.cols("mixed", n, dh)), (va, sp.lead("mixed", n, dh + 128)),
           early(gaug, n, dh + 128), early(sttot, nch, srows, dh), early(gloc, nch - 1, srows, dh),
           late(pre), late(br), late(ogg), late(dskip), turn(pack, *pack.shape[1:]), turn(w_all, d, 2 * dh),
           turn(sums, 8, dh)]
    sums_here = [sds((H, 72, dh), F32), sds((HALO, d), F32)]
    scratch = [vmem((H, n, dh), BF16), vmem((H, n, dh), BF16), vmem((H, n, dh), BF16), vmem((n, 128), BF16),
               vmem((8, 128), F32), vmem((dh + 128, dh), BF16), vmem((dh + 128, dh), BF16), vmem((n, 128), F32),
               vmem((128, n), F32), vmem((8, 128), F32), vmem((n + 2 * HALO, dh), F32), vmem((n, 2 * dh), BF16),
               vmem((n, dh), BF16), vmem((dh // 128, 128, 256), BF16), vmem((dh // 128, 128, 128), BF16),
               vmem((3, 128, dh), BF16), vmem((d, 128), F32), vmem((H - first, srows, dh), BF16), state, sem, sem]
    if inside:
        ins.append((dng, anywhere))
        outs = [sds((rows, 2 * dh), F32), sds((rows, dh), F32), sds((72, dh), F32), sds((HALO, d), F32), sds((n, d), F32)]
        small = lambda count: vmem((count, 72, dh), F32)
        dma = pltpu.SemaphoreType.DMA
        scratch += [vmem((d, 2 * dh), BF16), vmem((H, 72, dh), F32), vmem((HALO, d), F32), vmem((HALO, d), F32), small(2), small(3), small(2),
                    small(4), dma((2,)), dma((7,)), dma((7,)), *Scatter.scratch(d, rows, 2 * dh),
                    *Scatter.scratch(d, rows, dh)]
        outs = [whole(o) for o in outs]
    else:
        outs = [(sds((H, d, 2 * dh), BF16), sp.cols("turned", d, 2 * dh)), *(whole(o) for o in sums_here),
                whole(sds((n, d), F32))]
    made = call(partial(backward_kernel, inside, H, log_scale), "backward", 2, ins, outs, scratch,
                collective_id=3, has_side_effects=True)
    if inside:
        up_total, down_total, minor, corr, ng = made
    else:
        upg, minor, corr, ng = made

        def summed(part):
            part = lax.psum_scatter(part, "head", scatter_dimension=0, tiled=True)
            return lax.psum_scatter(part, "dp", scatter_dimension=1, tiled=True)[0].astype(F32)

        up_total, down_total = summed(upg), summed(dng)
        minor = lax.psum(lax.psum_scatter(minor, "head", scatter_dimension=0, tiled=True), "dp")[0]
        corr = shifted(corr, -1)

    once = lambda *shape: pl.BlockSpec(shape, lambda i: (0,) * len(shape))
    chunk = pl.BlockSpec((CH, d), lambda i: (i, 0))
    lines = (dh // 128, 128)
    shapes = [(rows, 2, dh), (rows, dh), (TAPS, dh), lines, (3, 4, 4, dh // 4), (3, 2 * H, dh), (1, 2), lines, lines,
              (d // 128, 128)]
    up, down, conv_w, conv_b, maps, gate_w, gate_b, group, skip, norm, ing, output = pl.pallas_call(
        partial(finish_kernel, H),
        grid=(n // CH,),
        out_shape=[*(sds(shape, F32) for shape in shapes), sds((n, d), F32), sds((n, d), BF16)],
        in_specs=[chunk, chunk, *(once(*a.shape) for a in (gain, up_total, down_total, minor, corr)), chunk, chunk],
        out_specs=[*(once(*shape) for shape in shapes), chunk, chunk],
        compiler_params=params(),
        name="finish",
    )(inputs, out_grad, gain, up_total, down_total, minor, corr, ng, output)
    return (output, ing, norm.reshape(d), up, conv_w, conv_b.reshape(dh), maps.transpose(0, 3, 1, 2),
            gate_w.transpose(0, 2, 1), gate_b.T, group.reshape(dh), skip.reshape(dh), down.T)


def solution(mesh):
    rows = P(("dp", "head"), None)
    small = (P(None, "head"), P("head"), P(None, "head", None, None), P(None, "head", None), P(None, "head"))
    return jax.shard_map(
        local,
        mesh=mesh,
        in_specs=(rows, P("dp"), P(), P("dp", None, "head"), *small, P("head"), P("head"), P("head", "dp"), rows),
        out_specs=(rows, rows, P(), P("dp", None, "head"), *small, P("head"), P("head"), P("head", "dp")),
        check_vma=False,
    )
```
